32 devices in a mesh: seq: 4 (over z), ctx: 8 (over y, x, core).
Axes of the slice: x: 2, y: 2, z: 4, core: 2. Of those that a mesh axis runs over, the one named last changes fastest.
Arguments:
- queries: bfloat16 [4096, 2048], P(('seq', 'ctx')), parts along dimension 0, may hold values from -6 to 6
- key_rows: bfloat16 [4096, 2048], P(('seq', 'ctx')), parts along dimension 0, may hold values from -6 to 6
- values: bfloat16 [4096, 2048], P(('seq', 'ctx')), parts along dimension 0, may hold values from -6 to 6
- out_grad: bfloat16 [4096, 2048], P(('seq', 'ctx')), parts along dimension 0, may hold values from -0.016479492 to 0.016479492
- feature_map: bfloat16 [16, 128, 128], replicated, may hold values from -0.5 to 0.5
Outputs:
- query_grad: bfloat16 [4096, 2048], P(('seq', 'ctx')), parts along dimension 0
- key_grad: bfloat16 [4096, 2048], P(('seq', 'ctx')), parts along dimension 0
- value_grad: bfloat16 [4096, 2048], P(('seq', 'ctx')), parts along dimension 0
- map_grad: float32 [64, 128, 128], P('seq'), parts along dimension 0
The draws below stay inside these ranges and needn't reach their ends.
There are 4 independent parts, one for each index of `seq`. The reference program is written for one: setup_inputs(seed, part) draws one part's arguments, and reference() takes and returns one part's arrays. A program takes and returns all parts, laid end to end along the dimension named above; an argument that names none is the same for every part. Nothing has to cross between parts.
All inputs are finite; a program needn't handle non-finite values.
Results may differ from the reference program's by a relative error of at most 0.033.
Values may be sent and summed in bfloat16 or wider, within the bound.
No kernel may reach another device: no remote copies, remote signals or barrier semaphores. Data moves between devices by JAX's collectives and lax.ppermute only.
A program may use at most 128 MiB of HBM per device.

```python
import math
import jax
import jax.numpy as jnp
from jax import lax

HEADS = 16
HD = 128
TOK_DEV = 128
TOKENS = 1024
N_CTX = 8


def steps_of(stream_key, extent, cuts, smallest, high):
    def one(axis_at, parts):
        steps = jax.random.uniform(jax.random.fold_in(jax.random.fold_in(stream_key, 6), axis_at), (parts,), jnp.float32, smallest / len(cuts), high / len(cuts))
        return jnp.repeat(jnp.exp(steps), extent[axis_at] // parts).reshape((-1,) + (1,) * (len(extent) - axis_at - 1))

    loudness = one(*cuts[0])
    for cut in cuts[1:]:
        loudness = loudness * one(*cut)
    return loudness


def centred(key, extent, deviation, most, shards=(), dtype=jnp.bfloat16):
    loudness = steps_of(key, extent, shards, -0.22, 0.18) if shards else 1.0
    drawn = jax.random.normal(key, extent, jnp.float32) * deviation * loudness
    return jnp.minimum(jnp.maximum(drawn, -most), most).astype(dtype)


def setup_inputs(seed: int = 0, part: int = 0) -> dict:
    keys = jax.random.split(jax.random.key(seed), 6)
    part_splits = jax.random.split(jax.random.fold_in(keys[5], part), 6)
    return {
        "queries": centred(part_splits[0], (TOKENS, HEADS * HD), 1.0, 6.0, ((0, 8),)),
        "key_rows": centred(part_splits[1], (TOKENS, HEADS * HD), 1.0, 6.0, ((0, 8),)),
        "values": centred(part_splits[2], (TOKENS, HEADS * HD), 1.0, 6.0, ((0, 8),)),
        "out_grad": centred(part_splits[3], (TOKENS, HEADS * HD), ((HD * TOKENS) ** -0.5), 0.016479492, ((0, 8),)),
        "feature_map": centred(keys[4], (HEADS, HD, HD), HD ** -0.5, 0.5),
    }


def rounded(x):
    return lax.optimization_barrier(x.astype(jnp.bfloat16)).astype(jnp.float32)

def reference(queries, key_rows, values, out_grad, feature_map):
    f32 = jnp.float32

    def split(x):
        return x.astype(f32).reshape(N_CTX, TOK_DEV, HEADS, HD)
    query_h = split(queries)
    key_h = split(key_rows)
    value_h = split(values)
    grad_h = split(out_grad)
    weights = feature_map.astype(f32)
    query_feat = rounded(jnp.einsum('bthd,hde->bthe', query_h, weights))
    key_feat = rounded(jnp.einsum('bthd,hde->bthe', key_h, weights))
    key_state = rounded(jnp.einsum('bthe,bthv->bhev', key_feat, value_h))
    grad_state = rounded(jnp.einsum('bthe,bthv->bhev', query_feat, grad_h))
    empty = jnp.zeros_like(key_state[:1])
    prefix = jnp.concatenate([empty, jnp.cumsum(key_state, 0)[:-1]], 0)
    backward = jnp.cumsum(grad_state[::-1], 0)[::-1]
    suffix = jnp.concatenate([backward[1:], empty], 0)
    prefix = rounded(prefix)
    suffix = rounded(suffix)
    rows_idx = lax.broadcasted_iota(jnp.int32, (TOK_DEV, TOK_DEV), 0)
    cols_idx = lax.broadcasted_iota(jnp.int32, (TOK_DEV, TOK_DEV), 1)
    causal = rows_idx >= cols_idx
    scores = jnp.einsum('bthe,bshe->bhts', query_feat, key_feat)
    scores = rounded(jnp.where(causal, scores, 0.0))
    mixing = jnp.einsum('bthv,bshv->bhts', grad_h, value_h)
    mixing = rounded(jnp.where(causal, mixing, 0.0))
    feat_qgrad = rounded(jnp.einsum('bhts,bshe->bthe', mixing, key_feat) + jnp.einsum('bthv,bhev->bthe', grad_h, prefix))
    feat_kgrad = rounded(jnp.einsum('bhts,bthe->bshe', mixing, query_feat) + jnp.einsum('bshv,bhev->bshe', value_h, suffix))
    value_grad = jnp.einsum('bhts,bthv->bshv', scores, grad_h) + jnp.einsum('bshe,bhev->bshv', key_feat, suffix)
    query_grad = jnp.einsum('bthe,hde->bthd', feat_qgrad, weights)
    key_grad = jnp.einsum('bthe,hde->bthd', feat_kgrad, weights)
    block_mgrad = jnp.einsum('bthd,bthe->bhde', query_h, feat_qgrad) + jnp.einsum('bthd,bthe->bhde', key_h, feat_kgrad)
    block_mgrad = rounded(block_mgrad)
    map_grad = lax.optimization_barrier(jnp.sum(block_mgrad, 0)) / math.sqrt(TOKENS)
    whole = (TOKENS, HEADS * HD)
    return (query_grad.reshape(whole).astype(jnp.bfloat16), key_grad.reshape(whole).astype(jnp.bfloat16), value_grad.reshape(whole).astype(jnp.bfloat16), map_grad.astype(f32))
```

```python
import functools
import math

import jax
import jax.numpy as jnp
from jax import lax
from jax.experimental import pallas as pl
from jax.experimental.pallas import tpu as pltpu
from jax.sharding import PartitionSpec as P

F32 = jnp.float32
BF16 = jnp.bfloat16
VMEM = pl.BlockSpec(memory_space=pltpu.VMEM)
PARAMS = pltpu.CompilerParams(vmem_limit_bytes=8 * 2**20)
GROUPS = 4
EXTRA = 16


def dot_nn(a, b):
    return lax.dot_general(a, b, (((1,), (0,)), ((), ())), preferred_element_type=F32)


def dot_nt(a, b):
    return lax.dot_general(a, b, (((1,), (1,)), ((), ())), preferred_element_type=F32)


def dot_tn(a, b):
    return lax.dot_general(a, b, (((0,), (0,)), ((), ())), preferred_element_type=F32)


def call(body, outs, *operands):
    return pl.pallas_call(
        body,
        out_shape=[jax.ShapeDtypeStruct(shape, dtype) for shape, dtype in outs],
        in_specs=[VMEM] * len(operands),
        out_specs=[VMEM] * len(outs),
        compiler_params=PARAMS,
    )(*operands)


def place():
    me = lax.axis_index("ctx")
    return lax.rem(me, 2), lax.div(me, 2)


def head_of(half, chip, apart, i, per_owner):
    return half * (GROUPS * per_owner) + (chip ^ apart) * per_owner + i


def columns(head, size):
    return pl.ds(pl.multiple_of(head * size, size), size)


def triangle(size):
    rows = lax.broadcasted_iota(jnp.int32, (size, size), 0)
    cols = lax.broadcasted_iota(jnp.int32, (size, size), 1)
    return rows, cols


def states_body(mine, per_owner, q, k, v, g, *outs):
    out = outs[0]
    size = out.shape[-1]
    core, chip = place()
    half = core if mine else 1 - core
    for apart in range(GROUPS):
        for i in range(per_owner):
            at = columns(head_of(half, chip, apart, i, per_owner), size)
            early = dot_tn(k[:, at], v[:, at]).astype(BF16)
            late = dot_tn(q[:, at], g[:, at]).astype(BF16)
            out[apart, 0, i] = early
            out[apart, 1, i] = late
            if mine:
                outs[1][apart, i] = jnp.where(core == 0, early, late)


def add_body(own, other, *outs):
    for apart in range(GROUPS):
        outs[apart][...] = (own[apart].astype(F32) + other[apart].astype(F32)).astype(BF16)


def local_body(per_owner, q, k, v, g, own_c, send_c, part_q):
    size = own_c.shape[-1]
    core, chip = place()
    rows, cols = triangle(q.shape[0])
    causal = rows >= cols
    for which, out in ((1, send_c), (0, own_c)):
        half = core if which == 0 else 1 - core
        for apart in range(GROUPS):
            for i in range(per_owner):
                at = columns(head_of(half, chip, apart, i, per_owner), size)
                mixing = jnp.where(causal, dot_nt(g[:, at], v[:, at]), 0.0).astype(BF16)
                mixed = dot_nn(mixing, k[:, at])
                part_q[which, apart, i] = mixed
                out[apart, i] = dot_tn(q[:, at], mixed.astype(BF16)).astype(BF16)


def local_rest_body(per_owner, q, k, v, g, w, part_k, part_v, key_w, gram):
    size = w.shape[-1]
    core, chip = place()
    rows, cols = triangle(q.shape[0])
    causal = rows >= cols
    for which in (0, 1):
        half = core if which == 0 else 1 - core
        for apart in range(GROUPS):
            for i in range(per_owner):
                head = head_of(half, chip, apart, i, per_owner)
                at = columns(head, size)
                mixing = jnp.where(causal, dot_nt(g[:, at], v[:, at]), 0.0).astype(BF16)
                part_k[which, apart, i] = dot_tn(mixing, q[:, at])
                square = dot_nt(w[head], w[head]).astype(BF16)
                gram[which, apart, i] = square
                keyed = dot_nn(k[:, at], square).astype(BF16)
                key_w[which, apart, i] = keyed
                scores = jnp.where(causal, dot_nt(q[:, at], keyed), 0.0).astype(BF16)
                part_v[which, apart, i] = dot_tn(scores, g[:, at])


def pack(first, second):
    size = first.shape[0]
    rows, cols = triangle(size)
    both = jnp.where(rows >= cols, first, second)
    diagonal = jnp.sum(jnp.where(rows == cols, second, 0.0), axis=0, keepdims=True)
    return both, jnp.broadcast_to(diagonal, (EXTRA, size))


def pack_body(per_owner, own, other, own_c, other_c, *outs):
    size = own_c.shape[-1]
    core, _ = place()
    last = core == 1
    for apart in range(GROUPS):
        for pair in range(per_owner // 2):
            sums = []
            for i in (2 * pair, 2 * pair + 1):
                early = jnp.where(last, other[apart, 0, i], own[apart, 0, i])
                late = jnp.where(last, own[apart, 1, i], other[apart, 1, i])
                total = dot_nt(late, early)
                total += own_c[apart, i].astype(F32) + other_c[apart, i].astype(F32)
                sums.append(total + total.T)
            both, diagonal = pack(*sums)
            outs[apart][pair, :size] = both.astype(BF16)
            outs[apart][pair, size:] = diagonal.astype(BF16)


def carry_body(*refs):
    parts, outs = refs[:GROUPS], refs[GROUPS:]
    _, chip = place()
    early = [part[0].astype(F32) for part in parts]
    late = [part[1].astype(F32) for part in parts]
    for to in range(GROUPS):
        prefix = jnp.zeros_like(early[0])
        suffix = jnp.zeros_like(early[0])
        for apart in range(GROUPS):
            if apart == to:
                continue
            before = (chip ^ apart) < (chip ^ to)
            prefix += jnp.where(before, early[apart], 0.0)
            suffix += jnp.where(before, 0.0, late[apart])
        outs[to][0] = prefix.astype(BF16)
        outs[to][1] = suffix.astype(BF16)


def cross_body(per_owner, *refs):
    parts, carried, packed = refs[:GROUPS], refs[GROUPS : 2 * GROUPS], refs[2 * GROUPS : 3 * GROUPS]
    out = refs[3 * GROUPS]
    size = out.shape[-1]
    for pair in range(per_owner // 2):
        sums = []
        for i in (2 * pair, 2 * pair + 1):
            total = dot_nt(parts[0][1, i], carried[0][0, i])
            for apart in range(1, GROUPS):
                total += dot_nt(parts[apart][1, i], carried[apart][0, i])
            sums.append(total + total.T)
        both, diagonal = pack(*sums)
        for apart in range(GROUPS):
            both += packed[apart][pair, :size].astype(F32)
            diagonal += packed[apart][pair, size:].astype(F32)
        out[pair, :size] = both.astype(BF16)
        out[pair, size:] = diagonal.astype(BF16)


def final_body(per_owner, *refs):
    q, k, v, g, key_w, gram, part_q, part_k, part_v, other, extra = refs[:11]
    carried = refs[11 : 11 + 2 * GROUPS]
    query_grad, key_grad, value_grad = refs[11 + 2 * GROUPS :]
    size = gram.shape[-1]
    core, chip = place()
    for which in (0, 1):
        half = core if which == 0 else 1 - core
        for apart in range(GROUPS):
            for i in range(per_owner):
                at = columns(head_of(half, chip, apart, i, per_owner), size)
                state = carried[which * GROUPS + apart]
                if which == 0:
                    near_early, near_late = other[apart, 0, i], other[apart, 1, i]
                else:
                    near_early = near_late = extra[apart, i]
                prefix = state[0, i].astype(F32)
                prefix += jnp.where(core == 1, near_early.astype(F32), 0.0)
                suffix = state[1, i].astype(F32)
                suffix += jnp.where(core == 0, near_late.astype(F32), 0.0)
                prefix = prefix.astype(BF16)
                suffix = suffix.astype(BF16)
                square = gram[which, apart, i]
                raw_q = (part_q[which, apart, i] + dot_nt(g[:, at], prefix)).astype(BF16)
                query_grad[:, at] = dot_nn(raw_q, square).astype(BF16)
                raw_k = (part_k[which, apart, i] + dot_nt(v[:, at], suffix)).astype(BF16)
                key_grad[:, at] = dot_nn(raw_k, square).astype(BF16)
                whole = part_v[which, apart, i] + dot_nn(key_w[which, apart, i], suffix)
                value_grad[:, at] = whole.astype(BF16)


def map_body(per_owner, scale, w, *refs):
    packed, out = refs[: 2 * GROUPS], refs[2 * GROUPS]
    size = w.shape[-1]
    core, chip = place()
    rows, cols = triangle(size)
    for which in (0, 1):
        half = core if which == 0 else 1 - core
        for apart in range(GROUPS):
            for pair in range(per_owner // 2):
                ref = packed[which * GROUPS + apart]
                both = ref[pair, :size].astype(F32)
                diagonal = ref[pair, size:][:1].astype(F32)
                turned = both.T
                first = jnp.where(rows >= cols, both, turned)
                second = jnp.where(rows < cols, both, turned)
                second = jnp.where(rows == cols, diagonal, second)
                for i, whole in ((2 * pair, first), (2 * pair + 1, second)):
                    head = head_of(half, chip, apart, i, per_owner)
                    out[head] = dot_nn(whole.astype(BF16), w[head]) * scale


def swap(x, apart):
    count = lax.axis_size("ctx")
    return lax.ppermute(x, "ctx", [(i, i ^ apart) for i in range(count)])


def paired(q, k, v, g, w):
    rows, width = q.shape
    heads, size = w.shape[0], w.shape[-1]
    per_owner = heads // (2 * GROUPS)
    pairs = per_owner // 2
    length = rows * lax.axis_size("ctx")
    block = (size, size)
    both_shape = (GROUPS, 2, per_owner) + block
    one_shape = (GROUPS, per_owner) + block
    state_shape = (2, per_owner) + block
    pack_shape = (pairs, size + EXTRA, size)
    all_shape = (2, GROUPS, per_owner) + block
    bind = functools.partial

    (send,) = call(bind(states_body, False, per_owner), [(both_shape, BF16)], q, k, v, g)
    other = swap(send, 1)
    own, extra = call(
        bind(states_body, True, per_owner), [(both_shape, BF16), (one_shape, BF16)], q, k, v, g
    )
    chip_states = call(add_body, [(state_shape, BF16)] * GROUPS, own, other)
    parts = [chip_states[0]] + [swap(chip_states[j], 2 * j) for j in range(1, GROUPS)]
    extra = swap(extra, 1)

    own_c, send_c, part_q = call(
        bind(local_body, per_owner),
        [(one_shape, BF16), (one_shape, BF16), (all_shape, F32)],
        q, k, v, g,
    )
    other_c = swap(send_c, 1)
    chip_c = call(
        bind(pack_body, per_owner), [(pack_shape, BF16)] * GROUPS, own, other, own_c, other_c
    )
    packed = [chip_c[0]] + [swap(chip_c[j], 2 * j) for j in range(1, GROUPS)]
    part_k, part_v, key_w, gram = call(
        bind(local_rest_body, per_owner),
        [(all_shape, F32), (all_shape, F32), (all_shape, BF16), (all_shape, BF16)],
        q, k, v, g, w,
    )

    carried = call(carry_body, [(state_shape, BF16)] * GROUPS, *parts)
    near = [carried[0]] + [swap(carried[j], 2 * j) for j in range(1, GROUPS)]
    far = [swap(x, 1) for x in near]
    (total,) = call(
        bind(cross_body, per_owner), [(pack_shape, BF16)], *parts, *carried, *packed
    )
    near_map = [total] + [swap(total, 2 * j) for j in range(1, GROUPS)]
    far_map = [swap(x, 1) for x in near_map]
    grads = call(
        bind(final_body, per_owner),
        [((rows, width), BF16)] * 3,
        q, k, v, g, key_w, gram, part_q, part_k, part_v, other, extra, *near, *far,
    )
    (map_grad,) = call(
        bind(map_body, per_owner, 1.0 / math.sqrt(length)),
        [((heads,) + block, F32)],
        w, *near_map, *far_map,
    )
    return (*grads, map_grad)


def gathered(q, k, v, g, w):
    rows, width = q.shape
    heads, size = w.shape[0], w.shape[-1]
    count = lax.axis_size("ctx")
    me = lax.axis_index("ctx")
    q, k, v, g = (x.reshape(rows, heads, size) for x in (q, k, v, g))

    def mul(spec, a, b):
        return jnp.einsum(spec, a, b, preferred_element_type=F32)

    query_feat = mul("thd,hde->the", q, w).astype(BF16)
    key_feat = mul("thd,hde->the", k, w).astype(BF16)
    key_state = mul("the,thv->hev", key_feat, v).astype(BF16)
    grad_state = mul("the,thv->hev", query_feat, g).astype(BF16)
    index = jnp.arange(count).reshape(count, 1, 1, 1)
    keys = lax.all_gather(key_state, "ctx").astype(F32)
    prefix = jnp.sum(jnp.where(index < me, keys, 0.0), 0).astype(BF16)
    grads = lax.all_gather(grad_state, "ctx").astype(F32)
    suffix = jnp.sum(jnp.where(index > me, grads, 0.0), 0).astype(BF16)
    row, col = triangle(rows)
    causal = row >= col
    scores = jnp.where(causal, mul("the,she->hts", query_feat, key_feat), 0.0).astype(BF16)
    mixing = jnp.where(causal, mul("thv,shv->hts", g, v), 0.0).astype(BF16)
    feat_q = mul("hts,she->the", mixing, key_feat) + mul("thv,hev->the", g, prefix)
    feat_k = mul("hts,the->she", mixing, query_feat) + mul("shv,hev->she", v, suffix)
    feat_q, feat_k = feat_q.astype(BF16), feat_k.astype(BF16)
    value_grad = mul("hts,thv->shv", scores, g) + mul("she,hev->shv", key_feat, suffix)
    query_grad = mul("the,hde->thd", feat_q, w)
    key_grad = mul("the,hde->thd", feat_k, w)
    local = mul("thd,the->hde", q, feat_q) + mul("thd,the->hde", k, feat_k)
    map_grad = lax.psum(local.astype(BF16).astype(F32), "ctx") / math.sqrt(rows * count)
    flat = (rows, width)
    return (
        query_grad.reshape(flat).astype(BF16),
        key_grad.reshape(flat).astype(BF16),
        value_grad.reshape(flat).astype(BF16),
        map_grad,
    )


def per_device(queries, key_rows, values, out_grad, feature_map):
    fits = lax.axis_size("ctx") == 2 * GROUPS and feature_map.shape[0] % (4 * GROUPS) == 0
    plan = paired if fits else gathered
    return plan(queries, key_rows, values, out_grad, feature_map)


def solution(mesh):
    rows = P(("seq", "ctx"), None)
    return jax.shard_map(
        per_device,
        mesh=mesh,
        in_specs=(rows, rows, rows, rows, P()),
        out_specs=(rows, rows, rows, P("seq", None, None)),
        check_vma=False,
    )
```

```python
import functools
import math

import jax
import jax.numpy as jnp
from jax import lax
from jax.experimental import pallas as pl
from jax.experimental.pallas import tpu as pltpu
from jax.sharding import PartitionSpec as P

F32 = jnp.float32
BF16 = jnp.bfloat16
VMEM = pl.BlockSpec(memory_space=pltpu.VMEM)
HBM = pl.BlockSpec(memory_space=pltpu.HBM)
ANY = pl.BlockSpec(memory_space=pl.ANY)
GROUPS = 4
EXTRA = 16


def dot_nn(a, b):
    return lax.dot_general(a, b, (((1,), (0,)), ((), ())), preferred_element_type=F32)


def dot_nt(a, b):
    return lax.dot_general(a, b, (((1,), (1,)), ((), ())), preferred_element_type=F32)


def dot_tn(a, b):
    return lax.dot_general(a, b, (((0,), (0,)), ((), ())), preferred_element_type=F32)


def call(body, outs, operands, cost, after=(), scratch=(), in_spec=VMEM, out_specs=None, aliases=None):
    count = len(operands)

    def run(*refs):
        return body(*refs[:count], *refs[count + len(after) :])

    return pl.pallas_call(
        run,
        out_shape=[jax.ShapeDtypeStruct(shape, dtype) for shape, dtype in outs],
        in_specs=[in_spec] * count + [ANY] * len(after),
        out_specs=out_specs or [VMEM] * len(outs),
        scratch_shapes=list(scratch),
        input_output_aliases=aliases or {},
        cost_estimate=pl.CostEstimate(
            flops=int(cost * 1.15e9), bytes_accessed=0, transcendentals=0
        ),
        compiler_params=pltpu.CompilerParams(vmem_limit_bytes=16 * 2**20),
    )(*operands, *after)


def place():
    me = lax.axis_index("ctx")
    return lax.rem(me, 2), lax.div(me, 2)


def owned(half, chip, per_owner):
    base = half * (GROUPS * per_owner)
    return [
        (apart, i, base + (chip ^ apart) * per_owner + i)
        for apart in range(GROUPS)
        for i in range(per_owner)
    ]


def columns(head, size):
    return pl.ds(pl.multiple_of(head * size, size), size)


def triangle(size):
    rows = lax.broadcasted_iota(jnp.int32, (size, size), 0)
    cols = lax.broadcasted_iota(jnp.int32, (size, size), 1)
    return rows, cols


def load_body(per_owner, q, k, v, g, q_here, k_here, v_here, g_here, send, sems):
    size = send.shape[-1]
    half_width = q.shape[1] // 2
    core, chip = place()
    pairs = ((k, k_here), (v, v_here), (q, q_here), (g, g_here))
    copies = []
    for turn, half in enumerate((1 - core, core)):
        at = columns(half, half_width)
        for n, (source, target) in enumerate(pairs):
            copy = pltpu.make_async_copy(source.at[:, at], target.at[:, at], sems.at[turn, n])
            copy.start()
            copies.append(copy)
    heads = owned(1 - core, chip, per_owner)
    ats = [columns(head, size) for _, _, head in heads]
    for kind, (left, right) in enumerate(((k_here, v_here), (q_here, g_here))):
        copies[2 * kind].wait()
        copies[2 * kind + 1].wait()
        states = [dot_tn(left[:, at], right[:, at]) for at in ats]
        for (apart, i, _), state in zip(heads, states):
            send[apart, kind, i] = state.astype(BF16)
    for copy in copies[4:]:
        copy.wait()


def mixed_keys(q, k, v, g, ats):
    rows, cols = triangle(q.shape[0])
    mixing = [dot_nt(g[:, at], v[:, at]) for at in ats]
    mixing = [jnp.where(rows >= cols, x, 0.0).astype(BF16) for x in mixing]
    return [dot_nn(x, k[:, at]) for x, at in zip(mixing, ats)]


def near_body(per_owner, q, k, v, g, own, extra_c, part_q):
    size = own.shape[-1]
    core, chip = place()
    heads = owned(core, chip, per_owner)
    ats = [columns(head, size) for _, _, head in heads]
    early = [dot_tn(k[:, at], v[:, at]).astype(BF16) for at in ats]
    late = [dot_tn(q[:, at], g[:, at]).astype(BF16) for at in ats]
    for n, (apart, i, _) in enumerate(heads):
        own[apart, 0, i] = early[n]
        own[apart, 1, i] = late[n]
        extra_c[0, apart, i] = jnp.where(core == 0, early[n], late[n])
    heads = owned(1 - core, chip, per_owner)
    ats = [columns(head, size) for _, _, head in heads]
    mixed = mixed_keys(q, k, v, g, ats)
    cross = [dot_tn(q[:, at], x.astype(BF16)) for x, at in zip(mixed, ats)]
    for n, (apart, i, _) in enumerate(heads):
        part_q[apart, i] = mixed[n]
        extra_c[1, apart, i] = cross[n].astype(BF16)


def add_body(own, other, *outs):
    for apart in range(GROUPS):
        outs[apart][...] = (own[apart].astype(F32) + other[apart].astype(F32)).astype(BF16)


def own_body(per_owner, q, k, v, g, own_c, part_q):
    size = own_c.shape[-1]
    core, chip = place()
    heads = owned(core, chip, per_owner)
    ats = [columns(head, size) for _, _, head in heads]
    mixed = mixed_keys(q, k, v, g, ats)
    cross = [dot_tn(q[:, at], x.astype(BF16)) for x, at in zip(mixed, ats)]
    for n, (apart, i, _) in enumerate(heads):
        part_q[apart, i] = mixed[n]
        own_c[apart, i] = cross[n].astype(BF16)


def rest_body(per_owner, q, k, v, g, w, part_k, part_v, key_w, gram):
    size = w.shape[-1]
    core, chip = place()
    rows, cols = triangle(q.shape[0])
    later = cols >= rows
    for which, half in enumerate((core, 1 - core)):
        heads = owned(half, chip, per_owner)
        ats = [columns(head, size) for _, _, head in heads]
        square = [dot_nt(w[head], w[head]).astype(BF16) for _, _, head in heads]
        mixing = [dot_nt(v[:, at], g[:, at]) for at in ats]
        mixing = [jnp.where(later, x, 0.0).astype(BF16) for x in mixing]
        keyed = [dot_nn(k[:, at], x).astype(BF16) for x, at in zip(square, ats)]
        mixed = [dot_nn(x, q[:, at]) for x, at in zip(mixing, ats)]
        scores = [dot_nt(x, q[:, at]) for x, at in zip(keyed, ats)]
        scores = [jnp.where(later, x, 0.0).astype(BF16) for x in scores]
        scored = [dot_nn(x, g[:, at]) for x, at in zip(scores, ats)]
        for n, (apart, i, _) in enumerate(heads):
            gram[which, apart, i] = square[n]
            key_w[which, apart, i] = keyed[n]
            part_k[which, apart, i] = mixed[n]
            part_v[which, apart, i] = scored[n]


def pack(first, second):
    size = first.shape[0]
    rows, cols = triangle(size)
    both = jnp.where(rows >= cols, first, second)
    diagonal = jnp.sum(jnp.where(rows == cols, second, 0.0), axis=0, keepdims=True)
    return both, jnp.broadcast_to(diagonal, (EXTRA, size))


def pack_body(per_owner, own, other, own_c, extra_c, *outs):
    size = own_c.shape[-1]
    core, _ = place()
    last = core == 1
    totals = []
    for apart in range(GROUPS):
        for i in range(per_owner):
            early = jnp.where(last, other[apart, 0, i], own[apart, 0, i])
            late = jnp.where(last, own[apart, 1, i], other[apart, 1, i])
            totals.append(dot_nt(late, early))
    for apart in range(GROUPS):
        for pair in range(per_owner // 2):
            sums = []
            for i in (2 * pair, 2 * pair + 1):
                total = totals[apart * per_owner + i]
                total += own_c[apart, i].astype(F32) + extra_c[1, apart, i].astype(F32)
                sums.append(total + total.T)
            both, diagonal = pack(*sums)
            outs[apart][pair, :size] = both.astype(BF16)
            outs[apart][pair, size:] = diagonal.astype(BF16)


def owner_body(per_owner, *refs):
    parts, packed, outs = refs[:GROUPS], refs[GROUPS : 2 * GROUPS], refs[2 * GROUPS :]
    size = outs[0].shape[-1]
    _, chip = place()
    turns = []
    for i in range(per_owner):
        early = [part[0, i].astype(F32) for part in parts]
        late = [part[1, i].astype(F32) for part in parts]
        cross = None
        for to in range(GROUPS):
            prefix = jnp.zeros_like(early[0])
            suffix = jnp.zeros_like(early[0])
            for apart in range(GROUPS):
                if apart == to:
                    continue
                before = (chip ^ apart) < (chip ^ to)
                prefix += jnp.where(before, early[apart], 0.0)
                suffix += jnp.where(before, 0.0, late[apart])
            prefix = prefix.astype(BF16)
            outs[to][i * size : (i + 1) * size] = prefix
            outs[to][(per_owner + i) * size : (per_owner + i + 1) * size] = suffix.astype(BF16)
            product = dot_nt(parts[to][1, i], prefix)
            cross = product if cross is None else cross + product
        turns.append(cross + cross.T)
    for pair in range(per_owner // 2):
        both, diagonal = pack(turns[2 * pair], turns[2 * pair + 1])
        for apart in range(GROUPS):
            both += packed[apart][pair, :size].astype(F32)
            diagonal += packed[apart][pair, size:].astype(F32)
        start = 2 * per_owner * size + pair * (size + EXTRA)
        for to in range(GROUPS):
            outs[to][start : start + size] = both.astype(BF16)
            outs[to][start + size : start + size + EXTRA] = diagonal.astype(BF16)


def tail_body(which, per_owner, scale, *refs):
    q, k, v, g, w, key_w, gram, part_q, part_k, part_v, near = refs[:11]
    carried = refs[11 : 11 + GROUPS]
    outs = refs[-9:-5]
    here = refs[-5:-1]
    sems = refs[-1]
    query_here, key_here, value_here, map_here = here
    size = gram.shape[-1]
    core, chip = place()
    half = 1 - core if which else core
    heads = owned(half, chip, per_owner)
    ats = [columns(head, size) for _, _, head in heads]
    slots = [columns((chip ^ apart) * per_owner + i, size) for apart, i, _ in heads]
    prefix, suffix = [], []
    for apart, i, _ in heads:
        if which:
            early = late = near[0, apart, i]
        else:
            early, late = near[apart, 0, i], near[apart, 1, i]
        before = carried[apart][i * size : (i + 1) * size].astype(F32)
        after = carried[apart][(per_owner + i) * size : (per_owner + i + 1) * size].astype(F32)
        prefix.append((before + jnp.where(core == 1, early.astype(F32), 0.0)).astype(BF16))
        suffix.append((after + jnp.where(core == 0, late.astype(F32), 0.0)).astype(BF16))
    raw_q = [dot_nt(g[:, at], x) for x, at in zip(prefix, ats)]
    raw_k = [dot_nt(v[:, at], x) for x, at in zip(suffix, ats)]
    raw_v = [dot_nn(key_w[which, a, i], x) for x, (a, i, _) in zip(suffix, heads)]
    raw_q = [(part_q[a, i] + x).astype(BF16) for x, (a, i, _) in zip(raw_q, heads)]
    raw_k = [(part_k[which, a, i] + x).astype(BF16) for x, (a, i, _) in zip(raw_k, heads)]
    for n, (a, i, _) in enumerate(heads):
        value_here[:, slots[n]] = (part_v[which, a, i] + raw_v[n]).astype(BF16)
    done_q = [dot_nn(x, gram[which, a, i]) for x, (a, i, _) in zip(raw_q, heads)]
    done_k = [dot_nn(x, gram[which, a, i]) for x, (a, i, _) in zip(raw_k, heads)]
    for n, slot in enumerate(slots):
        query_here[:, slot] = done_q[n].astype(BF16)
        key_here[:, slot] = done_k[n].astype(BF16)
    span = columns(half, q.shape[1] // 2)
    copies = [
        pltpu.make_async_copy(here[n], outs[n].at[:, span], sems.at[n]) for n in range(3)
    ]
    for copy in copies:
        copy.start()
    rows, cols = triangle(size)
    for apart in range(GROUPS):
        for pair in range(per_owner // 2):
            start = 2 * per_owner * size + pair * (size + EXTRA)
            both = carried[apart][start : start + size].astype(F32)
            diagonal = carried[apart][start + size : start + size + EXTRA][:1].astype(F32)
            turned = both.T
            first = jnp.where(rows >= cols, both, turned)
            second = jnp.where(rows < cols, both, turned)
            second = jnp.where(rows == cols, diagonal, second)
            for i, whole in ((2 * pair, first), (2 * pair + 1, second)):
                slot = (chip ^ apart) * per_owner + i
                head = half * (GROUPS * per_owner) + slot
                map_here[slot] = dot_nn(whole.astype(BF16), w[head]) * scale
    count = GROUPS * per_owner
    copies.append(
        pltpu.make_async_copy(map_here, outs[3].at[pl.ds(half * count, count)], sems.at[3])
    )
    copies[-1].start()
    for copy in copies:
        copy.wait()


def swap(x, apart):
    count = lax.axis_size("ctx")
    return lax.ppermute(x, "ctx", [(i, i ^ apart) for i in range(count)])


def paired(q, k, v, g, w):
    rows, width = q.shape
    heads, size = w.shape[0], w.shape[-1]
    per_owner = heads // (2 * GROUPS)
    length = rows * lax.axis_size("ctx")
    block = (size, size)
    one = (GROUPS, per_owner) + block
    both = (GROUPS, 2, per_owner) + block
    twice = (2,) + one
    state = (2, per_owner) + block
    pack_shape = (per_owner // 2, size + EXTRA, size)
    payload = (2 * per_owner * size + (per_owner // 2) * (size + EXTRA), size)
    bind = functools.partial

    *here, send = call(
        bind(load_body, per_owner),
        [((rows, width), BF16)] * 4 + [(both, BF16)],
        (q, k, v, g),
        2.0,
        in_spec=HBM,
        scratch=[pltpu.SemaphoreType.DMA((2, 4))],
    )
    other = swap(send, 1)
    own, extra_c, part_q1 = call(
        bind(near_body, per_owner), [(both, BF16), (twice, BF16), (one, F32)], here, 1.4
    )
    chip_states = call(add_body, [(state, BF16)] * GROUPS, (own, other), 0.2)
    parts = [chip_states[0]] + [swap(chip_states[j], 2 * j) for j in range(1, GROUPS)]
    extra_c = swap(extra_c, 1)
    own_c, part_q0 = call(
        bind(own_body, per_owner),
        [(one, BF16), (one, F32)],
        here,
        1.0,
        after=chip_states[:1],
    )
    chip_c = call(
        bind(pack_body, per_owner),
        [(pack_shape, BF16)] * GROUPS,
        (own, other, own_c, extra_c),
        0.4,
    )
    packed = [chip_c[0]] + [swap(chip_c[j], 2 * j) for j in range(1, GROUPS)]
    part_k, part_v, key_w, gram = call(
        bind(rest_body, per_owner),
        [(twice, F32), (twice, F32), (twice, BF16), (twice, BF16)],
        (*here, w),
        1.8,
        after=chip_c[:1],
    )
    carried = call(
        bind(owner_body, per_owner),
        [(payload, BF16)] * GROUPS,
        (*parts, *packed),
        0.5,
        after=(gram,),
    )
    near = [carried[0]] + [swap(carried[j], 2 * j) for j in range(1, GROUPS)]
    far = [swap(x, 1) for x in near]
    outs = [((rows, width), BF16)] * 3 + [((heads,) + block, F32)]
    scale = 1.0 / math.sqrt(length)

    def tail(which, part_q, other_states, payloads, before):
        return call(
            bind(tail_body, which, per_owner, scale),
            outs,
            (*here, w, key_w, gram, part_q, part_k, part_v, other_states, *payloads),
            1.6,
            after=before,
            scratch=[pltpu.VMEM((rows, width // 2), BF16)] * 3
            + [pltpu.VMEM((heads // 2,) + block, F32), pltpu.SemaphoreType.DMA((4,))],
            out_specs=[HBM] * 4,
            aliases={11 + GROUPS + n: n for n in range(len(before))},
        )

    first = tail(0, part_q0, other, near, ())
    return tuple(tail(1, part_q1, extra_c, far, tuple(first)))


def gathered(q, k, v, g, w):
    rows, width = q.shape
    heads, size = w.shape[0], w.shape[-1]
    count = lax.axis_size("ctx")
    me = lax.axis_index("ctx")
    q, k, v, g = (x.reshape(rows, heads, size) for x in (q, k, v, g))

    def mul(spec, a, b):
        return jnp.einsum(spec, a, b, preferred_element_type=F32)

    query_feat = mul("thd,hde->the", q, w).astype(BF16)
    key_feat = mul("thd,hde->the", k, w).astype(BF16)
    key_state = mul("the,thv->hev", key_feat, v).astype(BF16)
    grad_state = mul("the,thv->hev", query_feat, g).astype(BF16)
    index = jnp.arange(count).reshape(count, 1, 1, 1)
    keys = lax.all_gather(key_state, "ctx").astype(F32)
    prefix = jnp.sum(jnp.where(index < me, keys, 0.0), 0).astype(BF16)
    grads = lax.all_gather(grad_state, "ctx").astype(F32)
    suffix = jnp.sum(jnp.where(index > me, grads, 0.0), 0).astype(BF16)
    row, col = triangle(rows)
    causal = row >= col
    scores = jnp.where(causal, mul("the,she->hts", query_feat, key_feat), 0.0).astype(BF16)
    mixing = jnp.where(causal, mul("thv,shv->hts", g, v), 0.0).astype(BF16)
    feat_q = mul("hts,she->the", mixing, key_feat) + mul("thv,hev->the", g, prefix)
    feat_k = mul("hts,the->she", mixing, query_feat) + mul("shv,hev->she", v, suffix)
    feat_q, feat_k = feat_q.astype(BF16), feat_k.astype(BF16)
    value_grad = mul("hts,thv->shv", scores, g) + mul("she,hev->shv", key_feat, suffix)
    query_grad = mul("the,hde->thd", feat_q, w)
    key_grad = mul("the,hde->thd", feat_k, w)
    local = mul("thd,the->hde", q, feat_q) + mul("thd,the->hde", k, feat_k)
    map_grad = lax.psum(local.astype(BF16).astype(F32), "ctx") / math.sqrt(rows * count)
    flat = (rows, width)
    return (
        query_grad.reshape(flat).astype(BF16),
        key_grad.reshape(flat).astype(BF16),
        value_grad.reshape(flat).astype(BF16),
        map_grad,
    )


def per_device(queries, key_rows, values, out_grad, feature_map):
    fits = lax.axis_size("ctx") == 2 * GROUPS and feature_map.shape[0] % (4 * GROUPS) == 0
    plan = paired if fits else gathered
    return plan(queries, key_rows, values, out_grad, feature_map)


def solution(mesh):
    rows = P(("seq", "ctx"), None)
    return jax.shard_map(
        per_device,
        mesh=mesh,
        in_specs=(rows, rows, rows, rows, P()),
        out_specs=(rows, rows, rows, P("seq", None, None)),
        check_vma=False,
    )
```

```python
import functools
import math

import jax
import jax.numpy as jnp
from jax import lax
from jax.experimental import pallas as pl
from jax.experimental.pallas import tpu as pltpu
from jax.sharding import PartitionSpec as P

F32 = jnp.float32
BF16 = jnp.bfloat16
VMEM = pl.BlockSpec(memory_space=pltpu.VMEM)
HBM = pl.BlockSpec(memory_space=pltpu.HBM)
ANY = pl.BlockSpec(memory_space=pl.ANY)
GROUPS = 4
EXTRA = 16


def dot_nn(a, b):
    return lax.dot_general(a, b, (((1,), (0,)), ((), ())), preferred_element_type=F32)


def dot_nt(a, b):
    return lax.dot_general(a, b, (((1,), (1,)), ((), ())), preferred_element_type=F32)


def dot_tn(a, b):
    return lax.dot_general(a, b, (((0,), (0,)), ((), ())), preferred_element_type=F32)


def call(body, outs, operands, cost, after=(), scratch=(), in_spec=VMEM, out_specs=None, aliases=None):
    count = len(operands)

    def run(*refs):
        return body(*refs[:count], *refs[count + len(after) :])

    return pl.pallas_call(
        run,
        out_shape=[jax.ShapeDtypeStruct(shape, dtype) for shape, dtype in outs],
        in_specs=[in_spec] * count + [ANY] * len(after),
        out_specs=out_specs or [VMEM] * len(outs),
        scratch_shapes=list(scratch),
        input_output_aliases=aliases or {},
        cost_estimate=pl.CostEstimate(
            flops=int(cost * 1.15e9), bytes_accessed=0, transcendentals=0
        ),
        compiler_params=pltpu.CompilerParams(vmem_limit_bytes=16 * 2**20),
    )(*operands, *after)


def place():
    me = lax.axis_index("ctx")
    return lax.rem(me, 2), lax.div(me, 2)


def owned(half, chip, per_owner):
    base = half * (GROUPS * per_owner)
    return [
        (apart, i, base + (chip ^ apart) * per_owner + i)
        for apart in range(GROUPS)
        for i in range(per_owner)
    ]


def columns(head, size):
    return pl.ds(pl.multiple_of(head * size, size), size)


def triangle(size):
    rows = lax.broadcasted_iota(jnp.int32, (size, size), 0)
    cols = lax.broadcasted_iota(jnp.int32, (size, size), 1)
    return rows, cols


def load_body(per_owner, q, k, v, g, q_here, k_here, v_here, g_here, send, part_q, sems):
    half_width = q.shape[1] // 2
    core, chip = place()
    pairs = ((k, k_here), (v, v_here), (q, q_here), (g, g_here))
    copies = []
    for turn, half in enumerate((1 - core, core)):
        at = columns(half, half_width)
        for n, (source, target) in enumerate(pairs):
            copy = pltpu.make_async_copy(source.at[:, at], target.at[:, at], sems.at[turn, n])
            copy.start()
            copies.append(copy)
    for copy in copies[:4]:
        copy.wait()
    half_states(owned(1 - core, chip, per_owner), q_here, k_here, v_here, g_here, send, part_q)
    for copy in copies[4:]:
        copy.wait()


def half_states(heads, q, k, v, g, out, part_q):
    size = out.shape[-1]
    rows, cols = triangle(q.shape[0])
    ats = [columns(head, size) for _, _, head in heads]
    mixing = [dot_nt(g[:, at], v[:, at]) for at in ats]
    mixing = [jnp.where(rows >= cols, x, 0.0).astype(BF16) for x in mixing]
    mixed = [dot_nn(x, k[:, at]) for x, at in zip(mixing, ats)]
    early = [dot_tn(k[:, at], v[:, at]) for at in ats]
    late = [dot_tn(q[:, at], g[:, at]) for at in ats]
    cross = [dot_tn(q[:, at], x.astype(BF16)) for x, at in zip(mixed, ats)]
    for n, (apart, i, _) in enumerate(heads):
        part_q[apart, i] = mixed[n]
        for kind, states in enumerate((early, late, cross)):
            out[apart, kind, i] = states[n].astype(BF16)


def near_body(per_owner, q, k, v, g, own, extra, part_q):
    core, chip = place()
    heads = owned(core, chip, per_owner)
    half_states(heads, q, k, v, g, own, part_q)
    for apart, i, _ in heads:
        extra[apart, i] = jnp.where(core == 0, own[apart, 0, i], own[apart, 1, i])


def pack(first, second):
    size = first.shape[0]
    rows, cols = triangle(size)
    both = jnp.where(rows >= cols, first, second)
    diagonal = jnp.sum(jnp.where(rows == cols, second, 0.0), axis=0, keepdims=True)
    return both, jnp.broadcast_to(diagonal, (EXTRA, size))


def join_body(per_owner, own, other, *outs):
    size = own.shape[-1]
    core, _ = place()
    last = core == 1
    totals = []
    for apart in range(GROUPS):
        for i in range(per_owner):
            early = jnp.where(last, other[apart, 0, i], own[apart, 0, i])
            late = jnp.where(last, own[apart, 1, i], other[apart, 1, i])
            totals.append(dot_nt(late, early))
    for apart in range(GROUPS):
        for kind in range(2):
            for i in range(per_owner):
                start = (kind * per_owner + i) * size
                total = own[apart, kind, i].astype(F32) + other[apart, kind, i].astype(F32)
                outs[apart][start : start + size] = total.astype(BF16)
        for pair in range(per_owner // 2):
            sums = []
            for i in (2 * pair, 2 * pair + 1):
                total = totals[apart * per_owner + i]
                total += own[apart, 2, i].astype(F32) + other[apart, 2, i].astype(F32)
                sums.append(total + total.T)
            both, diagonal = pack(*sums)
            start = 2 * per_owner * size + pair * (size + EXTRA)
            outs[apart][start : start + size] = both.astype(BF16)
            outs[apart][start + size : start + size + EXTRA] = diagonal.astype(BF16)


def rest_body(per_owner, q, k, v, g, w, part_k, part_v, key_w, gram):
    size = w.shape[-1]
    core, chip = place()
    rows, cols = triangle(q.shape[0])
    later = cols >= rows
    for which, half in enumerate((core, 1 - core)):
        heads = owned(half, chip, per_owner)
        ats = [columns(head, size) for _, _, head in heads]
        square = [dot_nt(w[head], w[head]).astype(BF16) for _, _, head in heads]
        mixing = [dot_nt(v[:, at], g[:, at]) for at in ats]
        mixing = [jnp.where(later, x, 0.0).astype(BF16) for x in mixing]
        keyed = [dot_nn(k[:, at], x).astype(BF16) for x, at in zip(square, ats)]
        mixed = [dot_nn(x, q[:, at]) for x, at in zip(mixing, ats)]
        scores = [dot_nt(x, q[:, at]) for x, at in zip(keyed, ats)]
        scores = [jnp.where(later, x, 0.0).astype(BF16) for x in scores]
        scored = [dot_nn(x, g[:, at]) for x, at in zip(scores, ats)]
        for n, (apart, i, _) in enumerate(heads):
            gram[which, apart, i] = square[n]
            key_w[which, apart, i] = keyed[n]
            part_k[which, apart, i] = mixed[n]
            part_v[which, apart, i] = scored[n]


def owner_body(per_owner, *refs):
    parts, outs = refs[:GROUPS], refs[GROUPS:]
    size = outs[0].shape[-1]
    _, chip = place()
    turns = []
    for i in range(per_owner):
        ahead = slice(i * size, (i + 1) * size)
        behind = slice((per_owner + i) * size, (per_owner + i + 1) * size)
        early = [part[ahead].astype(F32) for part in parts]
        late = [part[behind].astype(F32) for part in parts]
        cross = None
        for to in range(GROUPS):
            prefix = jnp.zeros_like(early[0])
            suffix = jnp.zeros_like(early[0])
            for apart in range(GROUPS):
                if apart == to:
                    continue
                before = (chip ^ apart) < (chip ^ to)
                prefix += jnp.where(before, early[apart], 0.0)
                suffix += jnp.where(before, 0.0, late[apart])
            prefix = prefix.astype(BF16)
            outs[to][ahead] = prefix
            outs[to][behind] = suffix.astype(BF16)
            product = dot_nt(parts[to][behind], prefix)
            cross = product if cross is None else cross + product
        turns.append(cross + cross.T)
    for pair in range(per_owner // 2):
        both, diagonal = pack(turns[2 * pair], turns[2 * pair + 1])
        start = 2 * per_owner * size + pair * (size + EXTRA)
        for part in parts:
            both += part[start : start + size].astype(F32)
            diagonal += part[start + size : start + size + EXTRA].astype(F32)
        for out in outs:
            out[start : start + size] = both.astype(BF16)
            out[start + size : start + size + EXTRA] = diagonal.astype(BF16)


def tail_body(which, per_owner, scale, *refs):
    q, k, v, g, w, key_w, gram, part_q, part_k, part_v, near = refs[:11]
    carried = refs[11 : 11 + GROUPS]
    outs = refs[-9:-5]
    here = refs[-5:-1]
    sems = refs[-1]
    query_here, key_here, value_here, map_here = here
    size = gram.shape[-1]
    core, chip = place()
    half = 1 - core if which else core
    heads = owned(half, chip, per_owner)
    ats = [columns(head, size) for _, _, head in heads]
    slots = [columns((chip ^ apart) * per_owner + i, size) for apart, i, _ in heads]
    prefix, suffix = [], []
    for apart, i, _ in heads:
        if which:
            early = late = near[apart, i]
        else:
            early, late = near[apart, 0, i], near[apart, 1, i]
        before = carried[apart][i * size : (i + 1) * size].astype(F32)
        after = carried[apart][(per_owner + i) * size : (per_owner + i + 1) * size].astype(F32)
        prefix.append((before + jnp.where(core == 1, early.astype(F32), 0.0)).astype(BF16))
        suffix.append((after + jnp.where(core == 0, late.astype(F32), 0.0)).astype(BF16))
    raw_q = [dot_nt(g[:, at], x) for x, at in zip(prefix, ats)]
    raw_k = [dot_nt(v[:, at], x) for x, at in zip(suffix, ats)]
    raw_v = [dot_nn(key_w[which, a, i], x) for x, (a, i, _) in zip(suffix, heads)]
    raw_q = [(part_q[a, i] + x).astype(BF16) for x, (a, i, _) in zip(raw_q, heads)]
    raw_k = [(part_k[which, a, i] + x).astype(BF16) for x, (a, i, _) in zip(raw_k, heads)]
    for n, (a, i, _) in enumerate(heads):
        value_here[:, slots[n]] = (part_v[which, a, i] + raw_v[n]).astype(BF16)
    done_q = [dot_nn(x, gram[which, a, i]) for x, (a, i, _) in zip(raw_q, heads)]
    done_k = [dot_nn(x, gram[which, a, i]) for x, (a, i, _) in zip(raw_k, heads)]
    for n, slot in enumerate(slots):
        query_here[:, slot] = done_q[n].astype(BF16)
        key_here[:, slot] = done_k[n].astype(BF16)
    span = columns(half, q.shape[1] // 2)
    copies = [
        pltpu.make_async_copy(here[n], outs[n].at[:, span], sems.at[n]) for n in range(3)
    ]
    for copy in copies:
        copy.start()
    rows, cols = triangle(size)
    for apart in range(GROUPS):
        for pair in range(per_owner // 2):
            start = 2 * per_owner * size + pair * (size + EXTRA)
            both = carried[apart][start : start + size].astype(F32)
            diagonal = carried[apart][start + size : start + size + EXTRA][:1].astype(F32)
            turned = both.T
            first = jnp.where(rows >= cols, both, turned)
            second = jnp.where(rows < cols, both, turned)
            second = jnp.where(rows == cols, diagonal, second)
            for i, whole in ((2 * pair, first), (2 * pair + 1, second)):
                slot = (chip ^ apart) * per_owner + i
                head = half * (GROUPS * per_owner) + slot
                map_here[slot] = dot_nn(whole.astype(BF16), w[head]) * scale
    count = GROUPS * per_owner
    copies.append(
        pltpu.make_async_copy(map_here, outs[3].at[pl.ds(half * count, count)], sems.at[3])
    )
    copies[-1].start()
    for copy in copies:
        copy.wait()


def swap(x, apart):
    count = lax.axis_size("ctx")
    return lax.ppermute(x, "ctx", [(i, i ^ apart) for i in range(count)])


def paired(q, k, v, g, w):
    rows, width = q.shape
    heads, size = w.shape[0], w.shape[-1]
    per_owner = heads // (2 * GROUPS)
    length = rows * lax.axis_size("ctx")
    block = (size, size)
    one = (GROUPS, per_owner) + block
    triple = (GROUPS, 3, per_owner) + block
    twice = (2,) + one
    payload = (2 * per_owner * size + (per_owner // 2) * (size + EXTRA), size)
    bind = functools.partial

    *here, send, part_q1 = call(
        bind(load_body, per_owner),
        [((rows, width), BF16)] * 4 + [(triple, BF16), (one, F32)],
        [pltpu.with_memory_space_constraint(x, pltpu.HBM) for x in (q, k, v, g)],
        2.0,
        in_spec=HBM,
        scratch=[pltpu.SemaphoreType.DMA((2, 4))],
    )
    other = swap(send, 1)
    own, extra, part_q0 = call(
        bind(near_body, per_owner), [(triple, BF16), (one, BF16), (one, F32)], here, 1.0
    )
    chip_sums = call(bind(join_body, per_owner), [(payload, BF16)] * GROUPS, (own, other), 0.5)
    parts = [chip_sums[0]] + [swap(chip_sums[j], 2 * j) for j in range(1, GROUPS)]
    extra = swap(extra, 1)
    part_k, part_v, key_w, gram = call(
        bind(rest_body, per_owner),
        [(twice, F32), (twice, F32), (twice, BF16), (twice, BF16)],
        (*here, w),
        1.8,
        after=chip_sums[:1],
    )
    carried = call(
        bind(owner_body, per_owner), [(payload, BF16)] * GROUPS, parts, 0.5, after=(gram,)
    )
    near = [carried[0]] + [swap(carried[j], 2 * j) for j in range(1, GROUPS)]
    far = [swap(x, 1) for x in near]
    outs = [((rows, width), BF16)] * 3 + [((heads,) + block, F32)]
    scale = 1.0 / math.sqrt(length)

    def tail(which, part_q, other_states, payloads, before):
        return call(
            bind(tail_body, which, per_owner, scale),
            outs,
            (*here, w, key_w, gram, part_q, part_k, part_v, other_states, *payloads),
            1.6,
            after=before,
            scratch=[pltpu.VMEM((rows, width // 2), BF16)] * 3
            + [pltpu.VMEM((heads // 2,) + block, F32), pltpu.SemaphoreType.DMA((4,))],
            out_specs=[HBM] * 4,
            aliases={11 + GROUPS + n: n for n in range(len(before))},
        )

    first = tail(0, part_q0, other, near, ())
    return tuple(tail(1, part_q1, extra, far, tuple(first)))


def gathered(q, k, v, g, w):
    rows, width = q.shape
    heads, size = w.shape[0], w.shape[-1]
    count = lax.axis_size("ctx")
    me = lax.axis_index("ctx")
    q, k, v, g = (x.reshape(rows, heads, size) for x in (q, k, v, g))

    def mul(spec, a, b):
        return jnp.einsum(spec, a, b, preferred_element_type=F32)

    query_feat = mul("thd,hde->the", q, w).astype(BF16)
    key_feat = mul("thd,hde->the", k, w).astype(BF16)
    key_state = mul("the,thv->hev", key_feat, v).astype(BF16)
    grad_state = mul("the,thv->hev", query_feat, g).astype(BF16)
    index = jnp.arange(count).reshape(count, 1, 1, 1)
    keys = lax.all_gather(key_state, "ctx").astype(F32)
    prefix = jnp.sum(jnp.where(index < me, keys, 0.0), 0).astype(BF16)
    grads = lax.all_gather(grad_state, "ctx").astype(F32)
    suffix = jnp.sum(jnp.where(index > me, grads, 0.0), 0).astype(BF16)
    row, col = triangle(rows)
    causal = row >= col
    scores = jnp.where(causal, mul("the,she->hts", query_feat, key_feat), 0.0).astype(BF16)
    mixing = jnp.where(causal, mul("thv,shv->hts", g, v), 0.0).astype(BF16)
    feat_q = mul("hts,she->the", mixing, key_feat) + mul("thv,hev->the", g, prefix)
    feat_k = mul("hts,the->she", mixing, query_feat) + mul("shv,hev->she", v, suffix)
    feat_q, feat_k = feat_q.astype(BF16), feat_k.astype(BF16)
    value_grad = mul("hts,thv->shv", scores, g) + mul("she,hev->shv", key_feat, suffix)
    query_grad = mul("the,hde->thd", feat_q, w)
    key_grad = mul("the,hde->thd", feat_k, w)
    local = mul("thd,the->hde", q, feat_q) + mul("thd,the->hde", k, feat_k)
    map_grad = lax.psum(local.astype(BF16).astype(F32), "ctx") / math.sqrt(rows * count)
    flat = (rows, width)
    return (
        query_grad.reshape(flat).astype(BF16),
        key_grad.reshape(flat).astype(BF16),
        value_grad.reshape(flat).astype(BF16),
        map_grad,
    )


def per_device(queries, key_rows, values, out_grad, feature_map):
    fits = lax.axis_size("ctx") == 2 * GROUPS and feature_map.shape[0] % (4 * GROUPS) == 0
    plan = paired if fits else gathered
    return plan(queries, key_rows, values, out_grad, feature_map)


def solution(mesh):
    rows = P(("seq", "ctx"), None)
    return jax.shard_map(
        per_device,
        mesh=mesh,
        in_specs=(rows, rows, rows, rows, P()),
        out_specs=(rows, rows, rows, P("seq", None, None)),
        check_vma=False,
    )
```

```python
import functools
import math

import jax
import jax.numpy as jnp
from jax import lax
from jax.experimental import pallas as pl
from jax.experimental.pallas import tpu as pltpu
from jax.sharding import PartitionSpec as P

F32 = jnp.float32
BF16 = jnp.bfloat16
VMEM = pl.BlockSpec(memory_space=pltpu.VMEM)
HBM = pl.BlockSpec(memory_space=pltpu.HBM)
ANY = pl.BlockSpec(memory_space=pl.ANY)
GROUPS = 4
FIRST = 0
EXTRA = 16


def dot_nn(a, b):
    return lax.dot_general(a, b, (((1,), (0,)), ((), ())), preferred_element_type=F32)


def dot_nt(a, b):
    return lax.dot_general(a, b, (((1,), (1,)), ((), ())), preferred_element_type=F32)


def dot_tn(a, b):
    return lax.dot_general(a, b, (((0,), (0,)), ((), ())), preferred_element_type=F32)


def call(
    body, outs, operands, cost, after=(), scratch=(), in_spec=VMEM, out_specs=None, aliases=None, in_after=ANY
):
    count = len(operands)

    def run(*refs):
        return body(*refs[:count], *refs[count + len(after) :])

    return pl.pallas_call(
        run,
        out_shape=[jax.ShapeDtypeStruct(shape, dtype) for shape, dtype in outs],
        in_specs=[in_spec] * count + [in_after] * len(after),
        out_specs=out_specs or [VMEM] * len(outs),
        scratch_shapes=list(scratch),
        input_output_aliases=aliases or {},
        cost_estimate=pl.CostEstimate(
            flops=int(cost * 1.15e9), bytes_accessed=0, transcendentals=0
        ),
        compiler_params=pltpu.CompilerParams(vmem_limit_bytes=16 * 2**20),
    )(*operands, *after)


def place():
    me = lax.axis_index("ctx")
    return lax.rem(me, 2), lax.div(me, 2)


def owned(half, chip, per_owner):
    base = half * (GROUPS * per_owner)
    return [
        (apart, i, base + (chip ^ apart) * per_owner + i)
        for apart in range(GROUPS)
        for i in range(per_owner)
    ]


def columns(head, size):
    return pl.ds(pl.multiple_of(head * size, size), size)


def triangle(size):
    rows = lax.broadcasted_iota(jnp.int32, (size, size), 0)
    cols = lax.broadcasted_iota(jnp.int32, (size, size), 1)
    return rows, cols


def load_body(per_owner, q, k, v, g, q_here, k_here, v_here, g_here, send, part_q, sems):
    half_width = q.shape[1] // 2
    core, chip = place()
    pairs = ((k, k_here), (v, v_here), (q, q_here), (g, g_here))
    copies = []
    for turn, half in enumerate((1 - core, core)):
        at = columns(half, half_width)
        for n, (source, target) in enumerate(pairs):
            copy = pltpu.make_async_copy(source.at[:, at], target.at[:, at], sems.at[turn, n])
            copy.start()
            copies.append(copy)
    for copy in copies[:4]:
        copy.wait()
    half_states(owned(1 - core, chip, per_owner), q_here, k_here, v_here, g_here, send, part_q)
    for copy in copies[4:]:
        copy.wait()


def half_states(heads, q, k, v, g, out, part_q):
    size = out.shape[-1]
    rows, cols = triangle(q.shape[0])
    ats = [columns(head, size) for _, _, head in heads]
    mixing = [dot_nt(g[:, at], v[:, at]) for at in ats]
    mixing = [jnp.where(rows >= cols, x, 0.0).astype(BF16) for x in mixing]
    mixed = [dot_nn(x, k[:, at]) for x, at in zip(mixing, ats)]
    early = [dot_tn(k[:, at], v[:, at]) for at in ats]
    late = [dot_tn(q[:, at], g[:, at]) for at in ats]
    cross = [dot_tn(q[:, at], x.astype(BF16)) for x, at in zip(mixed, ats)]
    for n, (apart, i, _) in enumerate(heads):
        part_q[apart, i] = mixed[n]
        for kind, states in enumerate((early, late, cross)):
            out[apart, kind, i] = states[n].astype(BF16)


def near_body(per_owner, q, k, v, g, own, extra, part_q):
    core, chip = place()
    heads = owned(core, chip, per_owner)
    half_states(heads, q, k, v, g, own, part_q)
    for apart, i, _ in heads:
        extra[apart, i] = jnp.where(core == 0, own[apart, 0, i], own[apart, 1, i])


def pack(first, second):
    size = first.shape[0]
    rows, cols = triangle(size)
    both = jnp.where(rows >= cols, first, second)
    both += jnp.where(rows <= cols, first, second).T
    diagonal = 2.0 * jnp.sum(jnp.where(rows == cols, second, 0.0), axis=0, keepdims=True)
    return both, jnp.broadcast_to(diagonal, (EXTRA, size))


def join_body(per_owner, own, other, *outs):
    size = own.shape[-1]
    core, _ = place()
    last = core == 1
    totals = []
    for apart in range(GROUPS):
        for i in range(per_owner):
            early = jnp.where(last, other[apart, 0, i], own[apart, 0, i])
            late = jnp.where(last, own[apart, 1, i], other[apart, 1, i])
            totals.append(dot_nt(late, early))
    for apart in range(GROUPS):
        for kind in range(2):
            for i in range(per_owner):
                start = (kind * per_owner + i) * size
                total = own[apart, kind, i].astype(F32) + other[apart, kind, i].astype(F32)
                outs[apart][start : start + size] = total.astype(BF16)
        for pair in range(per_owner // 2):
            sums = []
            for i in (2 * pair, 2 * pair + 1):
                total = totals[apart * per_owner + i]
                sums.append(total + own[apart, 2, i].astype(F32) + other[apart, 2, i].astype(F32))
            both, diagonal = pack(*sums)
            start = 2 * per_owner * size + pair * (size + EXTRA)
            outs[apart][start : start + size] = both.astype(BF16)
            outs[apart][start + size : start + size + EXTRA] = diagonal.astype(BF16)


def rest_first_body(per_owner, *refs):
    core, _ = place()

    @pl.when(core == FIRST)
    def _():
        rest(per_owner, *refs)


def rest_second_body(per_owner, *refs):
    core, _ = place()

    @pl.when(core != FIRST)
    def _():
        rest(per_owner, *refs[:5], *refs[-4:])


def rest(per_owner, q, k, v, g, w, part_k, part_v, key_w, gram):
    size = w.shape[-1]
    core, chip = place()
    rows, cols = triangle(q.shape[0])
    later = cols >= rows
    for which, half in enumerate((core, 1 - core)):
        heads = owned(half, chip, per_owner)
        ats = [columns(head, size) for _, _, head in heads]
        square = [dot_nt(w[head], w[head]).astype(BF16) for _, _, head in heads]
        mixing = [dot_nt(v[:, at], g[:, at]) for at in ats]
        mixing = [jnp.where(later, x, 0.0).astype(BF16) for x in mixing]
        keyed = [dot_nn(k[:, at], x).astype(BF16) for x, at in zip(square, ats)]
        mixed = [dot_nn(x, q[:, at]) for x, at in zip(mixing, ats)]
        scores = [dot_nt(x, q[:, at]) for x, at in zip(keyed, ats)]
        scores = [jnp.where(later, x, 0.0).astype(BF16) for x in scores]
        scored = [dot_nn(x, g[:, at]) for x, at in zip(scores, ats)]
        for n, (apart, i, _) in enumerate(heads):
            gram[which, apart, i] = square[n]
            key_w[which, apart, i] = keyed[n]
            part_k[which, apart, i] = mixed[n]
            part_v[which, apart, i] = scored[n]


def owner_body(per_owner, *refs):
    parts, outs = refs[:GROUPS], refs[GROUPS:]
    size = outs[0].shape[-1]
    _, chip = place()
    turns = []
    for i in range(per_owner):
        ahead = slice(i * size, (i + 1) * size)
        behind = slice((per_owner + i) * size, (per_owner + i + 1) * size)
        early = [part[ahead].astype(F32) for part in parts]
        late = [part[behind].astype(F32) for part in parts]
        cross = None
        for to in range(GROUPS):
            prefix = jnp.zeros_like(early[0])
            suffix = jnp.zeros_like(early[0])
            for apart in range(GROUPS):
                if apart == to:
                    continue
                before = (chip ^ apart) < (chip ^ to)
                prefix += jnp.where(before, early[apart], 0.0)
                suffix += jnp.where(before, 0.0, late[apart])
            prefix = prefix.astype(BF16)
            outs[to][ahead] = prefix
            outs[to][behind] = suffix.astype(BF16)
            product = dot_nt(parts[to][behind], prefix)
            cross = product if cross is None else cross + product
        turns.append(cross)
    for pair in range(per_owner // 2):
        both, diagonal = pack(turns[2 * pair], turns[2 * pair + 1])
        start = 2 * per_owner * size + pair * (size + EXTRA)
        for part in parts:
            both += part[start : start + size].astype(F32)
            diagonal += part[start + size : start + size + EXTRA].astype(F32)
        for out in outs:
            out[start : start + size] = both.astype(BF16)
            out[start + size : start + size + EXTRA] = diagonal.astype(BF16)


def tail_body(which, per_owner, scale, *refs):
    q, k, v, g, w, key_w, gram, part_q, part_k, part_v, near = refs[:11]
    carried = refs[11 : 11 + GROUPS]
    outs = refs[-9:-5]
    here = refs[-5:-1]
    sems = refs[-1]
    query_here, key_here, value_here, map_here = here
    size = gram.shape[-1]
    core, chip = place()
    half = 1 - core if which else core
    heads = owned(half, chip, per_owner)
    ats = [columns(head, size) for _, _, head in heads]
    slots = [columns((chip ^ apart) * per_owner + i, size) for apart, i, _ in heads]
    prefix, suffix = [], []
    for apart, i, _ in heads:
        if which:
            early = late = near[apart, i]
        else:
            early, late = near[apart, 0, i], near[apart, 1, i]
        before = carried[apart][i * size : (i + 1) * size].astype(F32)
        after = carried[apart][(per_owner + i) * size : (per_owner + i + 1) * size].astype(F32)
        prefix.append((before + jnp.where(core == 1, early.astype(F32), 0.0)).astype(BF16))
        suffix.append((after + jnp.where(core == 0, late.astype(F32), 0.0)).astype(BF16))
    raw_q = [dot_nt(g[:, at], x) for x, at in zip(prefix, ats)]
    raw_k = [dot_nt(v[:, at], x) for x, at in zip(suffix, ats)]
    raw_v = [dot_nn(key_w[which, a, i], x) for x, (a, i, _) in zip(suffix, heads)]
    raw_q = [(part_q[a, i] + x).astype(BF16) for x, (a, i, _) in zip(raw_q, heads)]
    raw_k = [(part_k[which, a, i] + x).astype(BF16) for x, (a, i, _) in zip(raw_k, heads)]
    for n, (a, i, _) in enumerate(heads):
        value_here[:, slots[n]] = (part_v[which, a, i] + raw_v[n]).astype(BF16)
    done_q = [dot_nn(x, gram[which, a, i]) for x, (a, i, _) in zip(raw_q, heads)]
    done_k = [dot_nn(x, gram[which, a, i]) for x, (a, i, _) in zip(raw_k, heads)]
    for n, slot in enumerate(slots):
        query_here[:, slot] = done_q[n].astype(BF16)
        key_here[:, slot] = done_k[n].astype(BF16)
    span = columns(half, q.shape[1] // 2)
    copies = [
        pltpu.make_async_copy(here[n], outs[n].at[:, span], sems.at[n]) for n in range(3)
    ]
    for copy in copies:
        copy.start()
    rows, cols = triangle(size)
    for apart in range(GROUPS):
        for pair in range(per_owner // 2):
            start = 2 * per_owner * size + pair * (size + EXTRA)
            both = carried[apart][start : start + size].astype(F32)
            diagonal = carried[apart][start + size : start + size + EXTRA][:1].astype(F32)
            turned = both.T
            first = jnp.where(rows >= cols, both, turned)
            second = jnp.where(rows < cols, both, turned)
            second = jnp.where(rows == cols, diagonal, second)
            for i, whole in ((2 * pair, first), (2 * pair + 1, second)):
                slot = (chip ^ apart) * per_owner + i
                head = half * (GROUPS * per_owner) + slot
                map_here[slot] = dot_nn(whole.astype(BF16), w[head]) * scale
    count = GROUPS * per_owner
    copies.append(
        pltpu.make_async_copy(map_here, outs[3].at[pl.ds(half * count, count)], sems.at[3])
    )
    copies[-1].start()
    for copy in copies:
        copy.wait()


def swap(x, apart):
    count = lax.axis_size("ctx")
    return lax.ppermute(x, "ctx", [(i, i ^ apart) for i in range(count)])


def paired(q, k, v, g, w):
    rows, width = q.shape
    heads, size = w.shape[0], w.shape[-1]
    per_owner = heads // (2 * GROUPS)
    length = rows * lax.axis_size("ctx")
    block = (size, size)
    one = (GROUPS, per_owner) + block
    triple = (GROUPS, 3, per_owner) + block
    twice = (2,) + one
    payload = (2 * per_owner * size + (per_owner // 2) * (size + EXTRA), size)
    bind = functools.partial

    *here, send, part_q1 = call(
        bind(load_body, per_owner),
        [((rows, width), BF16)] * 4 + [(triple, BF16), (one, F32)],
        [pltpu.with_memory_space_constraint(x, pltpu.HBM) for x in (q, k, v, g)],
        2.0,
        in_spec=HBM,
        scratch=[pltpu.SemaphoreType.DMA((2, 4))],
    )
    other = swap(send, 1)
    own, extra, part_q0 = call(
        bind(near_body, per_owner), [(triple, BF16), (one, BF16), (one, F32)], here, 1.0
    )
    chip_sums = call(bind(join_body, per_owner), [(payload, BF16)] * GROUPS, (own, other), 0.5)
    locals_ = [(twice, F32), (twice, F32), (twice, BF16), (twice, BF16)]
    local = list(
        call(bind(rest_first_body, per_owner), locals_, (*here, w), 1.8, after=chip_sums[:1])
    )
    held = lax.optimization_barrier((*chip_sums, local[0]))
    chip_sums, local[0] = list(held[:GROUPS]), held[GROUPS]
    parts = [chip_sums[0]] + [swap(chip_sums[j], 2 * j) for j in range(1, GROUPS)]
    extra = swap(extra, 1)
    local = call(
        bind(rest_second_body, per_owner),
        locals_,
        (*here, w),
        1.8,
        after=tuple(local),
        aliases={5 + n: n for n in range(4)},
        in_after=VMEM,
    )
    part_k, part_v, key_w, gram = local
    carried = call(
        bind(owner_body, per_owner), [(payload, BF16)] * GROUPS, parts, 0.5, after=(gram,)
    )
    near = [carried[0]] + [swap(carried[j], 2 * j) for j in range(1, GROUPS)]
    far = [swap(x, 1) for x in near]
    outs = [((rows, width), BF16)] * 3 + [((heads,) + block, F32)]
    scale = 1.0 / math.sqrt(length)

    def tail(which, part_q, other_states, payloads, before):
        return call(
            bind(tail_body, which, per_owner, scale),
            outs,
            (*here, w, key_w, gram, part_q, part_k, part_v, other_states, *payloads),
            1.6,
            after=before,
            scratch=[pltpu.VMEM((rows, width // 2), BF16)] * 3
            + [pltpu.VMEM((heads // 2,) + block, F32), pltpu.SemaphoreType.DMA((4,))],
            out_specs=[HBM] * 4,
            aliases={11 + GROUPS + n: n for n in range(len(before))},
        )

    first = tail(0, part_q0, other, near, ())
    return tuple(tail(1, part_q1, extra, far, tuple(first)))


def gathered(q, k, v, g, w):
    rows, width = q.shape
    heads, size = w.shape[0], w.shape[-1]
    count = lax.axis_size("ctx")
    me = lax.axis_index("ctx")
    q, k, v, g = (x.reshape(rows, heads, size) for x in (q, k, v, g))

    def mul(spec, a, b):
        return jnp.einsum(spec, a, b, preferred_element_type=F32)

    query_feat = mul("thd,hde->the", q, w).astype(BF16)
    key_feat = mul("thd,hde->the", k, w).astype(BF16)
    key_state = mul("the,thv->hev", key_feat, v).astype(BF16)
    grad_state = mul("the,thv->hev", query_feat, g).astype(BF16)
    index = jnp.arange(count).reshape(count, 1, 1, 1)
    keys = lax.all_gather(key_state, "ctx").astype(F32)
    prefix = jnp.sum(jnp.where(index < me, keys, 0.0), 0).astype(BF16)
    grads = lax.all_gather(grad_state, "ctx").astype(F32)
    suffix = jnp.sum(jnp.where(index > me, grads, 0.0), 0).astype(BF16)
    row, col = triangle(rows)
    causal = row >= col
    scores = jnp.where(causal, mul("the,she->hts", query_feat, key_feat), 0.0).astype(BF16)
    mixing = jnp.where(causal, mul("thv,shv->hts", g, v), 0.0).astype(BF16)
    feat_q = mul("hts,she->the", mixing, key_feat) + mul("thv,hev->the", g, prefix)
    feat_k = mul("hts,the->she", mixing, query_feat) + mul("shv,hev->she", v, suffix)
    feat_q, feat_k = feat_q.astype(BF16), feat_k.astype(BF16)
    value_grad = mul("hts,thv->shv", scores, g) + mul("she,hev->shv", key_feat, suffix)
    query_grad = mul("the,hde->thd", feat_q, w)
    key_grad = mul("the,hde->thd", feat_k, w)
    local = mul("thd,the->hde", q, feat_q) + mul("thd,the->hde", k, feat_k)
    map_grad = lax.psum(local.astype(BF16).astype(F32), "ctx") / math.sqrt(rows * count)
    flat = (rows, width)
    return (
        query_grad.reshape(flat).astype(BF16),
        key_grad.reshape(flat).astype(BF16),
        value_grad.reshape(flat).astype(BF16),
        map_grad,
    )


def per_device(queries, key_rows, values, out_grad, feature_map):
    fits = lax.axis_size("ctx") == 2 * GROUPS and feature_map.shape[0] % (4 * GROUPS) == 0
    plan = paired if fits else gathered
    return plan(queries, key_rows, values, out_grad, feature_map)


def solution(mesh):
    rows = P(("seq", "ctx"), None)
    return jax.shard_map(
        per_device,
        mesh=mesh,
        in_specs=(rows, rows, rows, rows, P()),
        out_specs=(rows, rows, rows, P("seq", None, None)),
        check_vma=False,
    )
```

```python
import functools
import math

import jax
import jax.numpy as jnp
from jax import lax
from jax.experimental import pallas as pl
from jax.experimental.pallas import tpu as pltpu
from jax.sharding import PartitionSpec as P

F32 = jnp.float32
BF16 = jnp.bfloat16
VMEM = pl.BlockSpec(memory_space=pltpu.VMEM)
HBM = pl.BlockSpec(memory_space=pltpu.HBM)
ANY = pl.BlockSpec(memory_space=pl.ANY)
GROUPS = 4
FIRST = 0
EXTRA = 16


def dot_nn(a, b):
    return lax.dot_general(a, b, (((1,), (0,)), ((), ())), preferred_element_type=F32)


def dot_nt(a, b):
    return lax.dot_general(a, b, (((1,), (1,)), ((), ())), preferred_element_type=F32)


def dot_tn(a, b):
    return lax.dot_general(a, b, (((0,), (0,)), ((), ())), preferred_element_type=F32)


def call(
    body, outs, operands, cost, after=(), scratch=(), in_spec=None, out_specs=None, aliases=None, in_after=ANY
):
    count = len(operands)

    def run(*refs):
        return body(*refs[:count], *refs[count + len(after) :])

    return pl.pallas_call(
        run,
        out_shape=[jax.ShapeDtypeStruct(shape, dtype) for shape, dtype in outs],
        in_specs=(in_spec or [VMEM] * count) + [in_after] * len(after),
        out_specs=out_specs or [VMEM] * len(outs),
        scratch_shapes=list(scratch),
        input_output_aliases=aliases or {},
        cost_estimate=pl.CostEstimate(
            flops=int(cost * 1.15e9), bytes_accessed=0, transcendentals=0
        ),
        compiler_params=pltpu.CompilerParams(vmem_limit_bytes=16 * 2**20),
    )(*operands, *after)


def place():
    me = lax.axis_index("ctx")
    return lax.rem(me, 2), lax.div(me, 2)


def owned(half, chip, per_owner):
    base = half * (GROUPS * per_owner)
    return [
        (apart, i, base + (chip ^ apart) * per_owner + i)
        for apart in range(GROUPS)
        for i in range(per_owner)
    ]


def columns(head, size):
    return pl.ds(pl.multiple_of(head * size, size), size)


def triangle(size):
    rows = lax.broadcasted_iota(jnp.int32, (size, size), 0)
    cols = lax.broadcasted_iota(jnp.int32, (size, size), 1)
    return rows, cols


def load_body(per_owner, q, k, v, g, q_here, k_here, v_here, g_here, send, part_q, sems):
    half_width = q.shape[1] // 2
    core, chip = place()
    pairs = ((k, k_here), (v, v_here), (q, q_here), (g, g_here))
    copies = []
    for turn, half in enumerate((1 - core, core)):
        at = columns(half, half_width)
        for n, (source, target) in enumerate(pairs):
            copy = pltpu.make_async_copy(source.at[:, at], target.at[:, at], sems.at[turn, n])
            copy.start()
            copies.append(copy)
    for copy in copies[:4]:
        copy.wait()
    half_states(owned(1 - core, chip, per_owner), q_here, k_here, v_here, g_here, send, part_q)
    for copy in copies[4:]:
        copy.wait()


def half_states(heads, q, k, v, g, out, part_q):
    size = out.shape[-1]
    rows, cols = triangle(q.shape[0])
    ats = [columns(head, size) for _, _, head in heads]
    mixing = [dot_nt(g[:, at], v[:, at]) for at in ats]
    mixing = [jnp.where(rows >= cols, x, 0.0).astype(BF16) for x in mixing]
    mixed = [dot_nn(x, k[:, at]) for x, at in zip(mixing, ats)]
    early = [dot_tn(k[:, at], v[:, at]) for at in ats]
    late = [dot_tn(q[:, at], g[:, at]) for at in ats]
    cross = [dot_tn(q[:, at], x.astype(BF16)) for x, at in zip(mixed, ats)]
    for n, (apart, i, _) in enumerate(heads):
        part_q[apart, i] = mixed[n]
        for kind, states in enumerate((early, late, cross)):
            out[apart, kind, i] = states[n].astype(BF16)


def near_body(per_owner, q, k, v, g, w, own, extra, part_q, w_here, sem):
    core, chip = place()
    copy = pltpu.make_async_copy(w, w_here, sem)
    copy.start()
    heads = owned(core, chip, per_owner)
    half_states(heads, q, k, v, g, own, part_q)
    for apart, i, _ in heads:
        extra[apart, i] = jnp.where(core == 0, own[apart, 0, i], own[apart, 1, i])
    copy.wait()


def pack(first, second):
    size = first.shape[0]
    rows, cols = triangle(size)
    both = jnp.where(rows >= cols, first, second)
    both += jnp.where(rows <= cols, first, second).T
    diagonal = 2.0 * jnp.sum(jnp.where(rows == cols, second, 0.0), axis=0, keepdims=True)
    return both, jnp.broadcast_to(diagonal, (EXTRA, size))


def join_body(per_owner, own, other, *outs):
    size = own.shape[-1]
    core, _ = place()
    last = core == 1
    totals = []
    for apart in range(GROUPS):
        for i in range(per_owner):
            early = jnp.where(last, other[apart, 0, i], own[apart, 0, i])
            late = jnp.where(last, own[apart, 1, i], other[apart, 1, i])
            totals.append(dot_nt(late, early))
    for apart in range(GROUPS):
        for kind in range(2):
            for i in range(per_owner):
                start = (kind * per_owner + i) * size
                outs[apart][start : start + size] = own[apart, kind, i] + other[apart, kind, i]
        for pair in range(per_owner // 2):
            sums = []
            for i in (2 * pair, 2 * pair + 1):
                total = totals[apart * per_owner + i]
                sums.append(total + own[apart, 2, i].astype(F32) + other[apart, 2, i].astype(F32))
            both, diagonal = pack(*sums)
            start = 2 * per_owner * size + pair * (size + EXTRA)
            outs[apart][start : start + size] = both.astype(BF16)
            outs[apart][start + size : start + size + EXTRA] = diagonal.astype(BF16)


def rest_first_body(per_owner, *refs):
    core, _ = place()

    @pl.when(core == FIRST)
    def _():
        rest(per_owner, *refs)


def rest_second_body(per_owner, *refs):
    core, _ = place()

    @pl.when(core != FIRST)
    def _():
        rest(per_owner, *refs[:5], *refs[-4:])


def rest(per_owner, q, k, v, g, w, part_k, part_v, key_w, gram):
    size = w.shape[-1]
    core, chip = place()
    rows, cols = triangle(q.shape[0])
    later = cols >= rows
    for which, half in enumerate((core, 1 - core)):
        heads = owned(half, chip, per_owner)
        ats = [columns(head, size) for _, _, head in heads]
        square = [dot_nt(w[head], w[head]).astype(BF16) for _, _, head in heads]
        mixing = [dot_nt(v[:, at], g[:, at]) for at in ats]
        mixing = [jnp.where(later, x, 0.0).astype(BF16) for x in mixing]
        keyed = [dot_nn(k[:, at], x).astype(BF16) for x, at in zip(square, ats)]
        mixed = [dot_nn(x, q[:, at]) for x, at in zip(mixing, ats)]
        scores = [dot_nt(x, q[:, at]) for x, at in zip(keyed, ats)]
        scores = [jnp.where(later, x, 0.0).astype(BF16) for x in scores]
        scored = [dot_nn(x, g[:, at]) for x, at in zip(scores, ats)]
        for n, (apart, i, _) in enumerate(heads):
            gram[which, apart, i] = square[n]
            key_w[which, apart, i] = keyed[n]
            part_k[which, apart, i] = mixed[n]
            part_v[which, apart, i] = scored[n]


def owner_body(per_owner, *refs):
    parts, outs = refs[:GROUPS], refs[GROUPS:]
    size = outs[0].shape[-1]
    _, chip = place()
    turns = []
    for i in range(per_owner):
        ahead = slice(i * size, (i + 1) * size)
        behind = slice((per_owner + i) * size, (per_owner + i + 1) * size)
        early = [part[ahead].astype(F32) for part in parts]
        late = [part[behind].astype(F32) for part in parts]
        cross = None
        for to in range(GROUPS):
            prefix = jnp.zeros_like(early[0])
            suffix = jnp.zeros_like(early[0])
            for apart in range(GROUPS):
                if apart == to:
                    continue
                before = (chip ^ apart) < (chip ^ to)
                prefix += jnp.where(before, early[apart], 0.0)
                suffix += jnp.where(before, 0.0, late[apart])
            prefix = prefix.astype(BF16)
            outs[to][ahead] = prefix
            outs[to][behind] = suffix.astype(BF16)
            product = dot_nt(parts[to][behind], prefix)
            cross = product if cross is None else cross + product
        turns.append(cross)
    for pair in range(per_owner // 2):
        both, diagonal = pack(turns[2 * pair], turns[2 * pair + 1])
        start = 2 * per_owner * size + pair * (size + EXTRA)
        for part in parts:
            both += part[start : start + size].astype(F32)
            diagonal += part[start + size : start + size + EXTRA].astype(F32)
        for out in outs:
            out[start : start + size] = both.astype(BF16)
            out[start + size : start + size + EXTRA] = diagonal.astype(BF16)


def finish(which, per_owner, refs, outs):
    q, k, v, g, w, key_w, gram, part_q, part_k, part_v, near = refs[:11]
    carried = refs[11:]
    query_here, key_here, value_here = outs
    size = gram.shape[-1]
    core, chip = place()
    half = 1 - core if which else core
    heads = owned(half, chip, per_owner)
    ats = [columns(head, size) for _, _, head in heads]
    slots = [columns((chip ^ apart) * per_owner + i, size) for apart, i, _ in heads]
    prefix, suffix = [], []
    for apart, i, _ in heads:
        if which:
            early = late = near[apart, i]
        else:
            early, late = near[apart, 0, i], near[apart, 1, i]
        before = carried[apart][i * size : (i + 1) * size]
        after = carried[apart][(per_owner + i) * size : (per_owner + i + 1) * size]
        prefix.append(before + jnp.where(core == 1, early, jnp.zeros_like(early)))
        suffix.append(after + jnp.where(core == 0, late, jnp.zeros_like(late)))
    raw_q = [dot_nt(g[:, at], x) for x, at in zip(prefix, ats)]
    raw_k = [dot_nt(v[:, at], x) for x, at in zip(suffix, ats)]
    raw_v = [dot_nn(key_w[which, a, i], x) for x, (a, i, _) in zip(suffix, heads)]
    raw_q = [(part_q[a, i] + x).astype(BF16) for x, (a, i, _) in zip(raw_q, heads)]
    raw_k = [(part_k[which, a, i] + x).astype(BF16) for x, (a, i, _) in zip(raw_k, heads)]
    for n, (a, i, _) in enumerate(heads):
        value_here[:, slots[n]] = (part_v[which, a, i] + raw_v[n]).astype(BF16)
    done_q = [dot_nn(x, gram[which, a, i]) for x, (a, i, _) in zip(raw_q, heads)]
    done_k = [dot_nn(x, gram[which, a, i]) for x, (a, i, _) in zip(raw_k, heads)]
    for n, slot in enumerate(slots):
        query_here[:, slot] = done_q[n].astype(BF16)
        key_here[:, slot] = done_k[n].astype(BF16)


def maps(which, per_owner, scale, w, carried, out):
    size = w.shape[-1]
    core, chip = place()
    half = 1 - core if which else core
    rows, cols = triangle(size)
    for apart in range(GROUPS):
        for pair in range(per_owner // 2):
            start = 2 * per_owner * size + pair * (size + EXTRA)
            both = carried[apart][start : start + size].astype(F32)
            diagonal = carried[apart][start + size : start + size + EXTRA][:1].astype(F32)
            turned = both.T
            first = jnp.where(rows >= cols, both, turned)
            second = jnp.where(rows < cols, both, turned)
            second = jnp.where(rows == cols, diagonal, second)
            for i, whole in ((2 * pair, first), (2 * pair + 1, second)):
                slot = (chip ^ apart) * per_owner + i
                head = half * (GROUPS * per_owner) + slot
                out[slot] = dot_nn(whole.astype(BF16), w[head]) * scale


def tail_near_body(per_owner, scale, *refs):
    operands, outs = refs[: 11 + GROUPS], refs[11 + GROUPS :]
    maps(0, per_owner, scale, operands[4], operands[11:], outs[3])
    finish(0, per_owner, operands, outs[:3])


def tail_far_body(per_owner, scale, *refs):
    operands, near = refs[: 11 + GROUPS], refs[11 + GROUPS : 15 + GROUPS]
    outs, here, sems = refs[-9:-5], refs[-5:-1], refs[-1]
    core, _ = place()
    width = here[0].shape[1]
    count = here[3].shape[0]
    copies = []

    def leave(n, half, source):
        to = outs[n].at[pl.ds(half * count, count)] if n == 3 else outs[n].at[:, columns(half, width)]
        copies.append(pltpu.make_async_copy(source, to, sems.at[len(copies)]))
        copies[-1].start()

    for n in range(4):
        leave(n, core, near[n])
    maps(1, per_owner, scale, operands[4], operands[11:], here[3])
    finish(1, per_owner, operands, here[:3])
    for n in range(4):
        leave(n, 1 - core, here[n])
    for copy in copies:
        copy.wait()


def swap(x, apart):
    count = lax.axis_size("ctx")
    return lax.ppermute(x, "ctx", [(i, i ^ apart) for i in range(count)])


def paired(q, k, v, g, w):
    rows, width = q.shape
    heads, size = w.shape[0], w.shape[-1]
    per_owner = heads // (2 * GROUPS)
    length = rows * lax.axis_size("ctx")
    block = (size, size)
    one = (GROUPS, per_owner) + block
    triple = (GROUPS, 3, per_owner) + block
    twice = (2,) + one
    payload = (2 * per_owner * size + (per_owner // 2) * (size + EXTRA), size)
    bind = functools.partial

    *here, send, part_q1 = call(
        bind(load_body, per_owner),
        [((rows, width), BF16)] * 4 + [(triple, BF16), (one, F32)],
        [pltpu.with_memory_space_constraint(x, pltpu.HBM) for x in (q, k, v, g)],
        2.0,
        in_spec=[HBM] * 4,
        scratch=[pltpu.SemaphoreType.DMA((2, 4))],
    )
    other = swap(send, 1)
    own, extra, part_q0, w = call(
        bind(near_body, per_owner),
        [(triple, BF16), (one, BF16), (one, F32), (w.shape, BF16)],
        (*here, pltpu.with_memory_space_constraint(w, pltpu.HBM)),
        1.0,
        in_spec=[VMEM] * 4 + [HBM],
        scratch=[pltpu.SemaphoreType.DMA],
    )
    chip_sums = call(bind(join_body, per_owner), [(payload, BF16)] * GROUPS, (own, other), 0.5)
    locals_ = [(twice, F32), (twice, F32), (twice, BF16), (twice, BF16)]
    local = list(
        call(bind(rest_first_body, per_owner), locals_, (*here, w), 1.8, after=chip_sums[:1])
    )
    held = lax.optimization_barrier((*chip_sums, local[0]))
    chip_sums, local[0] = list(held[:GROUPS]), held[GROUPS]
    parts = [chip_sums[0]] + [swap(chip_sums[j], 2 * j) for j in range(1, GROUPS)]
    extra = swap(extra, 1)
    local = call(
        bind(rest_second_body, per_owner),
        locals_,
        (*here, w),
        1.8,
        after=tuple(local),
        aliases={5 + n: n for n in range(4)},
        in_after=VMEM,
    )
    part_k, part_v, key_w, gram = local
    carried = call(
        bind(owner_body, per_owner), [(payload, BF16)] * GROUPS, parts, 0.5, after=(gram,)
    )
    near = [carried[0]] + [swap(carried[j], 2 * j) for j in range(1, GROUPS)]
    far = [swap(x, 1) for x in near]
    scale = 1.0 / math.sqrt(length)
    outs = [((rows, width), BF16)] * 3 + [((heads,) + block, F32)]
    halves = [((rows, width // 2), BF16)] * 3 + [((heads // 2,) + block, F32)]
    shared = (*here, w, key_w, gram)
    near_half = call(
        bind(tail_near_body, per_owner, scale),
        halves,
        (*shared, part_q0, part_k, part_v, other, *near),
        1.0,
    )
    return tuple(
        call(
            bind(tail_far_body, per_owner, scale),
            outs,
            (*shared, part_q1, part_k, part_v, extra, *far, *near_half),
            2.0,
            scratch=[pltpu.VMEM(shape, dtype) for shape, dtype in halves]
            + [pltpu.SemaphoreType.DMA((8,))],
            out_specs=[HBM] * 4,
        )
    )


def gathered(q, k, v, g, w):
    rows, width = q.shape
    heads, size = w.shape[0], w.shape[-1]
    count = lax.axis_size("ctx")
    me = lax.axis_index("ctx")
    q, k, v, g = (x.reshape(rows, heads, size) for x in (q, k, v, g))

    def mul(spec, a, b):
        return jnp.einsum(spec, a, b, preferred_element_type=F32)

    query_feat = mul("thd,hde->the", q, w).astype(BF16)
    key_feat = mul("thd,hde->the", k, w).astype(BF16)
    key_state = mul("the,thv->hev", key_feat, v).astype(BF16)
    grad_state = mul("the,thv->hev", query_feat, g).astype(BF16)
    index = jnp.arange(count).reshape(count, 1, 1, 1)
    keys = lax.all_gather(key_state, "ctx").astype(F32)
    prefix = jnp.sum(jnp.where(index < me, keys, 0.0), 0).astype(BF16)
    grads = lax.all_gather(grad_state, "ctx").astype(F32)
    suffix = jnp.sum(jnp.where(index > me, grads, 0.0), 0).astype(BF16)
    row, col = triangle(rows)
    causal = row >= col
    scores = jnp.where(causal, mul("the,she->hts", query_feat, key_feat), 0.0).astype(BF16)
    mixing = jnp.where(causal, mul("thv,shv->hts", g, v), 0.0).astype(BF16)
    feat_q = mul("hts,she->the", mixing, key_feat) + mul("thv,hev->the", g, prefix)
    feat_k = mul("hts,the->she", mixing, query_feat) + mul("shv,hev->she", v, suffix)
    feat_q, feat_k = feat_q.astype(BF16), feat_k.astype(BF16)
    value_grad = mul("hts,thv->shv", scores, g) + mul("she,hev->shv", key_feat, suffix)
    query_grad = mul("the,hde->thd", feat_q, w)
    key_grad = mul("the,hde->thd", feat_k, w)
    local = mul("thd,the->hde", q, feat_q) + mul("thd,the->hde", k, feat_k)
    map_grad = lax.psum(local.astype(BF16).astype(F32), "ctx") / math.sqrt(rows * count)
    flat = (rows, width)
    return (
        query_grad.reshape(flat).astype(BF16),
        key_grad.reshape(flat).astype(BF16),
        value_grad.reshape(flat).astype(BF16),
        map_grad,
    )


def per_device(queries, key_rows, values, out_grad, feature_map):
    fits = lax.axis_size("ctx") == 2 * GROUPS and feature_map.shape[0] % (4 * GROUPS) == 0
    plan = paired if fits else gathered
    return plan(queries, key_rows, values, out_grad, feature_map)


def solution(mesh):
    rows = P(("seq", "ctx"), None)
    return jax.shard_map(
        per_device,
        mesh=mesh,
        in_specs=(rows, rows, rows, rows, P()),
        out_specs=(rows, rows, rows, P("seq", None, None)),
        check_vma=False,
    )
```

```python
import functools
import math

import jax
import jax.numpy as jnp
from jax import lax
from jax.experimental import pallas as pl
from jax.experimental.pallas import tpu as pltpu
from jax.sharding import PartitionSpec as P

F32 = jnp.float32
BF16 = jnp.bfloat16
VMEM = pl.BlockSpec(memory_space=pltpu.VMEM)
HBM = pl.BlockSpec(memory_space=pltpu.HBM)
ANY = pl.BlockSpec(memory_space=pl.ANY)
GROUPS = 4
FIRST = 0
EXTRA = 16


def dot_nn(a, b):
    return lax.dot_general(a, b, (((1,), (0,)), ((), ())), preferred_element_type=F32)


def dot_nt(a, b):
    return lax.dot_general(a, b, (((1,), (1,)), ((), ())), preferred_element_type=F32)


def dot_tn(a, b):
    return lax.dot_general(a, b, (((0,), (0,)), ((), ())), preferred_element_type=F32)


def call(
    body, outs, operands, cost, after=(), scratch=(), in_spec=None, out_specs=None, aliases=None, in_after=ANY
):
    count = len(operands)

    def run(*refs):
        return body(*refs[:count], *refs[count + len(after) :])

    return pl.pallas_call(
        run,
        out_shape=[jax.ShapeDtypeStruct(shape, dtype) for shape, dtype in outs],
        in_specs=(in_spec or [VMEM] * count) + [in_after] * len(after),
        out_specs=out_specs or [VMEM] * len(outs),
        scratch_shapes=list(scratch),
        input_output_aliases=aliases or {},
        cost_estimate=pl.CostEstimate(
            flops=int(cost * 1.15e9), bytes_accessed=0, transcendentals=0
        ),
        compiler_params=pltpu.CompilerParams(vmem_limit_bytes=16 * 2**20),
    )(*operands, *after)


def place():
    me = lax.axis_index("ctx")
    return lax.rem(me, 2), lax.div(me, 2)


def owned(half, chip, per_owner):
    base = half * (GROUPS * per_owner)
    return [
        (apart, i, base + (chip ^ apart) * per_owner + i)
        for apart in range(GROUPS)
        for i in range(per_owner)
    ]


def columns(head, size):
    return pl.ds(pl.multiple_of(head * size, size), size)


def triangle(size):
    rows = lax.broadcasted_iota(jnp.int32, (size, size), 0)
    cols = lax.broadcasted_iota(jnp.int32, (size, size), 1)
    return rows, cols


def load_body(per_owner, q, k, v, g, w, q_here, k_here, v_here, g_here, w_here, send, part_q, sems):
    half_width = q.shape[1] // 2
    core, chip = place()
    pairs = ((k, k_here), (v, v_here), (q, q_here), (g, g_here))
    copies = []
    for turn, half in enumerate((1 - core, core)):
        at = columns(half, half_width)
        for n, (source, target) in enumerate(pairs):
            copies.append(
                pltpu.make_async_copy(source.at[:, at], target.at[:, at], sems.at[turn, n])
            )
    copies.append(pltpu.make_async_copy(w, w_here, sems.at[2, 0]))
    for copy in copies:
        copy.start()
    for copy in copies[:4]:
        copy.wait()
    states(send, part_q, owned(1 - core, chip, per_owner), q_here, k_here, v_here, g_here)
    for copy in copies[4:]:
        copy.wait()


def states(out, part_q, heads, q, k, v, g):
    size = out.shape[-1]
    per_owner = len(heads) // GROUPS
    rows, cols = triangle(q.shape[0])
    ats = [columns(head, size) for _, _, head in heads]
    mixing = [dot_nt(g[:, at], v[:, at]) for at in ats]
    early = [dot_tn(k[:, at], v[:, at]) for at in ats]
    mixing = [jnp.where(rows >= cols, x, 0.0).astype(BF16) for x in mixing]
    mixed = [dot_nn(x, k[:, at]) for x, at in zip(mixing, ats)]
    wide = [
        dot_tn(q[:, at], jnp.concatenate([g[:, at], x.astype(BF16)], axis=1))
        for x, at in zip(mixed, ats)
    ]
    for n, (apart, i, _) in enumerate(heads):
        part_q[apart, i] = mixed[n]
        out[apart, i * size : (i + 1) * size] = early[n].astype(BF16)
        out[apart, (per_owner + i) * size : (per_owner + i + 1) * size] = wide[n][:, :size].astype(BF16)
        if i % 2:
            both, diagonal = pack(wide[n - 1][:, size:], wide[n][:, size:])
            start = 2 * per_owner * size + (i // 2) * (size + EXTRA)
            out[apart, start : start + size] = both.astype(BF16)
            out[apart, start + size : start + size + EXTRA] = diagonal.astype(BF16)


def near_body(per_owner, q, k, v, g, own, extra, part_q):
    size = own.shape[-1]
    core, chip = place()
    heads = owned(core, chip, per_owner)
    states(own, part_q, heads, q, k, v, g)
    for apart in range(GROUPS):
        early = own[apart, : per_owner * size]
        late = own[apart, per_owner * size : 2 * per_owner * size]
        extra[apart] = jnp.where(core == 0, early, late)


def pack(first, second):
    size = first.shape[0]
    rows, cols = triangle(size)
    both = jnp.where(rows >= cols, first, second)
    both += jnp.where(rows <= cols, first, second).T
    diagonal = 2.0 * jnp.sum(jnp.where(rows == cols, second, 0.0), axis=0, keepdims=True)
    return both, jnp.broadcast_to(diagonal, (EXTRA, size))


def join_body(per_owner, own, other, *outs):
    size = own.shape[-1]
    count = 2 * per_owner * size
    core, _ = place()
    last = core == 1
    totals = []
    for apart in range(GROUPS):
        for i in range(per_owner):
            ahead = slice(i * size, (i + 1) * size)
            behind = slice((per_owner + i) * size, (per_owner + i + 1) * size)
            early = jnp.where(last, other[apart, ahead], own[apart, ahead])
            late = jnp.where(last, own[apart, behind], other[apart, behind])
            totals.append(dot_nt(late, early))
    for apart in range(GROUPS):
        outs[apart][:count] = own[apart, :count] + other[apart, :count]
        for pair in range(per_owner // 2):
            both, diagonal = pack(*totals[apart * per_owner + 2 * pair :][:2])
            start = count + pair * (size + EXTRA)
            for x in (own, other):
                both += x[apart, start : start + size].astype(F32)
                diagonal += x[apart, start + size : start + size + EXTRA].astype(F32)
            outs[apart][start : start + size] = both.astype(BF16)
            outs[apart][start + size : start + size + EXTRA] = diagonal.astype(BF16)


def rest_first_body(per_owner, *refs):
    core, _ = place()

    @pl.when(core == FIRST)
    def _():
        rest(per_owner, *refs)


def rest_second_body(per_owner, *refs):
    core, _ = place()

    @pl.when(core != FIRST)
    def _():
        rest(per_owner, *refs[:5], *refs[-4:])


def rest(per_owner, q, k, v, g, w, part_k, part_v, key_w, gram):
    size = w.shape[-1]
    core, chip = place()
    rows, cols = triangle(q.shape[0])
    later = cols >= rows
    for which, half in enumerate((core, 1 - core)):
        heads = owned(half, chip, per_owner)
        ats = [columns(head, size) for _, _, head in heads]
        square = [dot_nt(w[head], w[head]).astype(BF16) for _, _, head in heads]
        mixing = [dot_nt(v[:, at], g[:, at]) for at in ats]
        mixing = [jnp.where(later, x, 0.0).astype(BF16) for x in mixing]
        keyed = [dot_nn(k[:, at], x).astype(BF16) for x, at in zip(square, ats)]
        mixed = [dot_nn(x, q[:, at]) for x, at in zip(mixing, ats)]
        scores = [dot_nt(x, q[:, at]) for x, at in zip(keyed, ats)]
        scores = [jnp.where(later, x, 0.0).astype(BF16) for x in scores]
        scored = [dot_nn(x, g[:, at]) for x, at in zip(scores, ats)]
        for n, (apart, i, _) in enumerate(heads):
            gram[which, apart, i] = square[n]
            key_w[which, apart, i] = keyed[n]
            part_k[which, apart, i] = mixed[n]
            part_v[which, apart, i] = scored[n]


def owner_body(per_owner, *refs):
    parts, outs, (placed, carried) = refs[:GROUPS], refs[GROUPS : 2 * GROUPS], refs[2 * GROUPS :]
    size = outs[0].shape[-1]
    states = 2 * per_owner * size
    _, chip = place()
    for apart, part in enumerate(parts):
        placed[chip ^ apart] = part[:states]
    totals = []
    for i in range(per_owner):
        ahead = slice(i * size, (i + 1) * size)
        behind = slice((per_owner + i) * size, (per_owner + i + 1) * size)
        early = [placed[n, ahead] for n in range(GROUPS)]
        late = [placed[n, behind] for n in range(GROUPS)]
        prefix = [jnp.zeros_like(early[0])]
        suffix = [jnp.zeros_like(late[0])]
        before, after = early[0].astype(F32), late[-1].astype(F32)
        for n in range(1, GROUPS):
            prefix.append(before.astype(BF16))
            suffix.insert(0, after.astype(BF16))
            before += early[n].astype(F32)
            after += late[GROUPS - 1 - n].astype(F32)
        cross = dot_nt(late[1], prefix[1])
        for n in range(2, GROUPS):
            cross += dot_nt(late[n], prefix[n])
        totals.append(cross)
        for n in range(GROUPS):
            carried[n, ahead] = prefix[n]
            carried[n, behind] = suffix[n]
    for apart, out in enumerate(outs):
        out[:states] = carried[chip ^ apart]
    for pair in range(per_owner // 2):
        both, diagonal = pack(totals[2 * pair], totals[2 * pair + 1])
        start = states + pair * (size + EXTRA)
        for part in parts:
            both += part[start : start + size].astype(F32)
            diagonal += part[start + size : start + size + EXTRA].astype(F32)
        for out in outs:
            out[start : start + size] = both.astype(BF16)
            out[start + size : start + size + EXTRA] = diagonal.astype(BF16)


def finish(pieces, per_owner, scale, shared, sources, outs):
    g, v, w, key_w, gram, part_q, part_k, part_v, other, extra = shared
    size = gram.shape[-1]
    core, chip = place()
    heads = []
    for piece, (which, apart) in enumerate(pieces):
        half = 1 - core if which else core
        for i in range(per_owner):
            index = piece * per_owner + i
            head = (half * GROUPS + (chip ^ apart)) * per_owner + i
            heads.append((which, apart, i, sources[piece], head, slice(index * size, (index + 1) * size)))
    ats = [columns(head[4], size) for head in heads]
    prefix, suffix = [], []
    for which, apart, i, source, *_ in heads:
        ahead = slice(i * size, (i + 1) * size)
        behind = slice((per_owner + i) * size, (per_owner + i + 1) * size)
        if which:
            early = late = extra[apart, ahead]
        else:
            early, late = other[apart, ahead], other[apart, behind]
        before, after = source[ahead], source[behind]
        prefix.append(before + jnp.where(core == 1, early, jnp.zeros_like(early)))
        suffix.append(after + jnp.where(core == 0, late, jnp.zeros_like(late)))
    raw_q = [dot_nt(g[:, at], x) for x, at in zip(prefix, ats)]
    raw_k = [dot_nt(v[:, at], x) for x, at in zip(suffix, ats)]
    raw_v = [dot_nn(key_w[h, a, i], x) for x, (h, a, i, *_) in zip(suffix, heads)]
    raw_q = [(part_q[h][a, i] + x).astype(BF16) for x, (h, a, i, *_) in zip(raw_q, heads)]
    raw_k = [(part_k[h, a, i] + x).astype(BF16) for x, (h, a, i, *_) in zip(raw_k, heads)]
    for x, (h, a, i, _, _, to) in zip(raw_v, heads):
        outs[2][:, to] = (part_v[h, a, i] + x).astype(BF16)
    done_q = [dot_nn(x, gram[h, a, i]) for x, (h, a, i, *_) in zip(raw_q, heads)]
    done_k = [dot_nn(x, gram[h, a, i]) for x, (h, a, i, *_) in zip(raw_k, heads)]
    for x, y, (*_, to) in zip(done_q, done_k, heads):
        outs[0][:, to] = x.astype(BF16)
        outs[1][:, to] = y.astype(BF16)
    rows, cols = triangle(size)
    for piece, source in enumerate(sources):
        for pair in range(per_owner // 2):
            start = 2 * per_owner * size + pair * (size + EXTRA)
            both = source[start : start + size].astype(F32)
            diagonal = source[start + size : start + size + EXTRA][:1].astype(F32)
            turned = both.T
            first = jnp.where(rows >= cols, both, turned)
            second = jnp.where(rows < cols, both, turned)
            second = jnp.where(rows == cols, diagonal, second)
            for i, whole in ((2 * pair, first), (2 * pair + 1, second)):
                index = piece * per_owner + i
                outs[3][index] = dot_nn(whole.astype(BF16), w[heads[index][4]]) * scale


def leave(pieces, per_owner, here, outs, sems):
    core, chip = place()
    size = here[3].shape[-1]
    copies = []
    for piece, (which, apart) in enumerate(pieces):
        half = 1 - core if which else core
        owner = half * GROUPS + (chip ^ apart)
        at = pl.ds(piece * per_owner * size, per_owner * size)
        ends = [(here[n].at[:, at], outs[n].at[:, columns(owner, per_owner * size)]) for n in range(3)]
        at = pl.ds(piece * per_owner, per_owner)
        ends.append((here[3].at[at], outs[3].at[pl.ds(owner * per_owner, per_owner)]))
        for n, (source, target) in enumerate(ends):
            copies.append(pltpu.make_async_copy(source, target, sems.at[piece, n]))
            copies[-1].start()
    return copies


def tail_body(pieces, ready, per_owner, scale, *refs):
    shared, refs = (*refs[:5], refs[5:7], *refs[7:11]), refs[11:]
    sources, refs = refs[: len(pieces)], refs[len(pieces) :]
    if ready is None:
        finish(pieces, per_owner, scale, shared, sources, refs)
        return
    outs, here, sems, ready_sems = refs[-10:-6], refs[-6:-2], refs[-2], refs[-1]
    copies = leave(ready, per_owner, refs[:4], outs, ready_sems) if ready else []
    finish(pieces, per_owner, scale, shared, sources, here)
    copies += leave(pieces, per_owner, here, outs, sems)
    for copy in copies:
        copy.wait()


def swap(x, apart):
    count = lax.axis_size("ctx")
    return lax.ppermute(x, "ctx", [(i, i ^ apart) for i in range(count)])


def paired(q, k, v, g, w):
    rows, width = q.shape
    heads, size = w.shape[0], w.shape[-1]
    per_owner = heads // (2 * GROUPS)
    length = rows * lax.axis_size("ctx")
    block = (size, size)
    one = (GROUPS, per_owner) + block
    twice = (2,) + one
    payload = (2 * per_owner * size + (per_owner // 2) * (size + EXTRA), size)
    payloads = (GROUPS,) + payload
    bind = functools.partial

    *here, w, send, part_q1 = call(
        bind(load_body, per_owner),
        [((rows, width), BF16)] * 4 + [(w.shape, BF16), (payloads, BF16), (one, F32)],
        [pltpu.with_memory_space_constraint(x, pltpu.HBM) for x in (q, k, v, g, w)],
        2.0,
        in_spec=[HBM] * 5,
        scratch=[pltpu.SemaphoreType.DMA((3, 4))],
    )
    other = swap(send, 1)
    own, extra, part_q0 = call(
        bind(near_body, per_owner),
        [(payloads, BF16), ((GROUPS, per_owner * size, size), BF16), (one, F32)],
        here,
        1.0,
    )
    chip_sums = call(bind(join_body, per_owner), [(payload, BF16)] * GROUPS, (own, other), 0.4)
    locals_ = [(twice, F32), (twice, F32), (twice, BF16), (twice, BF16)]
    local = list(
        call(bind(rest_first_body, per_owner), locals_, (*here, w), 1.8, after=chip_sums[:1])
    )
    held = lax.optimization_barrier((*chip_sums, local[0]))
    chip_sums, local[0] = list(held[:GROUPS]), held[GROUPS]
    parts = [chip_sums[0]] + [swap(chip_sums[j], 2 * j) for j in range(1, GROUPS)]
    extra, local[0] = lax.optimization_barrier((extra, local[0]))
    extra = swap(extra, 1)
    local = call(
        bind(rest_second_body, per_owner),
        locals_,
        (*here, w),
        1.8,
        after=tuple(local),
        aliases={5 + n: n for n in range(4)},
        in_after=VMEM,
    )
    part_k, part_v, key_w, gram = local
    carried = call(
        bind(owner_body, per_owner),
        [(payload, BF16)] * GROUPS,
        parts,
        0.5,
        after=(gram,),
        scratch=[pltpu.VMEM((GROUPS, 2 * per_owner * size, size), BF16)] * 2,
    )
    near = [carried[0]] + [swap(carried[j], 2 * j) for j in range(1, GROUPS)]
    scale = 1.0 / math.sqrt(length)
    outs = [((rows, width), BF16)] * 3 + [((heads,) + block, F32)]
    shared = (here[3], here[2], w, key_w, gram, part_q0, part_q1, part_k, part_v, other)

    def tail(pieces, payloads, ready=(), done=(), before=()):
        count = len(pieces) * per_owner
        room = [((rows, count * size), BF16)] * 3 + [((count,) + block, F32)]
        operands = (*shared, extra, *payloads, *done)
        if ready is None:
            return call(bind(tail_body, pieces, None, per_owner, scale), room, operands, 0.9)
        return call(
            bind(tail_body, pieces, ready, per_owner, scale),
            outs,
            operands,
            1.2,
            after=before,
            scratch=[pltpu.VMEM(shape, dtype) for shape, dtype in room]
            + [pltpu.SemaphoreType.DMA((max(1, len(x)), 4)) for x in (pieces, ready)],
            out_specs=[HBM] * 4,
            aliases={len(operands) + n: n for n in range(len(before))},
        )

    far = [swap(x, 1) for x in near]
    middle = [(0, n) for n in range(GROUPS)] + [(1, n) for n in range(1)]
    done = tail(middle, (*near, *far[:1]), ready=None)
    last = [(1, n) for n in range(1, GROUPS)]
    return tuple(tail(last, far[1:], ready=middle, done=done))


def gathered(q, k, v, g, w):
    rows, width = q.shape
    heads, size = w.shape[0], w.shape[-1]
    count = lax.axis_size("ctx")
    me = lax.axis_index("ctx")
    q, k, v, g = (x.reshape(rows, heads, size) for x in (q, k, v, g))

    def mul(spec, a, b):
        return jnp.einsum(spec, a, b, preferred_element_type=F32)

    query_feat = mul("thd,hde->the", q, w).astype(BF16)
    key_feat = mul("thd,hde->the", k, w).astype(BF16)
    key_state = mul("the,thv->hev", key_feat, v).astype(BF16)
    grad_state = mul("the,thv->hev", query_feat, g).astype(BF16)
    index = jnp.arange(count).reshape(count, 1, 1, 1)
    keys = lax.all_gather(key_state, "ctx").astype(F32)
    prefix = jnp.sum(jnp.where(index < me, keys, 0.0), 0).astype(BF16)
    grads = lax.all_gather(grad_state, "ctx").astype(F32)
    suffix = jnp.sum(jnp.where(index > me, grads, 0.0), 0).astype(BF16)
    row, col = triangle(rows)
    causal = row >= col
    scores = jnp.where(causal, mul("the,she->hts", query_feat, key_feat), 0.0).astype(BF16)
    mixing = jnp.where(causal, mul("thv,shv->hts", g, v), 0.0).astype(BF16)
    feat_q = mul("hts,she->the", mixing, key_feat) + mul("thv,hev->the", g, prefix)
    feat_k = mul("hts,the->she", mixing, query_feat) + mul("shv,hev->she", v, suffix)
    feat_q, feat_k = feat_q.astype(BF16), feat_k.astype(BF16)
    value_grad = mul("hts,thv->shv", scores, g) + mul("she,hev->shv", key_feat, suffix)
    query_grad = mul("the,hde->thd", feat_q, w)
    key_grad = mul("the,hde->thd", feat_k, w)
    local = mul("thd,the->hde", q, feat_q) + mul("thd,the->hde", k, feat_k)
    map_grad = lax.psum(local.astype(BF16).astype(F32), "ctx") / math.sqrt(rows * count)
    flat = (rows, width)
    return (
        query_grad.reshape(flat).astype(BF16),
        key_grad.reshape(flat).astype(BF16),
        value_grad.reshape(flat).astype(BF16),
        map_grad,
    )


def per_device(queries, key_rows, values, out_grad, feature_map):
    fits = lax.axis_size("ctx") == 2 * GROUPS and feature_map.shape[0] % (4 * GROUPS) == 0
    plan = paired if fits else gathered
    return plan(queries, key_rows, values, out_grad, feature_map)


def solution(mesh):
    rows = P(("seq", "ctx"), None)
    return jax.shard_map(
        per_device,
        mesh=mesh,
        in_specs=(rows, rows, rows, rows, P()),
        out_specs=(rows, rows, rows, P("seq", None, None)),
        check_vma=False,
    )
```

```python
import functools
import math

import jax
import jax.numpy as jnp
from jax import lax
from jax.experimental import pallas as pl
from jax.experimental.pallas import tpu as pltpu
from jax.sharding import PartitionSpec as P

F32 = jnp.float32
BF16 = jnp.bfloat16
VMEM = pl.BlockSpec(memory_space=pltpu.VMEM)
HBM = pl.BlockSpec(memory_space=pltpu.HBM)
ANY = pl.BlockSpec(memory_space=pl.ANY)
GROUPS = 4
FIRST = 0
EXTRA = 16


def dot_nn(a, b):
    return lax.dot_general(a, b, (((1,), (0,)), ((), ())), preferred_element_type=F32)


def dot_nt(a, b):
    return lax.dot_general(a, b, (((1,), (1,)), ((), ())), preferred_element_type=F32)


def dot_tn(a, b):
    return lax.dot_general(a, b, (((0,), (0,)), ((), ())), preferred_element_type=F32)


def call(
    body, outs, operands, cost, after=(), scratch=(), in_spec=None, out_specs=None, aliases=None, in_after=ANY
):
    count = len(operands)

    def run(*refs):
        return body(*refs[:count], *refs[count + len(after) :])

    return pl.pallas_call(
        run,
        out_shape=[jax.ShapeDtypeStruct(shape, dtype) for shape, dtype in outs],
        in_specs=(in_spec or [VMEM] * count) + [in_after] * len(after),
        out_specs=out_specs or [VMEM] * len(outs),
        scratch_shapes=list(scratch),
        input_output_aliases=aliases or {},
        cost_estimate=pl.CostEstimate(
            flops=int(cost * 1.15e9), bytes_accessed=0, transcendentals=0
        ),
        compiler_params=pltpu.CompilerParams(vmem_limit_bytes=16 * 2**20),
    )(*operands, *after)


def place():
    me = lax.axis_index("ctx")
    return lax.rem(me, 2), lax.div(me, 2)


def owned(half, chip, per_owner):
    base = half * (GROUPS * per_owner)
    return [
        (apart, i, base + (chip ^ apart) * per_owner + i)
        for apart in range(GROUPS)
        for i in range(per_owner)
    ]


def columns(head, size):
    return pl.ds(pl.multiple_of(head * size, size), size)


def triangle(size):
    rows = lax.broadcasted_iota(jnp.int32, (size, size), 0)
    cols = lax.broadcasted_iota(jnp.int32, (size, size), 1)
    return rows, cols


def load_body(per_owner, q, k, v, g, w, q_here, k_here, v_here, g_here, w_here, send, part_q, sems):
    half_width = q.shape[1] // 2
    core, chip = place()
    pairs = ((g, g_here), (v, v_here), (k, k_here), (q, q_here))
    copies = []
    for turn, half in enumerate((1 - core, core)):
        at = columns(half, half_width)
        for n, (source, target) in enumerate(pairs):
            copies.append(
                pltpu.make_async_copy(source.at[:, at], target.at[:, at], sems.at[turn, n])
            )
    copies.append(pltpu.make_async_copy(w, w_here, sems.at[2, 0]))
    for copy in copies:
        copy.start()
    heads = owned(1 - core, chip, per_owner)
    states(send, part_q, heads, q_here, k_here, v_here, g_here, copies[:4])
    for copy in copies[4:]:
        copy.wait()


def states(out, part_q, heads, q, k, v, g, copies=()):
    size = out.shape[-1]
    per_owner = len(heads) // GROUPS
    rows, cols = triangle(q.shape[0])
    ats = [columns(head, size) for _, _, head in heads]
    for copy in copies[:2]:
        copy.wait()
    mixing = [dot_nt(g[:, at], v[:, at]) for at in ats]
    mixing = [jnp.where(rows >= cols, x, 0.0).astype(BF16) for x in mixing]
    for copy in copies[2:3]:
        copy.wait()
    mixed = [dot_nn(x, k[:, at]) for x, at in zip(mixing, ats)]
    early = [dot_tn(k[:, at], v[:, at]) for at in ats]
    for n, (apart, i, _) in enumerate(heads):
        part_q[apart, i] = mixed[n]
        out[apart, i * size : (i + 1) * size] = early[n].astype(BF16)
    for copy in copies[3:]:
        copy.wait()
    wide = [
        dot_tn(q[:, at], jnp.concatenate([g[:, at], x.astype(BF16)], axis=1))
        for x, at in zip(mixed, ats)
    ]
    for n, (apart, i, _) in enumerate(heads):
        out[apart, (per_owner + i) * size : (per_owner + i + 1) * size] = wide[n][:, :size].astype(BF16)
        if i % 2:
            both, diagonal = pack(wide[n - 1][:, size:], wide[n][:, size:])
            start = 2 * per_owner * size + (i // 2) * (size + EXTRA)
            out[apart, start : start + size] = both.astype(BF16)
            out[apart, start + size : start + size + EXTRA] = diagonal.astype(BF16)


def near_body(per_owner, q, k, v, g, own, *refs):
    size = own.shape[-1]
    core, chip = place()
    heads = owned(core, chip, per_owner)
    states(own, refs[2], heads, q, k, v, g)
    for apart in range(GROUPS):
        early = own[apart, : per_owner * size]
        late = own[apart, per_owner * size : 2 * per_owner * size]
        refs[apart // 2][apart % 2] = jnp.where(core == 0, early, late)


def pack(first, second):
    size = first.shape[0]
    rows, cols = triangle(size)
    both = jnp.where(rows >= cols, first, second)
    both += jnp.where(rows <= cols, first, second).T
    diagonal = 2.0 * jnp.sum(jnp.where(rows == cols, second, 0.0), axis=0, keepdims=True)
    return both, jnp.broadcast_to(diagonal, (EXTRA, size))


def join_body(per_owner, own, other, *outs):
    size = own.shape[-1]
    count = 2 * per_owner * size
    core, _ = place()
    last = core == 1
    totals = []
    for apart in range(GROUPS):
        for i in range(per_owner):
            ahead = slice(i * size, (i + 1) * size)
            behind = slice((per_owner + i) * size, (per_owner + i + 1) * size)
            early = jnp.where(last, other[apart, ahead], own[apart, ahead])
            late = jnp.where(last, own[apart, behind], other[apart, behind])
            totals.append(dot_nt(late, early))
    for apart in range(GROUPS):
        outs[apart][:count] = own[apart, :count] + other[apart, :count]
        for pair in range(per_owner // 2):
            both, diagonal = pack(*totals[apart * per_owner + 2 * pair :][:2])
            start = count + pair * (size + EXTRA)
            for x in (own, other):
                both += x[apart, start : start + size].astype(F32)
                diagonal += x[apart, start + size : start + size + EXTRA].astype(F32)
            outs[apart][start : start + size] = both.astype(BF16)
            outs[apart][start + size : start + size + EXTRA] = diagonal.astype(BF16)


def rest_first_body(per_owner, *refs):
    core, _ = place()

    @pl.when(core == FIRST)
    def _():
        rest(per_owner, *refs)


def rest_second_body(per_owner, *refs):
    core, _ = place()

    @pl.when(core != FIRST)
    def _():
        rest(per_owner, *refs[:5], *refs[-4:])


def rest(per_owner, q, k, v, g, w, part_k, part_v, key_w, gram):
    size = w.shape[-1]
    core, chip = place()
    rows, cols = triangle(q.shape[0])
    later = cols >= rows
    for which, half in enumerate((core, 1 - core)):
        heads = owned(half, chip, per_owner)
        ats = [columns(head, size) for _, _, head in heads]
        square = [dot_nt(w[head], w[head]).astype(BF16) for _, _, head in heads]
        mixing = [dot_nt(v[:, at], g[:, at]) for at in ats]
        mixing = [jnp.where(later, x, 0.0).astype(BF16) for x in mixing]
        keyed = [dot_nn(k[:, at], x).astype(BF16) for x, at in zip(square, ats)]
        mixed = [dot_nn(x, q[:, at]) for x, at in zip(mixing, ats)]
        scores = [dot_nt(x, q[:, at]) for x, at in zip(keyed, ats)]
        scores = [jnp.where(later, x, 0.0).astype(BF16) for x in scores]
        scored = [dot_nn(x, g[:, at]) for x, at in zip(scores, ats)]
        for n, (apart, i, _) in enumerate(heads):
            gram[which, apart, i] = square[n]
            key_w[which, apart, i] = keyed[n]
            part_k[which, apart, i] = mixed[n]
            part_v[which, apart, i] = scored[n]


def owner_body(per_owner, *refs):
    parts, outs, (placed, carried) = refs[:GROUPS], refs[GROUPS : 2 * GROUPS], refs[2 * GROUPS :]
    size = outs[0].shape[-1]
    states = 2 * per_owner * size
    _, chip = place()
    for apart, part in enumerate(parts):
        placed[chip ^ apart] = part[:states]
    totals = []
    for i in range(per_owner):
        ahead = slice(i * size, (i + 1) * size)
        behind = slice((per_owner + i) * size, (per_owner + i + 1) * size)
        early = [placed[n, ahead] for n in range(GROUPS)]
        late = [placed[n, behind] for n in range(GROUPS)]
        prefix = [jnp.zeros_like(early[0])]
        suffix = [jnp.zeros_like(late[0])]
        before, after = early[0].astype(F32), late[-1].astype(F32)
        for n in range(1, GROUPS):
            prefix.append(before.astype(BF16))
            suffix.insert(0, after.astype(BF16))
            before += early[n].astype(F32)
            after += late[GROUPS - 1 - n].astype(F32)
        cross = dot_nt(late[1], prefix[1])
        for n in range(2, GROUPS):
            cross += dot_nt(late[n], prefix[n])
        totals.append(cross)
        for n in range(GROUPS):
            carried[n, ahead] = prefix[n]
            carried[n, behind] = suffix[n]
    for apart, out in enumerate(outs):
        out[:states] = carried[chip ^ apart]
    for pair in range(per_owner // 2):
        both, diagonal = pack(totals[2 * pair], totals[2 * pair + 1])
        start = states + pair * (size + EXTRA)
        for part in parts:
            both += part[start : start + size].astype(F32)
            diagonal += part[start + size : start + size + EXTRA].astype(F32)
        for out in outs:
            out[start : start + size] = both.astype(BF16)
            out[start + size : start + size + EXTRA] = diagonal.astype(BF16)


def finish(pieces, per_owner, scale, shared, sources, near, far):
    g, v, w, key_w, gram, part_q, part_k, part_v, other, extra = shared
    size = gram.shape[-1]
    core, chip = place()
    heads = []
    for piece, (which, apart) in enumerate(pieces):
        half = 1 - core if which else core
        for i in range(per_owner):
            slot = (chip ^ apart) * per_owner + i
            head = half * GROUPS * per_owner + slot
            heads.append((which, apart, i, sources[piece], head, slot))
    ats = [columns(head[4], size) for head in heads]
    prefix, suffix = [], []
    for which, apart, i, source, *_ in heads:
        ahead = slice(i * size, (i + 1) * size)
        behind = slice((per_owner + i) * size, (per_owner + i + 1) * size)
        if which:
            early = late = extra[apart // 2][apart % 2, ahead]
        else:
            early, late = other[apart, ahead], other[apart, behind]
        before, after = source[ahead], source[behind]
        prefix.append(before + jnp.where(core == 1, early, jnp.zeros_like(early)))
        suffix.append(after + jnp.where(core == 0, late, jnp.zeros_like(late)))
    raw_q = [dot_nt(g[:, at], x) for x, at in zip(prefix, ats)]
    raw_k = [dot_nt(v[:, at], x) for x, at in zip(suffix, ats)]
    raw_v = [dot_nn(key_w[h, a, i], x) for x, (h, a, i, *_) in zip(suffix, heads)]
    raw_q = [(part_q[h][a, i] + x).astype(BF16) for x, (h, a, i, *_) in zip(raw_q, heads)]
    raw_k = [(part_k[h, a, i] + x).astype(BF16) for x, (h, a, i, *_) in zip(raw_k, heads)]
    for x, (h, a, i, _, _, to) in zip(raw_v, heads):
        outs = far if h else near
        outs[2][:, columns(to, size)] = (part_v[h, a, i] + x).astype(BF16)
    done_q = [dot_nn(x, gram[h, a, i]) for x, (h, a, i, *_) in zip(raw_q, heads)]
    done_k = [dot_nn(x, gram[h, a, i]) for x, (h, a, i, *_) in zip(raw_k, heads)]
    for x, y, (h, *_, to) in zip(done_q, done_k, heads):
        outs = far if h else near
        outs[0][:, columns(to, size)] = x.astype(BF16)
        outs[1][:, columns(to, size)] = y.astype(BF16)
    rows, cols = triangle(size)
    for piece, source in enumerate(sources):
        for pair in range(per_owner // 2):
            start = 2 * per_owner * size + pair * (size + EXTRA)
            both = source[start : start + size].astype(F32)
            diagonal = source[start + size : start + size + EXTRA][:1].astype(F32)
            turned = both.T
            first = jnp.where(rows >= cols, both, turned)
            second = jnp.where(rows < cols, both, turned)
            second = jnp.where(rows == cols, diagonal, second)
            for i, whole in ((2 * pair, first), (2 * pair + 1, second)):
                which, _, _, _, head, slot = heads[piece * per_owner + i]
                (far if which else near)[3][slot] = dot_nn(whole.astype(BF16), w[head]) * scale


def leave(half, here, outs, sems):
    width, count = here[0].shape[1], here[3].shape[0]
    copies = []
    for n in range(4):
        at = outs[n].at[pl.ds(half * count, count)] if n == 3 else outs[n].at[:, columns(half, width)]
        copies.append(pltpu.make_async_copy(here[n], at, sems.at[n]))
        copies[-1].start()
    return copies


def tail_first_body(pieces, per_owner, scale, *refs):
    shared, refs = (*refs[:5], refs[5:7], *refs[7:10], refs[10:12]), refs[12:]
    sources, refs = refs[: len(pieces)], refs[len(pieces) :]
    finish(pieces, per_owner, scale, shared, sources, refs[:4], refs[4:])


def tail_last_body(pieces, per_owner, scale, *refs):
    shared, refs = (*refs[:5], refs[5:7], *refs[7:10], refs[10:12]), refs[12:]
    sources, refs = refs[: len(pieces)], refs[len(pieces) :]
    near, far, outs, here, sems = refs[:4], refs[4:8], refs[8:12], refs[12:16], refs[16]
    core, chip = place()
    size = here[3].shape[-1]
    copies = leave(core, near, outs, sems.at[0])
    for apart in range(GROUPS - len(pieces)):
        spot = chip ^ apart
        for n in range(3):
            at = columns(spot, per_owner * size)
            here[n][:, at] = far[n][:, at]
        at = pl.ds(spot * per_owner, per_owner)
        here[3][at] = far[3][at]
    finish(pieces, per_owner, scale, shared, sources, None, here)
    copies += leave(1 - core, here, outs, sems.at[1])
    for copy in copies:
        copy.wait()


def swap(x, apart):
    count = lax.axis_size("ctx")
    return lax.ppermute(x, "ctx", [(i, i ^ apart) for i in range(count)])


def paired(q, k, v, g, w):
    rows, width = q.shape
    heads, size = w.shape[0], w.shape[-1]
    per_owner = heads // (2 * GROUPS)
    length = rows * lax.axis_size("ctx")
    block = (size, size)
    one = (GROUPS, per_owner) + block
    twice = (2,) + one
    payload = (2 * per_owner * size + (per_owner // 2) * (size + EXTRA), size)
    payloads = (GROUPS,) + payload
    bind = functools.partial

    *here, w, send, part_q1 = call(
        bind(load_body, per_owner),
        [((rows, width), BF16)] * 4 + [(w.shape, BF16), (payloads, BF16), (one, F32)],
        [pltpu.with_memory_space_constraint(x, pltpu.HBM) for x in (q, k, v, g, w)],
        2.0,
        in_spec=[HBM] * 5,
        scratch=[pltpu.SemaphoreType.DMA((3, 4))],
    )
    other = swap(send, 1)
    own, *extra, part_q0 = call(
        bind(near_body, per_owner),
        [(payloads, BF16), *[((GROUPS // 2, per_owner * size, size), BF16)] * 2, (one, F32)],
        here,
        1.0,
    )
    chip_sums = call(bind(join_body, per_owner), [(payload, BF16)] * GROUPS, (own, other), 0.4)
    locals_ = [(twice, F32), (twice, F32), (twice, BF16), (twice, BF16)]
    local = list(
        call(bind(rest_first_body, per_owner), locals_, (*here, w), 1.8, after=chip_sums[:1])
    )
    held = lax.optimization_barrier((*chip_sums, local[0]))
    chip_sums, local[0] = list(held[:GROUPS]), held[GROUPS]
    parts = [chip_sums[0]] + [swap(chip_sums[j], 2 * j) for j in range(1, GROUPS)]
    local = call(
        bind(rest_second_body, per_owner),
        locals_,
        (*here, w),
        1.8,
        after=tuple(local),
        aliases={5 + n: n for n in range(4)},
        in_after=VMEM,
    )
    part_k, part_v, key_w, gram = local
    *extra, gram = lax.optimization_barrier((*extra, gram))
    extra = [swap(x, 1) for x in extra]
    carried = call(
        bind(owner_body, per_owner),
        [(payload, BF16)] * GROUPS,
        parts,
        0.5,
        after=(gram, *extra),
        scratch=[pltpu.VMEM((GROUPS, 2 * per_owner * size, size), BF16)] * 2,
    )
    near = [carried[0]] + [swap(carried[j], 2 * j) for j in range(1, GROUPS)]
    scale = 1.0 / math.sqrt(length)
    outs = [((rows, width), BF16)] * 3 + [((heads,) + block, F32)]
    shared = (here[3], here[2], w, key_w, gram, part_q0, part_q1, part_k, part_v, other)

    half = [((rows, width // 2), BF16)] * 3 + [((heads // 2,) + block, F32)]
    far = [swap(x, 1) for x in near]
    pieces = [(0, n) for n in range(GROUPS)] + [(1, n) for n in range(2)]
    done = call(
        bind(tail_first_body, pieces, per_owner, scale),
        half * 2,
        (*shared, *extra, *near, *far[:2]),
        1.0,
    )
    pieces = [(1, n) for n in range(2, GROUPS)]
    return tuple(
        call(
            bind(tail_last_body, pieces, per_owner, scale),
            outs,
            (*shared, *extra, *far[2:], *done),
            1.2,
            scratch=[pltpu.VMEM(shape, dtype) for shape, dtype in half]
            + [pltpu.SemaphoreType.DMA((2, 4))],
            out_specs=[HBM] * 4,
        )
    )


def gathered(q, k, v, g, w):
    rows, width = q.shape
    heads, size = w.shape[0], w.shape[-1]
    count = lax.axis_size("ctx")
    me = lax.axis_index("ctx")
    q, k, v, g = (x.reshape(rows, heads, size) for x in (q, k, v, g))

    def mul(spec, a, b):
        return jnp.einsum(spec, a, b, preferred_element_type=F32)

    query_feat = mul("thd,hde->the", q, w).astype(BF16)
    key_feat = mul("thd,hde->the", k, w).astype(BF16)
    key_state = mul("the,thv->hev", key_feat, v).astype(BF16)
    grad_state = mul("the,thv->hev", query_feat, g).astype(BF16)
    index = jnp.arange(count).reshape(count, 1, 1, 1)
    keys = lax.all_gather(key_state, "ctx").astype(F32)
    prefix = jnp.sum(jnp.where(index < me, keys, 0.0), 0).astype(BF16)
    grads = lax.all_gather(grad_state, "ctx").astype(F32)
    suffix = jnp.sum(jnp.where(index > me, grads, 0.0), 0).astype(BF16)
    row, col = triangle(rows)
    causal = row >= col
    scores = jnp.where(causal, mul("the,she->hts", query_feat, key_feat), 0.0).astype(BF16)
    mixing = jnp.where(causal, mul("thv,shv->hts", g, v), 0.0).astype(BF16)
    feat_q = mul("hts,she->the", mixing, key_feat) + mul("thv,hev->the", g, prefix)
    feat_k = mul("hts,the->she", mixing, query_feat) + mul("shv,hev->she", v, suffix)
    feat_q, feat_k = feat_q.astype(BF16), feat_k.astype(BF16)
    value_grad = mul("hts,thv->shv", scores, g) + mul("she,hev->shv", key_feat, suffix)
    query_grad = mul("the,hde->thd", feat_q, w)
    key_grad = mul("the,hde->thd", feat_k, w)
    local = mul("thd,the->hde", q, feat_q) + mul("thd,the->hde", k, feat_k)
    map_grad = lax.psum(local.astype(BF16).astype(F32), "ctx") / math.sqrt(rows * count)
    flat = (rows, width)
    return (
        query_grad.reshape(flat).astype(BF16),
        key_grad.reshape(flat).astype(BF16),
        value_grad.reshape(flat).astype(BF16),
        map_grad,
    )


def per_device(queries, key_rows, values, out_grad, feature_map):
    fits = lax.axis_size("ctx") == 2 * GROUPS and feature_map.shape[0] % (4 * GROUPS) == 0
    plan = paired if fits else gathered
    return plan(queries, key_rows, values, out_grad, feature_map)


def solution(mesh):
    rows = P(("seq", "ctx"), None)
    return jax.shard_map(
        per_device,
        mesh=mesh,
        in_specs=(rows, rows, rows, rows, P()),
        out_specs=(rows, rows, rows, P("seq", None, None)),
        check_vma=False,
    )
```

```python
import functools
import math

import jax
import jax.numpy as jnp
from jax import lax
from jax.experimental import pallas as pl
from jax.experimental.pallas import tpu as pltpu
from jax.sharding import PartitionSpec as P

F32 = jnp.float32
BF16 = jnp.bfloat16
VMEM = pl.BlockSpec(memory_space=pltpu.VMEM)
HBM = pl.BlockSpec(memory_space=pltpu.HBM)
ANY = pl.BlockSpec(memory_space=pl.ANY)
GROUPS = 4
FIRST = 0
EXTRA = 16


def dot_nn(a, b):
    return lax.dot_general(a, b, (((1,), (0,)), ((), ())), preferred_element_type=F32)


def dot_nt(a, b):
    return lax.dot_general(a, b, (((1,), (1,)), ((), ())), preferred_element_type=F32)


def dot_tn(a, b):
    return lax.dot_general(a, b, (((0,), (0,)), ((), ())), preferred_element_type=F32)


def call(
    body, outs, operands, cost, after=(), scratch=(), in_spec=None, out_specs=None, aliases=None, in_after=ANY
):
    count = len(operands)

    def run(*refs):
        return body(*refs[:count], *refs[count + len(after) :])

    return pl.pallas_call(
        run,
        out_shape=[jax.ShapeDtypeStruct(shape, dtype) for shape, dtype in outs],
        in_specs=(in_spec or [VMEM] * count) + [in_after] * len(after),
        out_specs=out_specs or [VMEM] * len(outs),
        scratch_shapes=list(scratch),
        input_output_aliases=aliases or {},
        cost_estimate=pl.CostEstimate(
            flops=int(cost * 1.15e9), bytes_accessed=0, transcendentals=0
        ),
        compiler_params=pltpu.CompilerParams(vmem_limit_bytes=16 * 2**20),
    )(*operands, *after)


def place():
    me = lax.axis_index("ctx")
    return lax.rem(me, 2), lax.div(me, 2)


def owned(half, chip, per_owner):
    base = half * (GROUPS * per_owner)
    return [
        (apart, i, base + (chip ^ apart) * per_owner + i)
        for apart in range(GROUPS)
        for i in range(per_owner)
    ]


def columns(head, size):
    return pl.ds(pl.multiple_of(head * size, size), size)


def triangle(size):
    rows = lax.broadcasted_iota(jnp.int32, (size, size), 0)
    cols = lax.broadcasted_iota(jnp.int32, (size, size), 1)
    return rows, cols


def load_body(per_owner, q, k, v, g, w, q_here, k_here, v_here, g_here, w_here, send, part_q, sems):
    half_width = q.shape[1] // 2
    core, chip = place()
    pairs = ((g, g_here), (v, v_here), (k, k_here), (q, q_here))
    copies = []
    for turn, half in enumerate((1 - core, core)):
        at = columns(half, half_width)
        for n, (source, target) in enumerate(pairs):
            copies.append(
                pltpu.make_async_copy(source.at[:, at], target.at[:, at], sems.at[turn, n])
            )
    copies.append(pltpu.make_async_copy(w, w_here, sems.at[2, 0]))
    for copy in copies:
        copy.start()
    heads = owned(1 - core, chip, per_owner)
    states(send, part_q, heads, q_here, k_here, v_here, g_here, copies[:4])
    for copy in copies[4:]:
        copy.wait()


def states(out, part_q, heads, q, k, v, g, copies=()):
    size = out.shape[-1]
    per_owner = len(heads) // GROUPS
    rows, cols = triangle(q.shape[0])
    ats = [columns(head, size) for _, _, head in heads]
    for copy in copies[:2]:
        copy.wait()
    mixing = [dot_nt(g[:, at], v[:, at]) for at in ats]
    mixing = [jnp.where(rows >= cols, x, 0.0).astype(BF16) for x in mixing]
    for copy in copies[2:3]:
        copy.wait()
    mixed = [dot_nn(x, k[:, at]) for x, at in zip(mixing, ats)]
    early = [dot_tn(k[:, at], v[:, at]) for at in ats]
    for n, (apart, i, _) in enumerate(heads):
        part_q[apart, i] = mixed[n]
        out[apart, i * size : (i + 1) * size] = early[n].astype(BF16)
    for copy in copies[3:]:
        copy.wait()
    wide = [
        dot_tn(q[:, at], jnp.concatenate([g[:, at], x.astype(BF16)], axis=1))
        for x, at in zip(mixed, ats)
    ]
    for n, (apart, i, _) in enumerate(heads):
        out[apart, (per_owner + i) * size : (per_owner + i + 1) * size] = wide[n][:, :size].astype(BF16)
        if i % 2:
            both, diagonal = pack(wide[n - 1][:, size:], wide[n][:, size:])
            start = 2 * per_owner * size + (i // 2) * (size + EXTRA)
            out[apart, start : start + size] = both.astype(BF16)
            out[apart, start + size : start + size + EXTRA] = diagonal.astype(BF16)


def near_body(per_owner, q, k, v, g, own, *refs):
    size = own.shape[-1]
    core, chip = place()
    heads = owned(core, chip, per_owner)
    states(own, refs[2], heads, q, k, v, g)
    for apart in range(GROUPS):
        early = own[apart, : per_owner * size]
        late = own[apart, per_owner * size : 2 * per_owner * size]
        refs[apart // 2][apart % 2] = jnp.where(core == 0, early, late)


def pack(first, second):
    size = first.shape[0]
    rows, cols = triangle(size)
    both = jnp.where(rows >= cols, first, second)
    both += jnp.where(rows <= cols, first, second).T
    diagonal = 2.0 * jnp.sum(jnp.where(rows == cols, second, 0.0), axis=0, keepdims=True)
    return both, jnp.broadcast_to(diagonal, (EXTRA, size))


def join_body(per_owner, own, other, *outs):
    size = own.shape[-1]
    count = 2 * per_owner * size
    core, _ = place()
    last = core == 1
    totals = []
    for apart in range(GROUPS):
        for i in range(per_owner):
            ahead = slice(i * size, (i + 1) * size)
            behind = slice((per_owner + i) * size, (per_owner + i + 1) * size)
            early = jnp.where(last, other[apart, ahead], own[apart, ahead])
            late = jnp.where(last, own[apart, behind], other[apart, behind])
            totals.append(dot_nt(late, early))
    for apart in range(GROUPS):
        outs[apart][:count] = own[apart, :count] + other[apart, :count]
        for pair in range(per_owner // 2):
            both, diagonal = pack(*totals[apart * per_owner + 2 * pair :][:2])
            start = count + pair * (size + EXTRA)
            for x in (own, other):
                both += x[apart, start : start + size].astype(F32)
                diagonal += x[apart, start + size : start + size + EXTRA].astype(F32)
            outs[apart][start : start + size] = both.astype(BF16)
            outs[apart][start + size : start + size + EXTRA] = diagonal.astype(BF16)


def rest_first_body(per_owner, *refs):
    core, _ = place()

    @pl.when(core == FIRST)
    def _():
        rest(per_owner, *refs)


def rest_second_body(per_owner, *refs):
    core, _ = place()

    @pl.when(core != FIRST)
    def _():
        rest(per_owner, *refs[:5], *refs[-4:])


def rest(per_owner, q, k, v, g, w, part_k, part_v, key_w, gram):
    size = w.shape[-1]
    core, chip = place()
    rows, cols = triangle(q.shape[0])
    later = cols >= rows
    for which, half in enumerate((core, 1 - core)):
        heads = owned(half, chip, per_owner)
        ats = [columns(head, size) for _, _, head in heads]
        square = [dot_nt(w[head], w[head]).astype(BF16) for _, _, head in heads]
        mixing = [dot_nt(v[:, at], g[:, at]) for at in ats]
        mixing = [jnp.where(later, x, 0.0).astype(BF16) for x in mixing]
        keyed = [dot_nn(k[:, at], x).astype(BF16) for x, at in zip(square, ats)]
        mixed = [dot_nn(x, q[:, at]) for x, at in zip(mixing, ats)]
        scores = [dot_nt(x, q[:, at]) for x, at in zip(keyed, ats)]
        scores = [jnp.where(later, x, 0.0).astype(BF16) for x in scores]
        scored = [dot_nn(x, g[:, at]) for x, at in zip(scores, ats)]
        for n, (apart, i, _) in enumerate(heads):
            gram[which, apart, i] = square[n]
            key_w[which, apart, i] = keyed[n]
            part_k[which, apart, i] = mixed[n]
            part_v[which, apart, i] = scored[n]


def owner_body(per_owner, *refs):
    parts, outs, (placed, carried) = refs[:GROUPS], refs[GROUPS : 2 * GROUPS], refs[2 * GROUPS :]
    size = outs[0].shape[-1]
    states = 2 * per_owner * size
    _, chip = place()
    for apart, part in enumerate(parts):
        placed[chip ^ apart] = part[:states]
    totals = []
    for i in range(per_owner):
        ahead = slice(i * size, (i + 1) * size)
        behind = slice((per_owner + i) * size, (per_owner + i + 1) * size)
        early = [placed[n, ahead] for n in range(GROUPS)]
        late = [placed[n, behind] for n in range(GROUPS)]
        prefix = [jnp.zeros_like(early[0])]
        suffix = [jnp.zeros_like(late[0])]
        before, after = early[0].astype(F32), late[-1].astype(F32)
        for n in range(1, GROUPS):
            prefix.append(before.astype(BF16))
            suffix.insert(0, after.astype(BF16))
            before += early[n].astype(F32)
            after += late[GROUPS - 1 - n].astype(F32)
        cross = dot_nt(late[1], prefix[1])
        for n in range(2, GROUPS):
            cross += dot_nt(late[n], prefix[n])
        totals.append(cross)
        for n in range(GROUPS):
            carried[n, ahead] = prefix[n]
            carried[n, behind] = suffix[n]
    for apart, out in enumerate(outs):
        out[:states] = carried[chip ^ apart]
    for pair in range(per_owner // 2):
        both, diagonal = pack(totals[2 * pair], totals[2 * pair + 1])
        start = states + pair * (size + EXTRA)
        for part in parts:
            both += part[start : start + size].astype(F32)
            diagonal += part[start + size : start + size + EXTRA].astype(F32)
        for out in outs:
            out[start : start + size] = both.astype(BF16)
            out[start + size : start + size + EXTRA] = diagonal.astype(BF16)


def finish(pieces, per_owner, scale, shared, sources, blocks):
    g, v, w, key_w, gram, part_q, part_k, part_v, other, extra = shared
    size = gram.shape[-1]
    core, chip = place()
    heads = []
    for piece, (which, apart) in enumerate(pieces):
        half = 1 - core if which else core
        for i in range(per_owner):
            owner = chip ^ apart
            head = (half * GROUPS + owner) * per_owner + i
            slot = lax.rem(owner, 2) * per_owner + i
            heads.append((which, apart, i, sources[piece], head, slot))
    ats = [columns(head[4], size) for head in heads]
    prefix, suffix = [], []
    for which, apart, i, source, *_ in heads:
        ahead = slice(i * size, (i + 1) * size)
        behind = slice((per_owner + i) * size, (per_owner + i + 1) * size)
        if which:
            early = late = extra[apart // 2][apart % 2, ahead]
        else:
            early, late = other[apart, ahead], other[apart, behind]
        before, after = source[ahead], source[behind]
        prefix.append(before + jnp.where(core == 1, early, jnp.zeros_like(early)))
        suffix.append(after + jnp.where(core == 0, late, jnp.zeros_like(late)))
    raw_q = [dot_nt(g[:, at], x) for x, at in zip(prefix, ats)]
    raw_k = [dot_nt(v[:, at], x) for x, at in zip(suffix, ats)]
    raw_v = [dot_nn(key_w[h, a, i], x) for x, (h, a, i, *_) in zip(suffix, heads)]
    raw_q = [(part_q[h][a, i] + x).astype(BF16) for x, (h, a, i, *_) in zip(raw_q, heads)]
    raw_k = [(part_k[h, a, i] + x).astype(BF16) for x, (h, a, i, *_) in zip(raw_k, heads)]
    for x, (h, a, i, _, _, to) in zip(raw_v, heads):
        outs = blocks[h]
        outs[2][:, columns(to, size)] = (part_v[h, a, i] + x).astype(BF16)
    done_q = [dot_nn(x, gram[h, a, i]) for x, (h, a, i, *_) in zip(raw_q, heads)]
    done_k = [dot_nn(x, gram[h, a, i]) for x, (h, a, i, *_) in zip(raw_k, heads)]
    for x, y, (h, *_, to) in zip(done_q, done_k, heads):
        outs = blocks[h]
        outs[0][:, columns(to, size)] = x.astype(BF16)
        outs[1][:, columns(to, size)] = y.astype(BF16)
    rows, cols = triangle(size)
    for piece, source in enumerate(sources):
        for pair in range(per_owner // 2):
            start = 2 * per_owner * size + pair * (size + EXTRA)
            both = source[start : start + size].astype(F32)
            diagonal = source[start + size : start + size + EXTRA][:1].astype(F32)
            turned = both.T
            first = jnp.where(rows >= cols, both, turned)
            second = jnp.where(rows < cols, both, turned)
            second = jnp.where(rows == cols, diagonal, second)
            for i, whole in ((2 * pair, first), (2 * pair + 1, second)):
                which, _, _, _, head, slot = heads[piece * per_owner + i]
                blocks[which][3][slot] = dot_nn(whole.astype(BF16), w[head]) * scale


def leave(half, turn, here, outs, sems):
    _, chip = place()
    block = 2 * half + (lax.div(chip, 2) ^ turn)
    width, count = here[0].shape[1], here[3].shape[0]
    copies = []
    for n in range(4):
        at = outs[n].at[pl.ds(block * count, count)] if n == 3 else outs[n].at[:, columns(block, width)]
        copies.append(pltpu.make_async_copy(here[n], at, sems.at[n]))
        copies[-1].start()
    return copies


def opened(refs, count):
    shared = (*refs[:5], refs[5:7], *refs[7:10], refs[10:12])
    return shared, refs[12 : 12 + count], refs[12 + count :]


def tail_first_body(per_owner, scale, *refs):
    shared, sources, refs = opened(refs, 2)
    outs, here, sems = refs[:4], refs[4:8], refs[8]
    core, _ = place()
    finish([(0, 0), (0, 1)], per_owner, scale, shared, sources, [here, None])
    for copy in leave(core, 0, here, outs, sems):
        copy.wait()


def tail_second_body(per_owner, scale, *refs):
    shared, sources, outs = opened(refs, 4)
    finish([(0, 2), (0, 3), (1, 0), (1, 1)], per_owner, scale, shared, sources, [outs[:4], outs[4:]])


def tail_third_body(per_owner, scale, *refs):
    shared, sources, refs = opened(refs, 2)
    near, far, outs, here, sems = refs[:4], refs[4:8], refs[8:12], refs[12:16], refs[16]
    core, _ = place()
    copies = leave(core, 1, near, outs, sems.at[0]) + leave(1 - core, 0, far, outs, sems.at[1])
    finish([(1, 2), (1, 3)], per_owner, scale, shared, sources, [None, here])
    copies += leave(1 - core, 1, here, outs, sems.at[2])
    for copy in copies:
        copy.wait()


def swap(x, apart):
    count = lax.axis_size("ctx")
    return lax.ppermute(x, "ctx", [(i, i ^ apart) for i in range(count)])


def paired(q, k, v, g, w):
    rows, width = q.shape
    heads, size = w.shape[0], w.shape[-1]
    per_owner = heads // (2 * GROUPS)
    length = rows * lax.axis_size("ctx")
    block = (size, size)
    one = (GROUPS, per_owner) + block
    twice = (2,) + one
    payload = (2 * per_owner * size + (per_owner // 2) * (size + EXTRA), size)
    payloads = (GROUPS,) + payload
    bind = functools.partial

    *here, w, send, part_q1 = call(
        bind(load_body, per_owner),
        [((rows, width), BF16)] * 4 + [(w.shape, BF16), (payloads, BF16), (one, F32)],
        [pltpu.with_memory_space_constraint(x, pltpu.HBM) for x in (q, k, v, g, w)],
        2.0,
        in_spec=[HBM] * 5,
        scratch=[pltpu.SemaphoreType.DMA((3, 4))],
    )
    other = swap(send, 1)
    own, *extra, part_q0 = call(
        bind(near_body, per_owner),
        [(payloads, BF16), *[((GROUPS // 2, per_owner * size, size), BF16)] * 2, (one, F32)],
        here,
        1.0,
    )
    chip_sums = call(bind(join_body, per_owner), [(payload, BF16)] * GROUPS, (own, other), 0.4)
    locals_ = [(twice, F32), (twice, F32), (twice, BF16), (twice, BF16)]
    local = list(
        call(bind(rest_first_body, per_owner), locals_, (*here, w), 1.8, after=chip_sums[:1])
    )
    held = lax.optimization_barrier((*chip_sums, local[0]))
    chip_sums, local[0] = list(held[:GROUPS]), held[GROUPS]
    parts = [chip_sums[0]] + [swap(chip_sums[j], 2 * j) for j in range(1, GROUPS)]
    local = call(
        bind(rest_second_body, per_owner),
        locals_,
        (*here, w),
        1.8,
        after=tuple(local),
        aliases={5 + n: n for n in range(4)},
        in_after=VMEM,
    )
    part_k, part_v, key_w, gram = local
    *extra, gram = lax.optimization_barrier((*extra, gram))
    extra = [swap(x, 1) for x in extra]
    carried = call(
        bind(owner_body, per_owner),
        [(payload, BF16)] * GROUPS,
        parts,
        0.5,
        after=(gram, *extra),
        scratch=[pltpu.VMEM((GROUPS, 2 * per_owner * size, size), BF16)] * 2,
    )
    near = [carried[0]] + [swap(carried[j], 2 * j) for j in range(1, GROUPS)]
    scale = 1.0 / math.sqrt(length)
    outs = [((rows, width), BF16)] * 3 + [((heads,) + block, F32)]
    shared = (here[3], here[2], w, key_w, gram, part_q0, part_q1, part_k, part_v, other)

    part = [((rows, width // 4), BF16)] * 3 + [((heads // 4,) + block, F32)]
    room = [pltpu.VMEM(shape, dtype) for shape, dtype in part]
    done = call(
        bind(tail_first_body, per_owner, scale),
        outs,
        (*shared, part_q0, part_q0, *near[:2]),
        1.4,
        scratch=room + [pltpu.SemaphoreType.DMA((4,))],
        out_specs=[HBM] * 4,
    )
    done = list(done)
    near[2], done[0] = lax.optimization_barrier((near[2], done[0]))
    far = [swap(x, 1) for x in near]
    blocks = call(
        bind(tail_second_body, per_owner, scale),
        part * 2,
        (*shared, *extra, *near[2:], *far[:2]),
        1.0,
    )
    operands = (*shared, *extra, *far[2:], *blocks)
    return tuple(
        call(
            bind(tail_third_body, per_owner, scale),
            outs,
            operands,
            1.2,
            after=tuple(done),
            scratch=room + [pltpu.SemaphoreType.DMA((3, 4))],
            out_specs=[HBM] * 4,
            aliases={len(operands) + n: n for n in range(4)},
        )
    )


def gathered(q, k, v, g, w):
    rows, width = q.shape
    heads, size = w.shape[0], w.shape[-1]
    count = lax.axis_size("ctx")
    me = lax.axis_index("ctx")
    q, k, v, g = (x.reshape(rows, heads, size) for x in (q, k, v, g))

    def mul(spec, a, b):
        return jnp.einsum(spec, a, b, preferred_element_type=F32)

    query_feat = mul("thd,hde->the", q, w).astype(BF16)
    key_feat = mul("thd,hde->the", k, w).astype(BF16)
    key_state = mul("the,thv->hev", key_feat, v).astype(BF16)
    grad_state = mul("the,thv->hev", query_feat, g).astype(BF16)
    index = jnp.arange(count).reshape(count, 1, 1, 1)
    keys = lax.all_gather(key_state, "ctx").astype(F32)
    prefix = jnp.sum(jnp.where(index < me, keys, 0.0), 0).astype(BF16)
    grads = lax.all_gather(grad_state, "ctx").astype(F32)
    suffix = jnp.sum(jnp.where(index > me, grads, 0.0), 0).astype(BF16)
    row, col = triangle(rows)
    causal = row >= col
    scores = jnp.where(causal, mul("the,she->hts", query_feat, key_feat), 0.0).astype(BF16)
    mixing = jnp.where(causal, mul("thv,shv->hts", g, v), 0.0).astype(BF16)
    feat_q = mul("hts,she->the", mixing, key_feat) + mul("thv,hev->the", g, prefix)
    feat_k = mul("hts,the->she", mixing, query_feat) + mul("shv,hev->she", v, suffix)
    feat_q, feat_k = feat_q.astype(BF16), feat_k.astype(BF16)
    value_grad = mul("hts,thv->shv", scores, g) + mul("she,hev->shv", key_feat, suffix)
    query_grad = mul("the,hde->thd", feat_q, w)
    key_grad = mul("the,hde->thd", feat_k, w)
    local = mul("thd,the->hde", q, feat_q) + mul("thd,the->hde", k, feat_k)
    map_grad = lax.psum(local.astype(BF16).astype(F32), "ctx") / math.sqrt(rows * count)
    flat = (rows, width)
    return (
        query_grad.reshape(flat).astype(BF16),
        key_grad.reshape(flat).astype(BF16),
        value_grad.reshape(flat).astype(BF16),
        map_grad,
    )


def per_device(queries, key_rows, values, out_grad, feature_map):
    fits = lax.axis_size("ctx") == 2 * GROUPS and feature_map.shape[0] % (4 * GROUPS) == 0
    plan = paired if fits else gathered
    return plan(queries, key_rows, values, out_grad, feature_map)


def solution(mesh):
    rows = P(("seq", "ctx"), None)
    return jax.shard_map(
        per_device,
        mesh=mesh,
        in_specs=(rows, rows, rows, rows, P()),
        out_specs=(rows, rows, rows, P("seq", None, None)),
        check_vma=False,
    )
```

```python
import functools
import math

import jax
import jax.numpy as jnp
from jax import lax
from jax.experimental import pallas as pl
from jax.experimental.pallas import tpu as pltpu
from jax.sharding import PartitionSpec as P

F32 = jnp.float32
BF16 = jnp.bfloat16
VMEM = pl.BlockSpec(memory_space=pltpu.VMEM)
HBM = pl.BlockSpec(memory_space=pltpu.HBM)
ANY = pl.BlockSpec(memory_space=pl.ANY)
GROUPS = 4
FIRST = 0
EXTRA = 16


def dot_nn(a, b):
    return lax.dot_general(a, b, (((1,), (0,)), ((), ())), preferred_element_type=F32)


def dot_nt(a, b):
    return lax.dot_general(a, b, (((1,), (1,)), ((), ())), preferred_element_type=F32)


def dot_tn(a, b):
    return lax.dot_general(a, b, (((0,), (0,)), ((), ())), preferred_element_type=F32)


def call(
    body, outs, operands, cost, after=(), scratch=(), in_spec=None, out_specs=None, aliases=None, in_after=ANY
):
    count = len(operands)

    def run(*refs):
        return body(*refs[:count], *refs[count + len(after) :])

    return pl.pallas_call(
        run,
        out_shape=[jax.ShapeDtypeStruct(shape, dtype) for shape, dtype in outs],
        in_specs=(in_spec or [VMEM] * count) + [in_after] * len(after),
        out_specs=out_specs or [VMEM] * len(outs),
        scratch_shapes=list(scratch),
        input_output_aliases=aliases or {},
        cost_estimate=pl.CostEstimate(
            flops=int(cost * 1.15e9), bytes_accessed=0, transcendentals=0
        ),
        compiler_params=pltpu.CompilerParams(vmem_limit_bytes=16 * 2**20),
    )(*operands, *after)


def place():
    me = lax.axis_index("ctx")
    return lax.rem(me, 2), lax.div(me, 2)


def owned(half, chip, per_owner):
    base = half * (GROUPS * per_owner)
    return [
        (apart, i, base + (chip ^ apart) * per_owner + i)
        for apart in range(GROUPS)
        for i in range(per_owner)
    ]


def pick(refs, apart):
    group, place_ = ((1, 0), (0, 0), (1, 1), (0, 1))[apart]
    return refs[group].at[place_]


def columns(head, size):
    return pl.ds(pl.multiple_of(head * size, size), size)


def triangle(size):
    rows = lax.broadcasted_iota(jnp.int32, (size, size), 0)
    cols = lax.broadcasted_iota(jnp.int32, (size, size), 1)
    return rows, cols


def load_body(per_owner, q, k, v, g, w, q_here, k_here, v_here, g_here, w_here, *refs):
    send, part_q, sems = refs[:2], refs[2], refs[3]
    half_width = q.shape[1] // 2
    core, chip = place()
    pairs = ((g, g_here), (v, v_here), (k, k_here), (q, q_here))
    copies = []
    for turn, half in enumerate((1 - core, core)):
        at = columns(half, half_width)
        for n, (source, target) in enumerate(pairs):
            copies.append(
                pltpu.make_async_copy(source.at[:, at], target.at[:, at], sems.at[turn, n])
            )
    copies.append(pltpu.make_async_copy(w, w_here, sems.at[2, 0]))
    for copy in copies:
        copy.start()
    heads = owned(1 - core, chip, per_owner)
    states(send, part_q, heads, q_here, k_here, v_here, g_here, copies[:4])
    for copy in copies[4:]:
        copy.wait()


def states(out, part_q, heads, q, k, v, g, copies=()):
    size = out[0].shape[-1]
    per_owner = len(heads) // GROUPS
    rows, cols = triangle(q.shape[0])
    ats = [columns(head, size) for _, _, head in heads]
    for copy in copies[:2]:
        copy.wait()
    mixing = [dot_nt(g[:, at], v[:, at]) for at in ats]
    mixing = [jnp.where(rows >= cols, x, 0.0).astype(BF16) for x in mixing]
    for copy in copies[2:3]:
        copy.wait()
    mixed = [dot_nn(x, k[:, at]) for x, at in zip(mixing, ats)]
    early = [dot_tn(k[:, at], v[:, at]) for at in ats]
    for n, (apart, i, _) in enumerate(heads):
        part_q[apart, i] = mixed[n]
        pick(out, apart)[i * size : (i + 1) * size] = early[n].astype(BF16)
    for copy in copies[3:]:
        copy.wait()
    wide = [
        dot_tn(q[:, at], jnp.concatenate([g[:, at], x.astype(BF16)], axis=1))
        for x, at in zip(mixed, ats)
    ]
    for n, (apart, i, _) in enumerate(heads):
        to = pick(out, apart)
        to[(per_owner + i) * size : (per_owner + i + 1) * size] = wide[n][:, :size].astype(BF16)
        if i % 2:
            both, diagonal = pack(wide[n - 1][:, size:], wide[n][:, size:])
            start = 2 * per_owner * size + (i // 2) * (size + EXTRA)
            to[start : start + size] = both.astype(BF16)
            to[start + size : start + size + EXTRA] = diagonal.astype(BF16)


def near_body(per_owner, q, k, v, g, *refs):
    own, extra, part_q = refs[:2], refs[2:4], refs[4]
    size = own[0].shape[-1]
    core, chip = place()
    heads = owned(core, chip, per_owner)
    states(own, part_q, heads, q, k, v, g)
    for apart in range(GROUPS):
        early = pick(own, apart)[: per_owner * size]
        late = pick(own, apart)[per_owner * size : 2 * per_owner * size]
        extra[apart // 2][apart % 2] = jnp.where(core == 0, early, late)


def pack(first, second):
    size = first.shape[0]
    rows, cols = triangle(size)
    both = jnp.where(rows >= cols, first, second)
    both += jnp.where(rows <= cols, first, second).T
    diagonal = 2.0 * jnp.sum(jnp.where(rows == cols, second, 0.0), axis=0, keepdims=True)
    return both, jnp.broadcast_to(diagonal, (EXTRA, size))


def join_body(per_owner, own, other, *outs):
    size = own.shape[-1]
    count = 2 * per_owner * size
    core, _ = place()
    last = core == 1
    totals = []
    for apart in range(len(outs)):
        for i in range(per_owner):
            ahead = slice(i * size, (i + 1) * size)
            behind = slice((per_owner + i) * size, (per_owner + i + 1) * size)
            early = jnp.where(last, other[apart, ahead], own[apart, ahead])
            late = jnp.where(last, own[apart, behind], other[apart, behind])
            totals.append(dot_nt(late, early))
    for apart in range(len(outs)):
        outs[apart][:count] = own[apart, :count] + other[apart, :count]
        for pair in range(per_owner // 2):
            both, diagonal = pack(*totals[apart * per_owner + 2 * pair :][:2])
            start = count + pair * (size + EXTRA)
            for x in (own, other):
                both += x[apart, start : start + size].astype(F32)
                diagonal += x[apart, start + size : start + size + EXTRA].astype(F32)
            outs[apart][start : start + size] = both.astype(BF16)
            outs[apart][start + size : start + size + EXTRA] = diagonal.astype(BF16)


def rest_first_body(per_owner, *refs):
    core, _ = place()

    @pl.when(core == FIRST)
    def _():
        rest(per_owner, *refs)


def rest_second_body(per_owner, *refs):
    core, _ = place()

    @pl.when(core != FIRST)
    def _():
        rest(per_owner, *refs[:5], *refs[-4:])


def rest(per_owner, q, k, v, g, w, part_k, part_v, key_w, gram):
    size = w.shape[-1]
    core, chip = place()
    rows, cols = triangle(q.shape[0])
    later = cols >= rows
    for which, half in enumerate((core, 1 - core)):
        heads = owned(half, chip, per_owner)
        ats = [columns(head, size) for _, _, head in heads]
        square = [dot_nt(w[head], w[head]).astype(BF16) for _, _, head in heads]
        mixing = [dot_nt(v[:, at], g[:, at]) for at in ats]
        mixing = [jnp.where(later, x, 0.0).astype(BF16) for x in mixing]
        keyed = [dot_nn(k[:, at], x).astype(BF16) for x, at in zip(square, ats)]
        mixed = [dot_nn(x, q[:, at]) for x, at in zip(mixing, ats)]
        scores = [dot_nt(x, q[:, at]) for x, at in zip(keyed, ats)]
        scores = [jnp.where(later, x, 0.0).astype(BF16) for x in scores]
        scored = [dot_nn(x, g[:, at]) for x, at in zip(scores, ats)]
        for n, (apart, i, _) in enumerate(heads):
            gram[which, apart, i] = square[n]
            key_w[which, apart, i] = keyed[n]
            part_k[which, apart, i] = mixed[n]
            part_v[which, apart, i] = scored[n]


def owner_body(per_owner, *refs):
    parts, outs, (placed, carried) = refs[:GROUPS], refs[GROUPS : 2 * GROUPS], refs[2 * GROUPS :]
    size = outs[0].shape[-1]
    states = 2 * per_owner * size
    _, chip = place()
    for apart, part in enumerate(parts):
        placed[chip ^ apart] = part[:states]
    totals = []
    for i in range(per_owner):
        ahead = slice(i * size, (i + 1) * size)
        behind = slice((per_owner + i) * size, (per_owner + i + 1) * size)
        early = [placed[n, ahead] for n in range(GROUPS)]
        late = [placed[n, behind] for n in range(GROUPS)]
        prefix = [jnp.zeros_like(early[0])]
        suffix = [jnp.zeros_like(late[0])]
        before, after = early[0].astype(F32), late[-1].astype(F32)
        for n in range(1, GROUPS):
            prefix.append(before.astype(BF16))
            suffix.insert(0, after.astype(BF16))
            before += early[n].astype(F32)
            after += late[GROUPS - 1 - n].astype(F32)
        cross = dot_nt(late[1], prefix[1])
        for n in range(2, GROUPS):
            cross += dot_nt(late[n], prefix[n])
        totals.append(cross)
        for n in range(GROUPS):
            carried[n, ahead] = prefix[n]
            carried[n, behind] = suffix[n]
    for apart, out in enumerate(outs):
        out[:states] = carried[chip ^ apart]
    for pair in range(per_owner // 2):
        both, diagonal = pack(totals[2 * pair], totals[2 * pair + 1])
        start = states + pair * (size + EXTRA)
        for part in parts:
            both += part[start : start + size].astype(F32)
            diagonal += part[start + size : start + size + EXTRA].astype(F32)
        for out in outs:
            out[start : start + size] = both.astype(BF16)
            out[start + size : start + size + EXTRA] = diagonal.astype(BF16)


def finish(pieces, per_owner, scale, shared, sources, blocks):
    g, v, w, key_w, gram, part_q, part_k, part_v, other, extra = shared
    size = gram.shape[-1]
    core, chip = place()
    heads = []
    for piece, (which, apart) in enumerate(pieces):
        half = 1 - core if which else core
        for i in range(per_owner):
            owner = chip ^ apart
            head = (half * GROUPS + owner) * per_owner + i
            slot = lax.rem(owner, 2) * per_owner + i
            heads.append((which, apart, i, sources[piece], head, slot))
    ats = [columns(head[4], size) for head in heads]
    prefix, suffix = [], []
    for which, apart, i, source, *_ in heads:
        ahead = slice(i * size, (i + 1) * size)
        behind = slice((per_owner + i) * size, (per_owner + i + 1) * size)
        if which:
            early = late = extra[apart // 2][apart % 2, ahead]
        else:
            early, late = pick(other, apart)[ahead], pick(other, apart)[behind]
        before, after = source[ahead], source[behind]
        prefix.append(before + jnp.where(core == 1, early, jnp.zeros_like(early)))
        suffix.append(after + jnp.where(core == 0, late, jnp.zeros_like(late)))
    raw_q = [dot_nt(g[:, at], x) for x, at in zip(prefix, ats)]
    raw_k = [dot_nt(v[:, at], x) for x, at in zip(suffix, ats)]
    raw_v = [dot_nn(key_w[h, a, i], x) for x, (h, a, i, *_) in zip(suffix, heads)]
    raw_q = [(part_q[h][a, i] + x).astype(BF16) for x, (h, a, i, *_) in zip(raw_q, heads)]
    raw_k = [(part_k[h, a, i] + x).astype(BF16) for x, (h, a, i, *_) in zip(raw_k, heads)]
    for x, (h, a, i, _, _, to) in zip(raw_v, heads):
        outs = blocks[h]
        outs[2][:, columns(to, size)] = (part_v[h, a, i] + x).astype(BF16)
    done_q = [dot_nn(x, gram[h, a, i]) for x, (h, a, i, *_) in zip(raw_q, heads)]
    done_k = [dot_nn(x, gram[h, a, i]) for x, (h, a, i, *_) in zip(raw_k, heads)]
    for x, y, (h, *_, to) in zip(done_q, done_k, heads):
        outs = blocks[h]
        outs[0][:, columns(to, size)] = x.astype(BF16)
        outs[1][:, columns(to, size)] = y.astype(BF16)
    rows, cols = triangle(size)
    for piece, source in enumerate(sources):
        for pair in range(per_owner // 2):
            start = 2 * per_owner * size + pair * (size + EXTRA)
            both = source[start : start + size].astype(F32)
            diagonal = source[start + size : start + size + EXTRA][:1].astype(F32)
            turned = both.T
            first = jnp.where(rows >= cols, both, turned)
            second = jnp.where(rows < cols, both, turned)
            second = jnp.where(rows == cols, diagonal, second)
            for i, whole in ((2 * pair, first), (2 * pair + 1, second)):
                which, _, _, _, head, slot = heads[piece * per_owner + i]
                blocks[which][3][slot] = dot_nn(whole.astype(BF16), w[head]) * scale


def leave(half, turn, here, outs, sems):
    _, chip = place()
    block = 2 * half + (lax.div(chip, 2) ^ turn)
    width, count = here[0].shape[1], here[3].shape[0]
    copies = []
    for n in range(4):
        at = outs[n].at[pl.ds(block * count, count)] if n == 3 else outs[n].at[:, columns(block, width)]
        copies.append(pltpu.make_async_copy(here[n], at, sems.at[n]))
        copies[-1].start()
    return copies


def opened(refs, count):
    shared = (*refs[:5], refs[5:7], *refs[7:9], refs[9:11], refs[11:13])
    return shared, refs[13 : 13 + count], refs[13 + count :]


def tail_first_body(per_owner, scale, *refs):
    shared, sources, refs = opened(refs, 2)
    outs, here, sems = refs[:4], refs[4:8], refs[8]
    core, _ = place()
    finish([(0, 0), (0, 1)], per_owner, scale, shared, sources, [here, None])
    for copy in leave(core, 0, here, outs, sems):
        copy.wait()


def tail_second_body(per_owner, scale, *refs):
    shared, sources, outs = opened(refs, 4)
    finish([(0, 2), (0, 3), (1, 0), (1, 1)], per_owner, scale, shared, sources, [outs[:4], outs[4:]])


def tail_third_body(per_owner, scale, *refs):
    shared, sources, refs = opened(refs, 2)
    near, far, outs, here, sems = refs[:4], refs[4:8], refs[8:12], refs[12:16], refs[16]
    core, _ = place()
    copies = leave(core, 1, near, outs, sems.at[0]) + leave(1 - core, 0, far, outs, sems.at[1])
    finish([(1, 2), (1, 3)], per_owner, scale, shared, sources, [None, here])
    copies += leave(1 - core, 1, here, outs, sems.at[2])
    for copy in copies:
        copy.wait()


def swap(x, apart):
    count = lax.axis_size("ctx")
    return lax.ppermute(x, "ctx", [(i, i ^ apart) for i in range(count)])


def paired(q, k, v, g, w):
    rows, width = q.shape
    heads, size = w.shape[0], w.shape[-1]
    per_owner = heads // (2 * GROUPS)
    length = rows * lax.axis_size("ctx")
    block = (size, size)
    one = (GROUPS, per_owner) + block
    twice = (2,) + one
    payload = (2 * per_owner * size + (per_owner // 2) * (size + EXTRA), size)
    payloads = (GROUPS // 2,) + payload
    bind = functools.partial

    *here, w, send_near, send_rest, part_q1 = call(
        bind(load_body, per_owner),
        [((rows, width), BF16)] * 4 + [(w.shape, BF16), (payloads, BF16), (payloads, BF16), (one, F32)],
        [pltpu.with_memory_space_constraint(x, pltpu.HBM) for x in (q, k, v, g, w)],
        2.0,
        in_spec=[HBM] * 5,
        scratch=[pltpu.SemaphoreType.DMA((3, 4))],
    )
    other = [swap(x, 1) for x in (send_near, send_rest)]
    *own, extra_a, extra_b, part_q0 = call(
        bind(near_body, per_owner),
        [(payloads, BF16)] * 2
        + [*[((GROUPS // 2, per_owner * size, size), BF16)] * 2, (one, F32)],
        here,
        1.0,
    )
    extra = [extra_a, extra_b]
    join = bind(join_body, per_owner)
    near_sums = call(join, [(payload, BF16)] * 2, (own[0], other[0]), 0.3)
    locals_ = [(twice, F32), (twice, F32), (twice, BF16), (twice, BF16)]
    local = list(
        call(bind(rest_first_body, per_owner), locals_, (*here, w), 1.8, after=near_sums[:1])
    )
    *near_sums, local[0] = lax.optimization_barrier((*near_sums, local[0]))
    rest_sums = call(join, [(payload, BF16)] * 2, (own[1], other[1]), 0.2, after=near_sums[:1])
    chip_sums = [rest_sums[0], near_sums[0], rest_sums[1], near_sums[1]]
    parts = [chip_sums[0]] + [swap(chip_sums[j], 2 * j) for j in range(1, GROUPS)]
    local = call(
        bind(rest_second_body, per_owner),
        locals_,
        (*here, w),
        1.8,
        after=tuple(local),
        aliases={5 + n: n for n in range(4)},
        in_after=VMEM,
    )
    part_k, part_v, key_w, gram = local
    *extra, gram = lax.optimization_barrier((*extra, gram))
    extra = [swap(x, 1) for x in extra]
    carried = call(
        bind(owner_body, per_owner),
        [(payload, BF16)] * GROUPS,
        parts,
        0.5,
        after=(gram, *extra),
        scratch=[pltpu.VMEM((GROUPS, 2 * per_owner * size, size), BF16)] * 2,
    )
    near = [carried[0]] + [swap(carried[j], 2 * j) for j in range(1, GROUPS)]
    scale = 1.0 / math.sqrt(length)
    outs = [((rows, width), BF16)] * 3 + [((heads,) + block, F32)]
    shared = (here[3], here[2], w, key_w, gram, part_q0, part_q1, part_k, part_v, *other)

    part = [((rows, width // 4), BF16)] * 3 + [((heads // 4,) + block, F32)]
    room = [pltpu.VMEM(shape, dtype) for shape, dtype in part]
    done = call(
        bind(tail_first_body, per_owner, scale),
        outs,
        (*shared, part_q0, part_q0, *near[:2]),
        1.4,
        scratch=room + [pltpu.SemaphoreType.DMA((4,))],
        out_specs=[HBM] * 4,
    )
    done = list(done)
    near[2], done[0] = lax.optimization_barrier((near[2], done[0]))
    far = [swap(x, 1) for x in near]
    blocks = call(
        bind(tail_second_body, per_owner, scale),
        part * 2,
        (*shared, *extra, *near[2:], *far[:2]),
        1.0,
    )
    operands = (*shared, *extra, *far[2:], *blocks)
    return tuple(
        call(
            bind(tail_third_body, per_owner, scale),
            outs,
            operands,
            1.2,
            after=tuple(done),
            scratch=room + [pltpu.SemaphoreType.DMA((3, 4))],
            out_specs=[HBM] * 4,
            aliases={len(operands) + n: n for n in range(4)},
        )
    )


def gathered(q, k, v, g, w):
    rows, width = q.shape
    heads, size = w.shape[0], w.shape[-1]
    count = lax.axis_size("ctx")
    me = lax.axis_index("ctx")
    q, k, v, g = (x.reshape(rows, heads, size) for x in (q, k, v, g))

    def mul(spec, a, b):
        return jnp.einsum(spec, a, b, preferred_element_type=F32)

    query_feat = mul("thd,hde->the", q, w).astype(BF16)
    key_feat = mul("thd,hde->the", k, w).astype(BF16)
    key_state = mul("the,thv->hev", key_feat, v).astype(BF16)
    grad_state = mul("the,thv->hev", query_feat, g).astype(BF16)
    index = jnp.arange(count).reshape(count, 1, 1, 1)
    keys = lax.all_gather(key_state, "ctx").astype(F32)
    prefix = jnp.sum(jnp.where(index < me, keys, 0.0), 0).astype(BF16)
    grads = lax.all_gather(grad_state, "ctx").astype(F32)
    suffix = jnp.sum(jnp.where(index > me, grads, 0.0), 0).astype(BF16)
    row, col = triangle(rows)
    causal = row >= col
    scores = jnp.where(causal, mul("the,she->hts", query_feat, key_feat), 0.0).astype(BF16)
    mixing = jnp.where(causal, mul("thv,shv->hts", g, v), 0.0).astype(BF16)
    feat_q = mul("hts,she->the", mixing, key_feat) + mul("thv,hev->the", g, prefix)
    feat_k = mul("hts,the->she", mixing, query_feat) + mul("shv,hev->she", v, suffix)
    feat_q, feat_k = feat_q.astype(BF16), feat_k.astype(BF16)
    value_grad = mul("hts,thv->shv", scores, g) + mul("she,hev->shv", key_feat, suffix)
    query_grad = mul("the,hde->thd", feat_q, w)
    key_grad = mul("the,hde->thd", feat_k, w)
    local = mul("thd,the->hde", q, feat_q) + mul("thd,the->hde", k, feat_k)
    map_grad = lax.psum(local.astype(BF16).astype(F32), "ctx") / math.sqrt(rows * count)
    flat = (rows, width)
    return (
        query_grad.reshape(flat).astype(BF16),
        key_grad.reshape(flat).astype(BF16),
        value_grad.reshape(flat).astype(BF16),
        map_grad,
    )


def per_device(queries, key_rows, values, out_grad, feature_map):
    fits = lax.axis_size("ctx") == 2 * GROUPS and feature_map.shape[0] % (4 * GROUPS) == 0
    plan = paired if fits else gathered
    return plan(queries, key_rows, values, out_grad, feature_map)


def solution(mesh):
    rows = P(("seq", "ctx"), None)
    return jax.shard_map(
        per_device,
        mesh=mesh,
        in_specs=(rows, rows, rows, rows, P()),
        out_specs=(rows, rows, rows, P("seq", None, None)),
        check_vma=False,
    )
```

```python
import functools
import math

import jax
import jax.numpy as jnp
from jax import lax
from jax.experimental import pallas as pl
from jax.experimental.pallas import tpu as pltpu
from jax.sharding import PartitionSpec as P

F32 = jnp.float32
BF16 = jnp.bfloat16
VMEM = pl.BlockSpec(memory_space=pltpu.VMEM)
HBM = pl.BlockSpec(memory_space=pltpu.HBM)
ANY = pl.BlockSpec(memory_space=pl.ANY)
GROUPS = 4
FIRST = 0
EXTRA = 16


def dot_nn(a, b):
    return lax.dot_general(a, b, (((1,), (0,)), ((), ())), preferred_element_type=F32)


def dot_nt(a, b):
    return lax.dot_general(a, b, (((1,), (1,)), ((), ())), preferred_element_type=F32)


def dot_tn(a, b):
    return lax.dot_general(a, b, (((0,), (0,)), ((), ())), preferred_element_type=F32)


def call(
    body, outs, operands, cost, after=(), scratch=(), in_spec=None, out_specs=None, aliases=None, in_after=ANY
):
    count = len(operands)

    def run(*refs):
        return body(*refs[:count], *refs[count + len(after) :])

    return pl.pallas_call(
        run,
        out_shape=[jax.ShapeDtypeStruct(shape, dtype) for shape, dtype in outs],
        in_specs=(in_spec or [VMEM] * count) + [in_after] * len(after),
        out_specs=out_specs or [VMEM] * len(outs),
        scratch_shapes=list(scratch),
        input_output_aliases=aliases or {},
        cost_estimate=pl.CostEstimate(
            flops=int(cost * 1.15e9), bytes_accessed=0, transcendentals=0
        ),
        compiler_params=pltpu.CompilerParams(vmem_limit_bytes=16 * 2**20),
    )(*operands, *after)


def place():
    me = lax.axis_index("ctx")
    return lax.rem(me, 2), lax.div(me, 2)


def owned(half, chip, per_owner):
    base = half * (GROUPS * per_owner)
    return [
        (apart, i, base + (chip ^ apart) * per_owner + i)
        for apart in range(GROUPS)
        for i in range(per_owner)
    ]


def pick(refs, apart):
    group, place_ = ((1, 0), (0, 0), (1, 1), (0, 1))[apart]
    return refs[group].at[place_]


def columns(head, size):
    return pl.ds(pl.multiple_of(head * size, size), size)


def triangle(size):
    rows = lax.broadcasted_iota(jnp.int32, (size, size), 0)
    cols = lax.broadcasted_iota(jnp.int32, (size, size), 1)
    return rows, cols


def load_body(per_owner, q, k, v, g, w, q_here, k_here, v_here, g_here, w_here, *refs):
    send, part_q, sems = refs[:2], refs[2], refs[3]
    half_width = q.shape[1] // 2
    core, chip = place()
    pairs = ((g, g_here), (v, v_here), (k, k_here), (q, q_here))
    copies = []
    for turn, half in enumerate((1 - core, core)):
        at = columns(half, half_width)
        for n, (source, target) in enumerate(pairs):
            copies.append(
                pltpu.make_async_copy(source.at[:, at], target.at[:, at], sems.at[turn, n])
            )
    copies.append(pltpu.make_async_copy(w, w_here, sems.at[2, 0]))
    for copy in copies:
        copy.start()
    heads = owned(1 - core, chip, per_owner)
    states(send, part_q, heads, q_here, k_here, v_here, g_here, copies[:4])
    for copy in copies[4:]:
        copy.wait()


def states(out, part_q, heads, q, k, v, g, copies=()):
    size = out[0].shape[-1]
    per_owner = len(heads) // GROUPS
    rows, cols = triangle(q.shape[0])
    ats = [columns(head, size) for _, _, head in heads]
    for copy in copies[:2]:
        copy.wait()
    mixing = [dot_nt(g[:, at], v[:, at]) for at in ats]
    mixing = [jnp.where(rows >= cols, x, 0.0).astype(BF16) for x in mixing]
    for copy in copies[2:3]:
        copy.wait()
    mixed = [dot_nn(x, k[:, at]) for x, at in zip(mixing, ats)]
    early = [dot_tn(k[:, at], v[:, at]) for at in ats]
    for n, (apart, i, _) in enumerate(heads):
        part_q[apart, i] = mixed[n]
        pick(out, apart)[i * size : (i + 1) * size] = early[n].astype(BF16)
    for copy in copies[3:]:
        copy.wait()
    wide = [
        dot_tn(q[:, at], jnp.concatenate([g[:, at], x.astype(BF16)], axis=1))
        for x, at in zip(mixed, ats)
    ]
    for n, (apart, i, _) in enumerate(heads):
        to = pick(out, apart)
        to[(per_owner + i) * size : (per_owner + i + 1) * size] = wide[n][:, :size].astype(BF16)
        if i % 2:
            both, diagonal = pack(wide[n - 1][:, size:], wide[n][:, size:])
            start = 2 * per_owner * size + (i // 2) * (size + EXTRA)
            to[start : start + size] = both.astype(BF16)
            to[start + size : start + size + EXTRA] = diagonal.astype(BF16)


def near_body(per_owner, q, k, v, g, *refs):
    own, extra, part_q = refs[:2], refs[2:4], refs[4]
    size = own[0].shape[-1]
    core, chip = place()
    heads = owned(core, chip, per_owner)
    states(own, part_q, heads, q, k, v, g)
    for apart in range(GROUPS):
        early = pick(own, apart)[: per_owner * size]
        late = pick(own, apart)[per_owner * size : 2 * per_owner * size]
        extra[apart // 2][apart % 2] = jnp.where(core == 0, early, late)


def pack(first, second):
    size = first.shape[0]
    rows, cols = triangle(size)
    both = jnp.where(rows >= cols, first, second)
    both += jnp.where(rows <= cols, first, second).T
    diagonal = 2.0 * jnp.sum(jnp.where(rows == cols, second, 0.0), axis=0, keepdims=True)
    return both, jnp.broadcast_to(diagonal, (EXTRA, size))


def join_body(places, per_owner, own, other, *outs):
    size = own.shape[-1]
    count = 2 * per_owner * size
    core, _ = place()
    last = core == 1
    totals = []
    for at in places:
        for i in range(per_owner):
            ahead = slice(i * size, (i + 1) * size)
            behind = slice((per_owner + i) * size, (per_owner + i + 1) * size)
            early = jnp.where(last, other[at, ahead], own[at, ahead])
            late = jnp.where(last, own[at, behind], other[at, behind])
            totals.append(dot_nt(late, early))
    for n, at in enumerate(places):
        outs[n][:count] = own[at, :count] + other[at, :count]
        for pair in range(per_owner // 2):
            both, diagonal = pack(*totals[n * per_owner + 2 * pair :][:2])
            start = count + pair * (size + EXTRA)
            for x in (own, other):
                both += x[at, start : start + size].astype(F32)
                diagonal += x[at, start + size : start + size + EXTRA].astype(F32)
            outs[n][start : start + size] = both.astype(BF16)
            outs[n][start + size : start + size + EXTRA] = diagonal.astype(BF16)


def rest_first_body(per_owner, *refs):
    core, _ = place()

    @pl.when(core == FIRST)
    def _():
        rest(per_owner, *refs)


def rest_second_body(per_owner, *refs):
    core, _ = place()

    @pl.when(core != FIRST)
    def _():
        rest(per_owner, *refs[:5], *refs[-4:])


def rest(per_owner, q, k, v, g, w, part_k, part_v, key_w, gram):
    size = w.shape[-1]
    core, chip = place()
    rows, cols = triangle(q.shape[0])
    later = cols >= rows
    for which, half in enumerate((core, 1 - core)):
        heads = owned(half, chip, per_owner)
        ats = [columns(head, size) for _, _, head in heads]
        square = [dot_nt(w[head], w[head]).astype(BF16) for _, _, head in heads]
        mixing = [dot_nt(v[:, at], g[:, at]) for at in ats]
        mixing = [jnp.where(later, x, 0.0).astype(BF16) for x in mixing]
        keyed = [dot_nn(k[:, at], x).astype(BF16) for x, at in zip(square, ats)]
        mixed = [dot_nn(x, q[:, at]) for x, at in zip(mixing, ats)]
        scores = [dot_nt(x, q[:, at]) for x, at in zip(keyed, ats)]
        scores = [jnp.where(later, x, 0.0).astype(BF16) for x in scores]
        scored = [dot_nn(x, g[:, at]) for x, at in zip(scores, ats)]
        for n, (apart, i, _) in enumerate(heads):
            gram[which, apart, i] = square[n]
            key_w[which, apart, i] = keyed[n]
            part_k[which, apart, i] = mixed[n]
            part_v[which, apart, i] = scored[n]


def owner_body(per_owner, *refs):
    parts, outs, (placed, carried) = refs[:GROUPS], refs[GROUPS : 2 * GROUPS], refs[2 * GROUPS :]
    size = outs[0].shape[-1]
    states = 2 * per_owner * size
    _, chip = place()
    for apart, part in enumerate(parts):
        placed[chip ^ apart] = part[:states]
    totals = []
    for i in range(per_owner):
        ahead = slice(i * size, (i + 1) * size)
        behind = slice((per_owner + i) * size, (per_owner + i + 1) * size)
        early = [placed[n, ahead] for n in range(GROUPS)]
        late = [placed[n, behind] for n in range(GROUPS)]
        prefix = [jnp.zeros_like(early[0])]
        suffix = [jnp.zeros_like(late[0])]
        before, after = early[0].astype(F32), late[-1].astype(F32)
        for n in range(1, GROUPS):
            prefix.append(before.astype(BF16))
            suffix.insert(0, after.astype(BF16))
            before += early[n].astype(F32)
            after += late[GROUPS - 1 - n].astype(F32)
        cross = dot_nt(late[1], prefix[1])
        for n in range(2, GROUPS):
            cross += dot_nt(late[n], prefix[n])
        totals.append(cross)
        for n in range(GROUPS):
            carried[n, ahead] = prefix[n]
            carried[n, behind] = suffix[n]
    for apart, out in enumerate(outs):
        out[:states] = carried[chip ^ apart]
    for pair in range(per_owner // 2):
        both, diagonal = pack(totals[2 * pair], totals[2 * pair + 1])
        start = states + pair * (size + EXTRA)
        for part in parts:
            both += part[start : start + size].astype(F32)
            diagonal += part[start + size : start + size + EXTRA].astype(F32)
        for out in outs:
            out[start : start + size] = both.astype(BF16)
            out[start + size : start + size + EXTRA] = diagonal.astype(BF16)


def finish(pieces, per_owner, scale, shared, sources, blocks):
    g, v, w, key_w, gram, part_q, part_k, part_v, other, extra = shared
    size = gram.shape[-1]
    core, chip = place()
    heads = []
    for piece, (which, apart) in enumerate(pieces):
        half = 1 - core if which else core
        for i in range(per_owner):
            owner = chip ^ apart
            head = (half * GROUPS + owner) * per_owner + i
            slot = lax.rem(owner, 2) * per_owner + i
            heads.append((which, apart, i, sources[piece], head, slot))
    ats = [columns(head[4], size) for head in heads]
    prefix, suffix = [], []
    for which, apart, i, source, *_ in heads:
        ahead = slice(i * size, (i + 1) * size)
        behind = slice((per_owner + i) * size, (per_owner + i + 1) * size)
        if which:
            early = late = extra[apart // 2][apart % 2, ahead]
        else:
            early, late = pick(other, apart)[ahead], pick(other, apart)[behind]
        before, after = source[ahead], source[behind]
        prefix.append(before + jnp.where(core == 1, early, jnp.zeros_like(early)))
        suffix.append(after + jnp.where(core == 0, late, jnp.zeros_like(late)))
    raw_q = [dot_nt(g[:, at], x) for x, at in zip(prefix, ats)]
    raw_k = [dot_nt(v[:, at], x) for x, at in zip(suffix, ats)]
    raw_v = [dot_nn(key_w[h, a, i], x) for x, (h, a, i, *_) in zip(suffix, heads)]
    raw_q = [(part_q[h][a, i] + x).astype(BF16) for x, (h, a, i, *_) in zip(raw_q, heads)]
    raw_k = [(part_k[h, a, i] + x).astype(BF16) for x, (h, a, i, *_) in zip(raw_k, heads)]
    for x, (h, a, i, _, _, to) in zip(raw_v, heads):
        outs = blocks[h]
        outs[2][:, columns(to, size)] = (part_v[h, a, i] + x).astype(BF16)
    done_q = [dot_nn(x, gram[h, a, i]) for x, (h, a, i, *_) in zip(raw_q, heads)]
    done_k = [dot_nn(x, gram[h, a, i]) for x, (h, a, i, *_) in zip(raw_k, heads)]
    for x, y, (h, *_, to) in zip(done_q, done_k, heads):
        outs = blocks[h]
        outs[0][:, columns(to, size)] = x.astype(BF16)
        outs[1][:, columns(to, size)] = y.astype(BF16)
    rows, cols = triangle(size)
    for piece, source in enumerate(sources):
        for pair in range(per_owner // 2):
            start = 2 * per_owner * size + pair * (size + EXTRA)
            both = source[start : start + size].astype(F32)
            diagonal = source[start + size : start + size + EXTRA][:1].astype(F32)
            turned = both.T
            first = jnp.where(rows >= cols, both, turned)
            second = jnp.where(rows < cols, both, turned)
            second = jnp.where(rows == cols, diagonal, second)
            for i, whole in ((2 * pair, first), (2 * pair + 1, second)):
                which, _, _, _, head, slot = heads[piece * per_owner + i]
                blocks[which][3][slot] = dot_nn(whole.astype(BF16), w[head]) * scale


def leave(half, turn, here, outs, sems):
    _, chip = place()
    block = 2 * half + (lax.div(chip, 2) ^ turn)
    width, count = here[0].shape[1], here[3].shape[0]
    copies = []
    for n in range(4):
        at = outs[n].at[pl.ds(block * count, count)] if n == 3 else outs[n].at[:, columns(block, width)]
        copies.append(pltpu.make_async_copy(here[n], at, sems.at[n]))
        copies[-1].start()
    return copies


def opened(refs, count):
    shared = (*refs[:5], refs[5:7], *refs[7:9], refs[9:11], refs[11:13])
    return shared, refs[13 : 13 + count], refs[13 + count :]


def tail_first_body(per_owner, scale, *refs):
    shared, sources, refs = opened(refs, 2)
    outs, here, sems = refs[:4], refs[4:8], refs[8]
    core, _ = place()
    finish([(0, 0), (0, 1)], per_owner, scale, shared, sources, [here, None])
    for copy in leave(core, 0, here, outs, sems):
        copy.wait()


def tail_second_body(per_owner, scale, *refs):
    shared, sources, outs = opened(refs, 4)
    finish([(0, 2), (0, 3), (1, 0), (1, 1)], per_owner, scale, shared, sources, [outs[:4], outs[4:]])


def tail_third_body(per_owner, scale, *refs):
    shared, sources, refs = opened(refs, 2)
    near, far, outs, here, sems = refs[:4], refs[4:8], refs[8:12], refs[12:16], refs[16]
    core, _ = place()
    copies = leave(core, 1, near, outs, sems.at[0]) + leave(1 - core, 0, far, outs, sems.at[1])
    finish([(1, 2), (1, 3)], per_owner, scale, shared, sources, [None, here])
    copies += leave(1 - core, 1, here, outs, sems.at[2])
    for copy in copies:
        copy.wait()


def swap(x, apart):
    count = lax.axis_size("ctx")
    return lax.ppermute(x, "ctx", [(i, i ^ apart) for i in range(count)])


def paired(q, k, v, g, w):
    rows, width = q.shape
    heads, size = w.shape[0], w.shape[-1]
    per_owner = heads // (2 * GROUPS)
    length = rows * lax.axis_size("ctx")
    block = (size, size)
    one = (GROUPS, per_owner) + block
    twice = (2,) + one
    payload = (2 * per_owner * size + (per_owner // 2) * (size + EXTRA), size)
    payloads = (GROUPS // 2,) + payload
    bind = functools.partial

    *here, w, send_near, send_rest, part_q1 = call(
        bind(load_body, per_owner),
        [((rows, width), BF16)] * 4 + [(w.shape, BF16), (payloads, BF16), (payloads, BF16), (one, F32)],
        [pltpu.with_memory_space_constraint(x, pltpu.HBM) for x in (q, k, v, g, w)],
        2.0,
        in_spec=[HBM] * 5,
        scratch=[pltpu.SemaphoreType.DMA((3, 4))],
    )
    other = [swap(x, 1) for x in (send_near, send_rest)]
    *own, extra_a, extra_b, part_q0 = call(
        bind(near_body, per_owner),
        [(payloads, BF16)] * 2
        + [*[((GROUPS // 2, per_owner * size, size), BF16)] * 2, (one, F32)],
        here,
        1.0,
    )
    extra = [extra_a, extra_b]

    def join(places, group, cost, after=()):
        body = bind(join_body, places, per_owner)
        return call(body, [(payload, BF16)] * len(places), (own[group], other[group]), cost, after)

    near_sums = join((0,), 0, 0.15)
    locals_ = [(twice, F32), (twice, F32), (twice, BF16), (twice, BF16)]
    local = list(
        call(bind(rest_first_body, per_owner), locals_, (*here, w), 1.8, after=near_sums[:1])
    )
    *near_sums, local[0] = lax.optimization_barrier((*near_sums, local[0]))
    (y_sum,) = join((1,), 1, 0.15, near_sums[:1])
    (far_sum,) = join((1,), 0, 0.15, near_sums[:1])
    chip_sums = [None, near_sums[0], y_sum, far_sum]
    parts = [None] + [swap(chip_sums[j], 2 * j) for j in range(1, GROUPS)]
    local = call(
        bind(rest_second_body, per_owner),
        locals_,
        (*here, w),
        1.8,
        after=tuple(local),
        aliases={5 + n: n for n in range(4)},
        in_after=VMEM,
    )
    part_k, part_v, key_w, gram = local
    (parts[0],) = join((0,), 1, 0.15, (gram,))
    *extra, gram = lax.optimization_barrier((*extra, gram))
    extra = [swap(x, 1) for x in extra]
    carried = call(
        bind(owner_body, per_owner),
        [(payload, BF16)] * GROUPS,
        parts,
        0.5,
        after=(gram, *extra),
        scratch=[pltpu.VMEM((GROUPS, 2 * per_owner * size, size), BF16)] * 2,
    )
    near = [carried[0]] + [swap(carried[j], 2 * j) for j in range(1, GROUPS)]
    scale = 1.0 / math.sqrt(length)
    outs = [((rows, width), BF16)] * 3 + [((heads,) + block, F32)]
    shared = (here[3], here[2], w, key_w, gram, part_q0, part_q1, part_k, part_v, *other)

    part = [((rows, width // 4), BF16)] * 3 + [((heads // 4,) + block, F32)]
    room = [pltpu.VMEM(shape, dtype) for shape, dtype in part]
    done = call(
        bind(tail_first_body, per_owner, scale),
        outs,
        (*shared, part_q0, part_q0, *near[:2]),
        1.4,
        scratch=room + [pltpu.SemaphoreType.DMA((4,))],
        out_specs=[HBM] * 4,
    )
    done = list(done)
    near[2], done[0] = lax.optimization_barrier((near[2], done[0]))
    far = [swap(x, 1) for x in near]
    blocks = call(
        bind(tail_second_body, per_owner, scale),
        part * 2,
        (*shared, *extra, *near[2:], *far[:2]),
        1.0,
    )
    operands = (*shared, *extra, *far[2:], *blocks)
    return tuple(
        call(
            bind(tail_third_body, per_owner, scale),
            outs,
            operands,
            1.2,
            after=tuple(done),
            scratch=room + [pltpu.SemaphoreType.DMA((3, 4))],
            out_specs=[HBM] * 4,
            aliases={len(operands) + n: n for n in range(4)},
        )
    )


def gathered(q, k, v, g, w):
    rows, width = q.shape
    heads, size = w.shape[0], w.shape[-1]
    count = lax.axis_size("ctx")
    me = lax.axis_index("ctx")
    q, k, v, g = (x.reshape(rows, heads, size) for x in (q, k, v, g))

    def mul(spec, a, b):
        return jnp.einsum(spec, a, b, preferred_element_type=F32)

    query_feat = mul("thd,hde->the", q, w).astype(BF16)
    key_feat = mul("thd,hde->the", k, w).astype(BF16)
    key_state = mul("the,thv->hev", key_feat, v).astype(BF16)
    grad_state = mul("the,thv->hev", query_feat, g).astype(BF16)
    index = jnp.arange(count).reshape(count, 1, 1, 1)
    keys = lax.all_gather(key_state, "ctx").astype(F32)
    prefix = jnp.sum(jnp.where(index < me, keys, 0.0), 0).astype(BF16)
    grads = lax.all_gather(grad_state, "ctx").astype(F32)
    suffix = jnp.sum(jnp.where(index > me, grads, 0.0), 0).astype(BF16)
    row, col = triangle(rows)
    causal = row >= col
    scores = jnp.where(causal, mul("the,she->hts", query_feat, key_feat), 0.0).astype(BF16)
    mixing = jnp.where(causal, mul("thv,shv->hts", g, v), 0.0).astype(BF16)
    feat_q = mul("hts,she->the", mixing, key_feat) + mul("thv,hev->the", g, prefix)
    feat_k = mul("hts,the->she", mixing, query_feat) + mul("shv,hev->she", v, suffix)
    feat_q, feat_k = feat_q.astype(BF16), feat_k.astype(BF16)
    value_grad = mul("hts,thv->shv", scores, g) + mul("she,hev->shv", key_feat, suffix)
    query_grad = mul("the,hde->thd", feat_q, w)
    key_grad = mul("the,hde->thd", feat_k, w)
    local = mul("thd,the->hde", q, feat_q) + mul("thd,the->hde", k, feat_k)
    map_grad = lax.psum(local.astype(BF16).astype(F32), "ctx") / math.sqrt(rows * count)
    flat = (rows, width)
    return (
        query_grad.reshape(flat).astype(BF16),
        key_grad.reshape(flat).astype(BF16),
        value_grad.reshape(flat).astype(BF16),
        map_grad,
    )


def per_device(queries, key_rows, values, out_grad, feature_map):
    fits = lax.axis_size("ctx") == 2 * GROUPS and feature_map.shape[0] % (4 * GROUPS) == 0
    plan = paired if fits else gathered
    return plan(queries, key_rows, values, out_grad, feature_map)


def solution(mesh):
    rows = P(("seq", "ctx"), None)
    return jax.shard_map(
        per_device,
        mesh=mesh,
        in_specs=(rows, rows, rows, rows, P()),
        out_specs=(rows, rows, rows, P("seq", None, None)),
        check_vma=False,
    )
```

```python
import functools
import math

import jax
import jax.numpy as jnp
from jax import lax
from jax.experimental import pallas as pl
from jax.experimental.pallas import tpu as pltpu
from jax.sharding import PartitionSpec as P

F32 = jnp.float32
BF16 = jnp.bfloat16
VMEM = pl.BlockSpec(memory_space=pltpu.VMEM)
HBM = pl.BlockSpec(memory_space=pltpu.HBM)
ANY = pl.BlockSpec(memory_space=pl.ANY)
GROUPS = 4
FIRST = 0
EXTRA = 16


def dot_nn(a, b):
    return lax.dot_general(a, b, (((1,), (0,)), ((), ())), preferred_element_type=F32)


def dot_nt(a, b):
    return lax.dot_general(a, b, (((1,), (1,)), ((), ())), preferred_element_type=F32)


def dot_tn(a, b):
    return lax.dot_general(a, b, (((0,), (0,)), ((), ())), preferred_element_type=F32)


def call(
    body, outs, operands, cost, after=(), scratch=(), in_spec=None, out_specs=None, aliases=None, in_after=ANY
):
    count = len(operands)

    def run(*refs):
        return body(*refs[:count], *refs[count + len(after) :])

    return pl.pallas_call(
        run,
        out_shape=[jax.ShapeDtypeStruct(shape, dtype) for shape, dtype in outs],
        in_specs=(in_spec or [VMEM] * count) + [in_after] * len(after),
        out_specs=out_specs or [VMEM] * len(outs),
        scratch_shapes=list(scratch),
        input_output_aliases=aliases or {},
        cost_estimate=pl.CostEstimate(
            flops=int(cost * 1.15e9), bytes_accessed=0, transcendentals=0
        ),
        compiler_params=pltpu.CompilerParams(vmem_limit_bytes=16 * 2**20),
    )(*operands, *after)


def place():
    me = lax.axis_index("ctx")
    return lax.rem(me, 2), lax.div(me, 2)


def owned(half, chip, per_owner):
    base = half * (GROUPS * per_owner)
    return [
        (apart, i, base + (chip ^ apart) * per_owner + i)
        for apart in range(GROUPS)
        for i in range(per_owner)
    ]


def pick(refs, apart):
    group, place_ = ((1, 0), (0, 0), (0, 1), (1, 1))[apart]
    return refs[group].at[place_]


def columns(head, size):
    return pl.ds(pl.multiple_of(head * size, size), size)


def triangle(size):
    rows = lax.broadcasted_iota(jnp.int32, (size, size), 0)
    cols = lax.broadcasted_iota(jnp.int32, (size, size), 1)
    return rows, cols


def load_body(per_owner, q, k, v, g, w, q_here, k_here, v_here, g_here, w_here, *refs):
    send, part_q, sems = refs[:2], refs[2], refs[3]
    half_width = q.shape[1] // 2
    core, chip = place()
    pairs = ((g, g_here), (v, v_here), (k, k_here), (q, q_here))
    copies = []
    for turn, half in enumerate((1 - core, core)):
        at = columns(half, half_width)
        for n, (source, target) in enumerate(pairs):
            copies.append(
                pltpu.make_async_copy(source.at[:, at], target.at[:, at], sems.at[turn, n])
            )
    copies.append(pltpu.make_async_copy(w, w_here, sems.at[2, 0]))
    for copy in copies:
        copy.start()
    heads = owned(1 - core, chip, per_owner)
    states(send, part_q, heads, q_here, k_here, v_here, g_here, copies[:4])
    for copy in copies[4:]:
        copy.wait()


def states(out, part_q, heads, q, k, v, g, copies=()):
    size = out[0].shape[-1]
    per_owner = len(heads) // GROUPS
    rows, cols = triangle(q.shape[0])
    ats = [columns(head, size) for _, _, head in heads]
    for copy in copies[:2]:
        copy.wait()
    mixing = [dot_nt(g[:, at], v[:, at]) for at in ats]
    mixing = [jnp.where(rows >= cols, x, 0.0).astype(BF16) for x in mixing]
    for copy in copies[2:3]:
        copy.wait()
    mixed = [dot_nn(x, k[:, at]) for x, at in zip(mixing, ats)]
    early = [dot_tn(k[:, at], v[:, at]) for at in ats]
    for n, (apart, i, _) in enumerate(heads):
        part_q[apart, i] = mixed[n]
        pick(out, apart)[i * size : (i + 1) * size] = early[n].astype(BF16)
    for copy in copies[3:]:
        copy.wait()
    wide = [
        dot_tn(q[:, at], jnp.concatenate([g[:, at], x.astype(BF16)], axis=1))
        for x, at in zip(mixed, ats)
    ]
    for n, (apart, i, _) in enumerate(heads):
        to = pick(out, apart)
        to[(per_owner + i) * size : (per_owner + i + 1) * size] = wide[n][:, :size].astype(BF16)
        if i % 2:
            both, diagonal = pack(wide[n - 1][:, size:], wide[n][:, size:])
            start = 2 * per_owner * size + (i // 2) * (size + EXTRA)
            to[start : start + size] = both.astype(BF16)
            to[start + size : start + size + EXTRA] = diagonal.astype(BF16)


def near_body(per_owner, q, k, v, g, *refs):
    own, extra, part_q = refs[:2], refs[2:4], refs[4]
    size = own[0].shape[-1]
    core, chip = place()
    heads = owned(core, chip, per_owner)
    states(own, part_q, heads, q, k, v, g)
    for apart in range(GROUPS):
        early = pick(own, apart)[: per_owner * size]
        late = pick(own, apart)[per_owner * size : 2 * per_owner * size]
        extra[apart // 2][apart % 2] = jnp.where(core == 0, early, late)


def pack(first, second):
    size = first.shape[0]
    rows, cols = triangle(size)
    both = jnp.where(rows >= cols, first, second)
    both += jnp.where(rows <= cols, first, second).T
    diagonal = 2.0 * jnp.sum(jnp.where(rows == cols, second, 0.0), axis=0, keepdims=True)
    return both, jnp.broadcast_to(diagonal, (EXTRA, size))


def join_body(places, per_owner, own, other, *outs):
    size = own.shape[-1]
    count = 2 * per_owner * size
    core, _ = place()
    last = core == 1
    totals = []
    for at in places:
        for i in range(per_owner):
            ahead = slice(i * size, (i + 1) * size)
            behind = slice((per_owner + i) * size, (per_owner + i + 1) * size)
            early = jnp.where(last, other[at, ahead], own[at, ahead])
            late = jnp.where(last, own[at, behind], other[at, behind])
            totals.append(dot_nt(late, early))
    for n, at in enumerate(places):
        outs[n][:count] = own[at, :count] + other[at, :count]
        for pair in range(per_owner // 2):
            both, diagonal = pack(*totals[n * per_owner + 2 * pair :][:2])
            start = count + pair * (size + EXTRA)
            for x in (own, other):
                both += x[at, start : start + size].astype(F32)
                diagonal += x[at, start + size : start + size + EXTRA].astype(F32)
            outs[n][start : start + size] = both.astype(BF16)
            outs[n][start + size : start + size + EXTRA] = diagonal.astype(BF16)


def rest_first_body(per_owner, *refs):
    core, _ = place()

    @pl.when(core == FIRST)
    def _():
        rest(per_owner, *refs)


def rest_second_body(per_owner, *refs):
    core, _ = place()

    @pl.when(core != FIRST)
    def _():
        rest(per_owner, *refs[:5], *refs[-4:])


def rest(per_owner, q, k, v, g, w, part_k, part_v, key_w, gram):
    size = w.shape[-1]
    core, chip = place()
    rows, cols = triangle(q.shape[0])
    later = cols >= rows
    for which, half in enumerate((core, 1 - core)):
        heads = owned(half, chip, per_owner)
        ats = [columns(head, size) for _, _, head in heads]
        square = [dot_nt(w[head], w[head]).astype(BF16) for _, _, head in heads]
        mixing = [dot_nt(v[:, at], g[:, at]) for at in ats]
        mixing = [jnp.where(later, x, 0.0).astype(BF16) for x in mixing]
        keyed = [dot_nn(k[:, at], x).astype(BF16) for x, at in zip(square, ats)]
        mixed = [dot_nn(x, q[:, at]) for x, at in zip(mixing, ats)]
        scores = [dot_nt(x, q[:, at]) for x, at in zip(keyed, ats)]
        scores = [jnp.where(later, x, 0.0).astype(BF16) for x in scores]
        scored = [dot_nn(x, g[:, at]) for x, at in zip(scores, ats)]
        for n, (apart, i, _) in enumerate(heads):
            gram[which, apart, i] = square[n]
            key_w[which, apart, i] = keyed[n]
            part_k[which, apart, i] = mixed[n]
            part_v[which, apart, i] = scored[n]


def owner_body(per_owner, *refs):
    parts, outs, (placed, carried) = refs[:GROUPS], refs[GROUPS : 2 * GROUPS], refs[2 * GROUPS :]
    size = outs[0].shape[-1]
    states = 2 * per_owner * size
    _, chip = place()
    for apart, part in enumerate(parts):
        placed[chip ^ apart] = part[:states]
    totals = []
    for i in range(per_owner):
        ahead = slice(i * size, (i + 1) * size)
        behind = slice((per_owner + i) * size, (per_owner + i + 1) * size)
        early = [placed[n, ahead] for n in range(GROUPS)]
        late = [placed[n, behind] for n in range(GROUPS)]
        prefix = [jnp.zeros_like(early[0])]
        suffix = [jnp.zeros_like(late[0])]
        before, after = early[0].astype(F32), late[-1].astype(F32)
        for n in range(1, GROUPS):
            prefix.append(before.astype(BF16))
            suffix.insert(0, after.astype(BF16))
            before += early[n].astype(F32)
            after += late[GROUPS - 1 - n].astype(F32)
        cross = dot_nt(late[1], prefix[1])
        for n in range(2, GROUPS):
            cross += dot_nt(late[n], prefix[n])
        totals.append(cross)
        for n in range(GROUPS):
            carried[n, ahead] = prefix[n]
            carried[n, behind] = suffix[n]
    for apart, out in enumerate(outs):
        out[:states] = carried[chip ^ apart]
    for pair in range(per_owner // 2):
        both, diagonal = pack(totals[2 * pair], totals[2 * pair + 1])
        start = states + pair * (size + EXTRA)
        for part in parts:
            both += part[start : start + size].astype(F32)
            diagonal += part[start + size : start + size + EXTRA].astype(F32)
        for out in outs:
            out[start : start + size] = both.astype(BF16)
            out[start + size : start + size + EXTRA] = diagonal.astype(BF16)


def finish(pieces, per_owner, scale, shared, sources, blocks):
    g, v, w, key_w, gram, part_q, part_k, part_v, other, extra = shared
    size = gram.shape[-1]
    core, chip = place()
    heads = []
    for piece, (which, apart) in enumerate(pieces):
        half = 1 - core if which else core
        for i in range(per_owner):
            owner = chip ^ apart
            head = (half * GROUPS + owner) * per_owner + i
            slot = lax.rem(owner, 2) * per_owner + i
            heads.append((which, apart, i, sources[piece], head, slot))
    ats = [columns(head[4], size) for head in heads]
    prefix, suffix = [], []
    for which, apart, i, source, *_ in heads:
        ahead = slice(i * size, (i + 1) * size)
        behind = slice((per_owner + i) * size, (per_owner + i + 1) * size)
        if which:
            early = late = extra[apart // 2][apart % 2, ahead]
        else:
            early, late = pick(other, apart)[ahead], pick(other, apart)[behind]
        before, after = source[ahead], source[behind]
        prefix.append(before + jnp.where(core == 1, early, jnp.zeros_like(early)))
        suffix.append(after + jnp.where(core == 0, late, jnp.zeros_like(late)))
    raw_q = [dot_nt(g[:, at], x) for x, at in zip(prefix, ats)]
    raw_k = [dot_nt(v[:, at], x) for x, at in zip(suffix, ats)]
    raw_v = [dot_nn(key_w[h, a, i], x) for x, (h, a, i, *_) in zip(suffix, heads)]
    raw_q = [(part_q[h][a, i] + x).astype(BF16) for x, (h, a, i, *_) in zip(raw_q, heads)]
    raw_k = [(part_k[h, a, i] + x).astype(BF16) for x, (h, a, i, *_) in zip(raw_k, heads)]
    for x, (h, a, i, _, _, to) in zip(raw_v, heads):
        outs = blocks[h]
        outs[2][:, columns(to, size)] = (part_v[h, a, i] + x).astype(BF16)
    done_q = [dot_nn(x, gram[h, a, i]) for x, (h, a, i, *_) in zip(raw_q, heads)]
    done_k = [dot_nn(x, gram[h, a, i]) for x, (h, a, i, *_) in zip(raw_k, heads)]
    for x, y, (h, *_, to) in zip(done_q, done_k, heads):
        outs = blocks[h]
        outs[0][:, columns(to, size)] = x.astype(BF16)
        outs[1][:, columns(to, size)] = y.astype(BF16)
    rows, cols = triangle(size)
    for piece, source in enumerate(sources):
        for pair in range(per_owner // 2):
            start = 2 * per_owner * size + pair * (size + EXTRA)
            both = source[start : start + size].astype(F32)
            diagonal = source[start + size : start + size + EXTRA][:1].astype(F32)
            turned = both.T
            first = jnp.where(rows >= cols, both, turned)
            second = jnp.where(rows < cols, both, turned)
            second = jnp.where(rows == cols, diagonal, second)
            for i, whole in ((2 * pair, first), (2 * pair + 1, second)):
                which, _, _, _, head, slot = heads[piece * per_owner + i]
                blocks[which][3][slot] = dot_nn(whole.astype(BF16), w[head]) * scale


def leave(half, turn, here, outs, sems):
    _, chip = place()
    block = 2 * half + (lax.div(chip, 2) ^ turn)
    width, count = here[0].shape[1], here[3].shape[0]
    copies = []
    for n in range(4):
        at = outs[n].at[pl.ds(block * count, count)] if n == 3 else outs[n].at[:, columns(block, width)]
        copies.append(pltpu.make_async_copy(here[n], at, sems.at[n]))
        copies[-1].start()
    return copies


def opened(refs, count):
    shared = (*refs[:5], refs[5:7], *refs[7:9], refs[9:11], refs[11:13])
    return shared, refs[13 : 13 + count], refs[13 + count :]


def tail_first_body(per_owner, scale, *refs):
    shared, sources, refs = opened(refs, 2)
    outs, here, sems = refs[:4], refs[4:8], refs[8]
    core, _ = place()
    finish([(0, 0), (0, 1)], per_owner, scale, shared, sources, [here, None])
    for copy in leave(core, 0, here, outs, sems):
        copy.wait()


def tail_second_body(per_owner, scale, *refs):
    shared, sources, outs = opened(refs, 4)
    finish([(0, 2), (0, 3), (1, 0), (1, 1)], per_owner, scale, shared, sources, [outs[:4], outs[4:]])


def tail_third_body(per_owner, scale, *refs):
    shared, sources, refs = opened(refs, 2)
    near, far, outs, here, sems = refs[:4], refs[4:8], refs[8:12], refs[12:16], refs[16]
    core, _ = place()
    copies = leave(core, 1, near, outs, sems.at[0]) + leave(1 - core, 0, far, outs, sems.at[1])
    finish([(1, 2), (1, 3)], per_owner, scale, shared, sources, [None, here])
    copies += leave(1 - core, 1, here, outs, sems.at[2])
    for copy in copies:
        copy.wait()


def swap(x, apart):
    count = lax.axis_size("ctx")
    return lax.ppermute(x, "ctx", [(i, i ^ apart) for i in range(count)])


def paired(q, k, v, g, w):
    rows, width = q.shape
    heads, size = w.shape[0], w.shape[-1]
    per_owner = heads // (2 * GROUPS)
    length = rows * lax.axis_size("ctx")
    block = (size, size)
    one = (GROUPS, per_owner) + block
    twice = (2,) + one
    payload = (2 * per_owner * size + (per_owner // 2) * (size + EXTRA), size)
    payloads = (GROUPS // 2,) + payload
    bind = functools.partial

    *here, w, send_near, send_rest, part_q1 = call(
        bind(load_body, per_owner),
        [((rows, width), BF16)] * 4 + [(w.shape, BF16), (payloads, BF16), (payloads, BF16), (one, F32)],
        [pltpu.with_memory_space_constraint(x, pltpu.HBM) for x in (q, k, v, g, w)],
        2.0,
        in_spec=[HBM] * 5,
        scratch=[pltpu.SemaphoreType.DMA((3, 4))],
    )
    other = [swap(x, 1) for x in (send_near, send_rest)]
    *own, extra_a, extra_b, part_q0 = call(
        bind(near_body, per_owner),
        [(payloads, BF16)] * 2
        + [*[((GROUPS // 2, per_owner * size, size), BF16)] * 2, (one, F32)],
        here,
        1.0,
    )
    extra = [extra_a, extra_b]

    def join(places, group, cost, after=()):
        body = bind(join_body, places, per_owner)
        return call(body, [(payload, BF16)] * len(places), (own[group], other[group]), cost, after)

    near_sums = join((0,), 0, 0.15)
    locals_ = [(twice, F32), (twice, F32), (twice, BF16), (twice, BF16)]
    local = list(
        call(bind(rest_first_body, per_owner), locals_, (*here, w), 1.8, after=near_sums[:1])
    )
    *near_sums, local[0] = lax.optimization_barrier((*near_sums, local[0]))
    (y_sum,) = join((1,), 0, 0.15, near_sums[:1])
    (far_sum,) = join((1,), 1, 0.15, (y_sum,))
    chip_sums = [None, near_sums[0], y_sum, far_sum]
    parts = [None] + [swap(chip_sums[j], 2 * j) for j in range(1, GROUPS)]
    local = call(
        bind(rest_second_body, per_owner),
        locals_,
        (*here, w),
        1.8,
        after=tuple(local),
        aliases={5 + n: n for n in range(4)},
        in_after=VMEM,
    )
    part_k, part_v, key_w, gram = local
    (parts[0],) = join((0,), 1, 0.15, (gram,))
    *extra, gram = lax.optimization_barrier((*extra, gram))
    extra = [swap(x, 1) for x in extra]
    carried = call(
        bind(owner_body, per_owner),
        [(payload, BF16)] * GROUPS,
        parts,
        0.5,
        after=(gram, *extra),
        scratch=[pltpu.VMEM((GROUPS, 2 * per_owner * size, size), BF16)] * 2,
    )
    near = [carried[0]] + [swap(carried[j], 2 * j) for j in range(1, GROUPS)]
    scale = 1.0 / math.sqrt(length)
    outs = [((rows, width), BF16)] * 3 + [((heads,) + block, F32)]
    shared = (here[3], here[2], w, key_w, gram, part_q0, part_q1, part_k, part_v, *other)

    part = [((rows, width // 4), BF16)] * 3 + [((heads // 4,) + block, F32)]
    room = [pltpu.VMEM(shape, dtype) for shape, dtype in part]
    done = call(
        bind(tail_first_body, per_owner, scale),
        outs,
        (*shared, part_q0, part_q0, *near[:2]),
        1.4,
        scratch=room + [pltpu.SemaphoreType.DMA((4,))],
        out_specs=[HBM] * 4,
    )
    done = list(done)
    near[2], done[0] = lax.optimization_barrier((near[2], done[0]))
    far = [swap(x, 1) for x in near]
    blocks = call(
        bind(tail_second_body, per_owner, scale),
        part * 2,
        (*shared, *extra, *near[2:], *far[:2]),
        1.0,
    )
    operands = (*shared, *extra, *far[2:], *blocks)
    return tuple(
        call(
            bind(tail_third_body, per_owner, scale),
            outs,
            operands,
            1.2,
            after=tuple(done),
            scratch=room + [pltpu.SemaphoreType.DMA((3, 4))],
            out_specs=[HBM] * 4,
            aliases={len(operands) + n: n for n in range(4)},
        )
    )


def gathered(q, k, v, g, w):
    rows, width = q.shape
    heads, size = w.shape[0], w.shape[-1]
    count = lax.axis_size("ctx")
    me = lax.axis_index("ctx")
    q, k, v, g = (x.reshape(rows, heads, size) for x in (q, k, v, g))

    def mul(spec, a, b):
        return jnp.einsum(spec, a, b, preferred_element_type=F32)

    query_feat = mul("thd,hde->the", q, w).astype(BF16)
    key_feat = mul("thd,hde->the", k, w).astype(BF16)
    key_state = mul("the,thv->hev", key_feat, v).astype(BF16)
    grad_state = mul("the,thv->hev", query_feat, g).astype(BF16)
    index = jnp.arange(count).reshape(count, 1, 1, 1)
    keys = lax.all_gather(key_state, "ctx").astype(F32)
    prefix = jnp.sum(jnp.where(index < me, keys, 0.0), 0).astype(BF16)
    grads = lax.all_gather(grad_state, "ctx").astype(F32)
    suffix = jnp.sum(jnp.where(index > me, grads, 0.0), 0).astype(BF16)
    row, col = triangle(rows)
    causal = row >= col
    scores = jnp.where(causal, mul("the,she->hts", query_feat, key_feat), 0.0).astype(BF16)
    mixing = jnp.where(causal, mul("thv,shv->hts", g, v), 0.0).astype(BF16)
    feat_q = mul("hts,she->the", mixing, key_feat) + mul("thv,hev->the", g, prefix)
    feat_k = mul("hts,the->she", mixing, query_feat) + mul("shv,hev->she", v, suffix)
    feat_q, feat_k = feat_q.astype(BF16), feat_k.astype(BF16)
    value_grad = mul("hts,thv->shv", scores, g) + mul("she,hev->shv", key_feat, suffix)
    query_grad = mul("the,hde->thd", feat_q, w)
    key_grad = mul("the,hde->thd", feat_k, w)
    local = mul("thd,the->hde", q, feat_q) + mul("thd,the->hde", k, feat_k)
    map_grad = lax.psum(local.astype(BF16).astype(F32), "ctx") / math.sqrt(rows * count)
    flat = (rows, width)
    return (
        query_grad.reshape(flat).astype(BF16),
        key_grad.reshape(flat).astype(BF16),
        value_grad.reshape(flat).astype(BF16),
        map_grad,
    )


def per_device(queries, key_rows, values, out_grad, feature_map):
    fits = lax.axis_size("ctx") == 2 * GROUPS and feature_map.shape[0] % (4 * GROUPS) == 0
    plan = paired if fits else gathered
    return plan(queries, key_rows, values, out_grad, feature_map)


def solution(mesh):
    rows = P(("seq", "ctx"), None)
    return jax.shard_map(
        per_device,
        mesh=mesh,
        in_specs=(rows, rows, rows, rows, P()),
        out_specs=(rows, rows, rows, P("seq", None, None)),
        check_vma=False,
    )
```

```python
import functools
import math

import jax
import jax.numpy as jnp
from jax import lax
from jax.experimental import pallas as pl
from jax.experimental.pallas import tpu as pltpu
from jax.sharding import PartitionSpec as P

F32 = jnp.float32
BF16 = jnp.bfloat16
VMEM = pl.BlockSpec(memory_space=pltpu.VMEM)
HBM = pl.BlockSpec(memory_space=pltpu.HBM)
ANY = pl.BlockSpec(memory_space=pl.ANY)
GROUPS = 4
FIRST = 0
EXTRA = 16


def dot_nn(a, b):
    return lax.dot_general(a, b, (((1,), (0,)), ((), ())), preferred_element_type=F32)


def dot_nt(a, b):
    return lax.dot_general(a, b, (((1,), (1,)), ((), ())), preferred_element_type=F32)


def dot_tn(a, b):
    return lax.dot_general(a, b, (((0,), (0,)), ((), ())), preferred_element_type=F32)


def call(
    body, outs, operands, cost, after=(), scratch=(), in_spec=None, out_specs=None, aliases=None, in_after=ANY
):
    count = len(operands)

    def run(*refs):
        return body(*refs[:count], *refs[count + len(after) :])

    return pl.pallas_call(
        run,
        out_shape=[jax.ShapeDtypeStruct(shape, dtype) for shape, dtype in outs],
        in_specs=(in_spec or [VMEM] * count) + [in_after] * len(after),
        out_specs=out_specs or [VMEM] * len(outs),
        scratch_shapes=list(scratch),
        input_output_aliases=aliases or {},
        cost_estimate=pl.CostEstimate(
            flops=int(cost * 1.15e9), bytes_accessed=0, transcendentals=0
        ),
        compiler_params=pltpu.CompilerParams(vmem_limit_bytes=16 * 2**20),
    )(*operands, *after)


def place():
    me = lax.axis_index("ctx")
    return lax.rem(me, 2), lax.div(me, 2)


def owned(half, chip, per_owner):
    base = half * (GROUPS * per_owner)
    return [
        (apart, i, base + (chip ^ apart) * per_owner + i)
        for apart in range(GROUPS)
        for i in range(per_owner)
    ]


def pick(refs, apart):
    group, place_ = ((1, 0), (0, 0), (0, 1), (1, 1))[apart]
    return refs[group].at[place_]


def columns(head, size):
    return pl.ds(pl.multiple_of(head * size, size), size)


def triangle(size):
    rows = lax.broadcasted_iota(jnp.int32, (size, size), 0)
    cols = lax.broadcasted_iota(jnp.int32, (size, size), 1)
    return rows, cols


def load_body(per_owner, q, k, v, g, w, q_here, k_here, v_here, g_here, w_here, *refs):
    send, part_q, sems = refs[:2], refs[2], refs[3]
    half_width = q.shape[1] // 2
    core, chip = place()
    pairs = ((g, g_here), (v, v_here), (k, k_here), (q, q_here))
    copies = []
    for turn, half in enumerate((1 - core, core)):
        at = columns(half, half_width)
        for n, (source, target) in enumerate(pairs):
            copies.append(
                pltpu.make_async_copy(source.at[:, at], target.at[:, at], sems.at[turn, n])
            )
    copies.append(pltpu.make_async_copy(w, w_here, sems.at[2, 0]))
    for copy in copies:
        copy.start()
    heads = owned(1 - core, chip, per_owner)
    states(send, part_q, heads, q_here, k_here, v_here, g_here, copies[:4])
    for copy in copies[4:]:
        copy.wait()


def states(out, part_q, heads, q, k, v, g, copies=()):
    size = out[0].shape[-1]
    per_owner = len(heads) // GROUPS
    rows, cols = triangle(q.shape[0])
    ats = [columns(head, size) for _, _, head in heads]
    for copy in copies[:2]:
        copy.wait()
    mixing = [dot_nt(g[:, at], v[:, at]) for at in ats]
    mixing = [jnp.where(rows >= cols, x, 0.0).astype(BF16) for x in mixing]
    for copy in copies[2:3]:
        copy.wait()
    mixed = [dot_nn(x, k[:, at]) for x, at in zip(mixing, ats)]
    early = [dot_tn(k[:, at], v[:, at]) for at in ats]
    for n, (apart, i, _) in enumerate(heads):
        part_q[apart, i] = mixed[n]
        pick(out, apart)[i * size : (i + 1) * size] = early[n].astype(BF16)
    for copy in copies[3:]:
        copy.wait()
    wide = [
        dot_tn(q[:, at], jnp.concatenate([g[:, at], x.astype(BF16)], axis=1))
        for x, at in zip(mixed, ats)
    ]
    for n, (apart, i, _) in enumerate(heads):
        to = pick(out, apart)
        to[(per_owner + i) * size : (per_owner + i + 1) * size] = wide[n][:, :size].astype(BF16)
        if i % 2:
            both, diagonal = pack(wide[n - 1][:, size:], wide[n][:, size:])
            start = 2 * per_owner * size + (i // 2) * (size + EXTRA)
            to[start : start + size] = both.astype(BF16)
            to[start + size : start + size + EXTRA] = diagonal.astype(BF16)


def near_body(per_owner, q, k, v, g, *refs):
    own, extra, part_q = refs[:2], refs[2:4], refs[4]
    size = own[0].shape[-1]
    core, chip = place()
    heads = owned(core, chip, per_owner)
    states(own, part_q, heads, q, k, v, g)
    for apart in range(GROUPS):
        early = pick(own, apart)[: per_owner * size]
        late = pick(own, apart)[per_owner * size : 2 * per_owner * size]
        extra[apart // 2][apart % 2] = jnp.where(core == 0, early, late)


def pack(first, second):
    size = first.shape[0]
    rows, cols = triangle(size)
    both = jnp.where(rows >= cols, first, second)
    both += jnp.where(rows <= cols, first, second).T
    diagonal = 2.0 * jnp.sum(jnp.where(rows == cols, second, 0.0), axis=0, keepdims=True)
    return both, jnp.broadcast_to(diagonal, (EXTRA, size))


def join_body(places, per_owner, own, other, *outs):
    size = own.shape[-1]
    count = 2 * per_owner * size
    core, _ = place()
    last = core == 1
    totals = []
    for at in places:
        for i in range(per_owner):
            ahead = slice(i * size, (i + 1) * size)
            behind = slice((per_owner + i) * size, (per_owner + i + 1) * size)
            early = jnp.where(last, other[at, ahead], own[at, ahead])
            late = jnp.where(last, own[at, behind], other[at, behind])
            totals.append(dot_nt(late, early))
    for n, at in enumerate(places):
        outs[n][:count] = own[at, :count] + other[at, :count]
        for pair in range(per_owner // 2):
            both, diagonal = pack(*totals[n * per_owner + 2 * pair :][:2])
            start = count + pair * (size + EXTRA)
            for x in (own, other):
                both += x[at, start : start + size].astype(F32)
                diagonal += x[at, start + size : start + size + EXTRA].astype(F32)
            outs[n][start : start + size] = both.astype(BF16)
            outs[n][start + size : start + size + EXTRA] = diagonal.astype(BF16)


def rest_first_body(per_owner, *refs):
    core, _ = place()

    @pl.when(core == FIRST)
    def _():
        rest(per_owner, *refs)


def rest_second_body(per_owner, *refs):
    core, _ = place()

    @pl.when(core != FIRST)
    def _():
        rest(per_owner, *refs[:5], *refs[-4:])


def rest(per_owner, q, k, v, g, w, part_k, part_v, key_w, gram):
    size = w.shape[-1]
    core, chip = place()
    rows, cols = triangle(q.shape[0])
    later = cols >= rows
    for which, half in enumerate((core, 1 - core)):
        heads = owned(half, chip, per_owner)
        ats = [columns(head, size) for _, _, head in heads]
        square = [dot_nt(w[head], w[head]).astype(BF16) for _, _, head in heads]
        mixing = [dot_nt(v[:, at], g[:, at]) for at in ats]
        mixing = [jnp.where(later, x, 0.0).astype(BF16) for x in mixing]
        keyed = [dot_nn(k[:, at], x).astype(BF16) for x, at in zip(square, ats)]
        mixed = [dot_nn(x, q[:, at]) for x, at in zip(mixing, ats)]
        scores = [dot_nt(x, q[:, at]) for x, at in zip(keyed, ats)]
        scores = [jnp.where(later, x, 0.0).astype(BF16) for x in scores]
        scored = [dot_nn(x, g[:, at]) for x, at in zip(scores, ats)]
        for n, (apart, i, _) in enumerate(heads):
            gram[which, apart, i] = square[n]
            key_w[which, apart, i] = keyed[n]
            part_k[which, apart, i] = mixed[n]
            part_v[which, apart, i] = scored[n]


def owner_body(per_owner, *refs):
    parts, outs, (placed, carried) = refs[:GROUPS], refs[GROUPS : 2 * GROUPS], refs[2 * GROUPS :]
    size = outs[0].shape[-1]
    states = 2 * per_owner * size
    _, chip = place()
    for apart, part in enumerate(parts):
        placed[chip ^ apart] = part[:states]
    totals = []
    for i in range(per_owner):
        ahead = slice(i * size, (i + 1) * size)
        behind = slice((per_owner + i) * size, (per_owner + i + 1) * size)
        early = [placed[n, ahead] for n in range(GROUPS)]
        late = [placed[n, behind] for n in range(GROUPS)]
        prefix = [jnp.zeros_like(early[0])]
        suffix = [jnp.zeros_like(late[0])]
        before, after = early[0].astype(F32), late[-1].astype(F32)
        for n in range(1, GROUPS):
            prefix.append(before.astype(BF16))
            suffix.insert(0, after.astype(BF16))
            before += early[n].astype(F32)
            after += late[GROUPS - 1 - n].astype(F32)
        cross = dot_nt(late[1], prefix[1])
        for n in range(2, GROUPS):
            cross += dot_nt(late[n], prefix[n])
        totals.append(cross)
        for n in range(GROUPS):
            carried[n, ahead] = prefix[n]
            carried[n, behind] = suffix[n]
    for apart, out in enumerate(outs):
        out[:states] = carried[chip ^ apart]
    for pair in range(per_owner // 2):
        both, diagonal = pack(totals[2 * pair], totals[2 * pair + 1])
        start = states + pair * (size + EXTRA)
        for part in parts:
            both += part[start : start + size].astype(F32)
            diagonal += part[start + size : start + size + EXTRA].astype(F32)
        for out in outs:
            out[start : start + size] = both.astype(BF16)
            out[start + size : start + size + EXTRA] = diagonal.astype(BF16)


def finish(pieces, per_owner, scale, shared, sources, blocks):
    g, v, w, key_w, gram, part_q, part_k, part_v, other, extra = shared
    size = gram.shape[-1]
    core, chip = place()
    heads = []
    for piece, (which, apart) in enumerate(pieces):
        half = 1 - core if which else core
        for i in range(per_owner):
            owner = chip ^ apart
            head = (half * GROUPS + owner) * per_owner + i
            slot = lax.rem(owner, 2) * per_owner + i
            heads.append((which, apart, i, sources[piece], head, slot))
    ats = [columns(head[4], size) for head in heads]
    prefix, suffix = [], []
    for which, apart, i, source, *_ in heads:
        ahead = slice(i * size, (i + 1) * size)
        behind = slice((per_owner + i) * size, (per_owner + i + 1) * size)
        if which:
            early = late = extra[apart // 2][apart % 2, ahead]
        else:
            early, late = pick(other, apart)[ahead], pick(other, apart)[behind]
        before, after = source[ahead], source[behind]
        prefix.append(before + jnp.where(core == 1, early, jnp.zeros_like(early)))
        suffix.append(after + jnp.where(core == 0, late, jnp.zeros_like(late)))
    raw_q = [dot_nt(g[:, at], x) for x, at in zip(prefix, ats)]
    raw_k = [dot_nt(v[:, at], x) for x, at in zip(suffix, ats)]
    raw_v = [dot_nn(key_w[h, a, i], x) for x, (h, a, i, *_) in zip(suffix, heads)]
    raw_q = [(part_q[h][a, i] + x).astype(BF16) for x, (h, a, i, *_) in zip(raw_q, heads)]
    raw_k = [(part_k[h, a, i] + x).astype(BF16) for x, (h, a, i, *_) in zip(raw_k, heads)]
    for x, (h, a, i, _, _, to) in zip(raw_v, heads):
        outs = blocks[h]
        outs[2][:, columns(to, size)] = (part_v[h, a, i] + x).astype(BF16)
    done_q = [dot_nn(x, gram[h, a, i]) for x, (h, a, i, *_) in zip(raw_q, heads)]
    done_k = [dot_nn(x, gram[h, a, i]) for x, (h, a, i, *_) in zip(raw_k, heads)]
    for x, y, (h, *_, to) in zip(done_q, done_k, heads):
        outs = blocks[h]
        outs[0][:, columns(to, size)] = x.astype(BF16)
        outs[1][:, columns(to, size)] = y.astype(BF16)
    rows, cols = triangle(size)
    for piece, source in enumerate(sources):
        for pair in range(per_owner // 2):
            start = 2 * per_owner * size + pair * (size + EXTRA)
            both = source[start : start + size].astype(F32)
            diagonal = source[start + size : start + size + EXTRA][:1].astype(F32)
            turned = both.T
            first = jnp.where(rows >= cols, both, turned)
            second = jnp.where(rows < cols, both, turned)
            second = jnp.where(rows == cols, diagonal, second)
            for i, whole in ((2 * pair, first), (2 * pair + 1, second)):
                which, _, _, _, head, slot = heads[piece * per_owner + i]
                blocks[which][3][slot] = dot_nn(whole.astype(BF16), w[head]) * scale


def leave(half, turn, here, outs, sems):
    _, chip = place()
    block = 2 * half + (lax.div(chip, 2) ^ turn)
    width, count = here[0].shape[1], here[3].shape[0]
    copies = []
    for n in range(4):
        at = outs[n].at[pl.ds(block * count, count)] if n == 3 else outs[n].at[:, columns(block, width)]
        copies.append(pltpu.make_async_copy(here[n], at, sems.at[n]))
        copies[-1].start()
    return copies


def opened(refs, count):
    shared = (*refs[:5], refs[5:7], *refs[7:9], refs[9:11], refs[11:13])
    return shared, refs[13 : 13 + count], refs[13 + count :]


def tail_first_body(per_owner, scale, *refs):
    shared, sources, refs = opened(refs, 2)
    outs, here, sems = refs[:4], refs[4:8], refs[8]
    core, _ = place()
    finish([(0, 0), (0, 1)], per_owner, scale, shared, sources, [here, None])
    for copy in leave(core, 0, here, outs, sems):
        copy.wait()


def tail_second_body(per_owner, scale, *refs):
    shared, sources, outs = opened(refs, 4)
    finish([(0, 2), (0, 3), (1, 0), (1, 1)], per_owner, scale, shared, sources, [outs[:4], outs[4:]])


def tail_third_body(per_owner, scale, *refs):
    shared, sources, refs = opened(refs, 2)
    near, far, outs, here, sems = refs[:4], refs[4:8], refs[8:12], refs[12:16], refs[16]
    core, _ = place()
    copies = leave(core, 1, near, outs, sems.at[0]) + leave(1 - core, 0, far, outs, sems.at[1])
    finish([(1, 2), (1, 3)], per_owner, scale, shared, sources, [None, here])
    copies += leave(1 - core, 1, here, outs, sems.at[2])
    for copy in copies:
        copy.wait()


def swap(x, apart):
    count = lax.axis_size("ctx")
    return lax.ppermute(x, "ctx", [(i, i ^ apart) for i in range(count)])


def paired(q, k, v, g, w):
    rows, width = q.shape
    heads, size = w.shape[0], w.shape[-1]
    per_owner = heads // (2 * GROUPS)
    length = rows * lax.axis_size("ctx")
    block = (size, size)
    one = (GROUPS, per_owner) + block
    twice = (2,) + one
    payload = (2 * per_owner * size + (per_owner // 2) * (size + EXTRA), size)
    payloads = (GROUPS // 2,) + payload
    bind = functools.partial

    *here, w, send_near, send_rest, part_q1 = call(
        bind(load_body, per_owner),
        [((rows, width), BF16)] * 4 + [(w.shape, BF16), (payloads, BF16), (payloads, BF16), (one, F32)],
        [pltpu.with_memory_space_constraint(x, pltpu.HBM) for x in (q, k, v, g, w)],
        2.0,
        in_spec=[HBM] * 5,
        scratch=[pltpu.SemaphoreType.DMA((3, 4))],
    )
    other = [swap(x, 1) for x in (send_near, send_rest)]
    *own, extra_a, extra_b, part_q0 = call(
        bind(near_body, per_owner),
        [(payloads, BF16)] * 2
        + [*[((GROUPS // 2, per_owner * size, size), BF16)] * 2, (one, F32)],
        here,
        1.0,
    )
    extra = [extra_a, extra_b]

    def join(places, group, cost, after=()):
        body = bind(join_body, places, per_owner)
        return call(body, [(payload, BF16)] * len(places), (own[group], other[group]), cost, after)

    near_sums = join((0,), 0, 0.15)
    locals_ = [(twice, F32), (twice, F32), (twice, BF16), (twice, BF16)]
    local = list(
        call(bind(rest_first_body, per_owner), locals_, (*here, w), 1.8, after=near_sums[:1])
    )
    *near_sums, local[0] = lax.optimization_barrier((*near_sums, local[0]))
    (y_sum,) = join((1,), 0, 0.15, near_sums[:1])
    (far_sum,) = join((1,), 1, 0.15, near_sums[:1])
    chip_sums = [None, near_sums[0], y_sum, far_sum]
    parts = [None] + [swap(chip_sums[j], 2 * j) for j in range(1, GROUPS)]
    local = call(
        bind(rest_second_body, per_owner),
        locals_,
        (*here, w),
        1.8,
        after=tuple(local),
        aliases={5 + n: n for n in range(4)},
        in_after=VMEM,
    )
    part_k, part_v, key_w, gram = local
    (parts[0],) = join((0,), 1, 0.15, (gram,))
    *extra, gram = lax.optimization_barrier((*extra, gram))
    extra = [swap(x, 1) for x in extra]
    carried = call(
        bind(owner_body, per_owner),
        [(payload, BF16)] * GROUPS,
        parts,
        0.5,
        after=(gram, *extra),
        scratch=[pltpu.VMEM((GROUPS, 2 * per_owner * size, size), BF16)] * 2,
    )
    near = [carried[0]] + [swap(carried[j], 2 * j) for j in range(1, GROUPS)]
    scale = 1.0 / math.sqrt(length)
    outs = [((rows, width), BF16)] * 3 + [((heads,) + block, F32)]
    shared = (here[3], here[2], w, key_w, gram, part_q0, part_q1, part_k, part_v, *other)

    part = [((rows, width // 4), BF16)] * 3 + [((heads // 4,) + block, F32)]
    room = [pltpu.VMEM(shape, dtype) for shape, dtype in part]
    done = call(
        bind(tail_first_body, per_owner, scale),
        outs,
        (*shared, part_q0, part_q0, *near[:2]),
        1.4,
        scratch=room + [pltpu.SemaphoreType.DMA((4,))],
        out_specs=[HBM] * 4,
    )
    done = list(done)
    near[2], done[0] = lax.optimization_barrier((near[2], done[0]))
    far = [swap(x, 1) for x in near]
    blocks = call(
        bind(tail_second_body, per_owner, scale),
        part * 2,
        (*shared, *extra, *near[2:], *far[:2]),
        1.0,
    )
    operands = (*shared, *extra, *far[2:], *blocks)
    return tuple(
        call(
            bind(tail_third_body, per_owner, scale),
            outs,
            operands,
            1.2,
            after=tuple(done),
            scratch=room + [pltpu.SemaphoreType.DMA((3, 4))],
            out_specs=[HBM] * 4,
            aliases={len(operands) + n: n for n in range(4)},
        )
    )


def gathered(q, k, v, g, w):
    rows, width = q.shape
    heads, size = w.shape[0], w.shape[-1]
    count = lax.axis_size("ctx")
    me = lax.axis_index("ctx")
    q, k, v, g = (x.reshape(rows, heads, size) for x in (q, k, v, g))

    def mul(spec, a, b):
        return jnp.einsum(spec, a, b, preferred_element_type=F32)

    query_feat = mul("thd,hde->the", q, w).astype(BF16)
    key_feat = mul("thd,hde->the", k, w).astype(BF16)
    key_state = mul("the,thv->hev", key_feat, v).astype(BF16)
    grad_state = mul("the,thv->hev", query_feat, g).astype(BF16)
    index = jnp.arange(count).reshape(count, 1, 1, 1)
    keys = lax.all_gather(key_state, "ctx").astype(F32)
    prefix = jnp.sum(jnp.where(index < me, keys, 0.0), 0).astype(BF16)
    grads = lax.all_gather(grad_state, "ctx").astype(F32)
    suffix = jnp.sum(jnp.where(index > me, grads, 0.0), 0).astype(BF16)
    row, col = triangle(rows)
    causal = row >= col
    scores = jnp.where(causal, mul("the,she->hts", query_feat, key_feat), 0.0).astype(BF16)
    mixing = jnp.where(causal, mul("thv,shv->hts", g, v), 0.0).astype(BF16)
    feat_q = mul("hts,she->the", mixing, key_feat) + mul("thv,hev->the", g, prefix)
    feat_k = mul("hts,the->she", mixing, query_feat) + mul("shv,hev->she", v, suffix)
    feat_q, feat_k = feat_q.astype(BF16), feat_k.astype(BF16)
    value_grad = mul("hts,thv->shv", scores, g) + mul("she,hev->shv", key_feat, suffix)
    query_grad = mul("the,hde->thd", feat_q, w)
    key_grad = mul("the,hde->thd", feat_k, w)
    local = mul("thd,the->hde", q, feat_q) + mul("thd,the->hde", k, feat_k)
    map_grad = lax.psum(local.astype(BF16).astype(F32), "ctx") / math.sqrt(rows * count)
    flat = (rows, width)
    return (
        query_grad.reshape(flat).astype(BF16),
        key_grad.reshape(flat).astype(BF16),
        value_grad.reshape(flat).astype(BF16),
        map_grad,
    )


def per_device(queries, key_rows, values, out_grad, feature_map):
    fits = lax.axis_size("ctx") == 2 * GROUPS and feature_map.shape[0] % (4 * GROUPS) == 0
    plan = paired if fits else gathered
    return plan(queries, key_rows, values, out_grad, feature_map)


def solution(mesh):
    rows = P(("seq", "ctx"), None)
    return jax.shard_map(
        per_device,
        mesh=mesh,
        in_specs=(rows, rows, rows, rows, P()),
        out_specs=(rows, rows, rows, P("seq", None, None)),
        check_vma=False,
    )
```
